32 devices in a mesh: gx: 16 (over z, y, x), gy: 2 (over core).
Axes of the slice: x: 2, y: 2, z: 4, core: 2. Of those that a mesh axis runs over, the one named last changes fastest.
Arguments:
- magnetization: float32 [3, 256, 32, 512], P(None, 'gx', 'gy'), may hold values from -2.2 to 2.2
- easy_axes: float32 [3, 256, 32, 512], P(None, 'gx', 'gy'), may hold values from -6 to 6
- pins: float32 [2, 3, 32, 512], P(None, None, 'gy'), may hold values from -4 to 4
Outputs:
- final_field: float32 [3, 256, 32, 512], P(None, 'gx', 'gy')
The draws below stay inside these ranges and needn't reach their ends.
All inputs are finite; a program needn't handle non-finite values.
Results may differ from the reference program's by a relative error of at most 0.0003.
Values sent between devices are 32-bit elements; how exact they have to be, the bound alone decides.
No kernel may reach another device: no remote copies, remote signals or barrier semaphores. Data moves between devices by JAX's collectives and lax.ppermute only.
A program may use at most 64 MiB of HBM per device.

```python
import jax
import jax.numpy as jnp
from jax import lax

NZ = 512
STEPS = 2
NX = 256
NY = 32


def draw_magnetization(key, part):
    first_key, second_key = jax.random.split(key, 2)
    position = (jnp.arange(NX, dtype=jnp.float32) + 0.5 - NX / 2.0) / (NX / 16.0)
    profile = jnp.stack([jnp.tanh(position), 1.0 / jnp.cosh(position), jnp.zeros_like(position)])
    amplitude = jax.random.uniform(first_key, (NY, NZ), jnp.float32, 0.3, 1.2)
    noise = jnp.clip(0.3 * jax.random.normal(second_key, (3, NX, NY, NZ), jnp.float32), -1.0, 1.0)
    return (profile[:, :, None, None] * amplitude[None, None] + noise).astype(jnp.float32)


def shard_levels(rng, dims, shards, smallest, largest):
    loudness = 1.0
    for axis_at, blocks in shards:
        draws = jax.random.uniform(jax.random.fold_in(jax.random.fold_in(rng, 6), axis_at), (blocks,), jnp.float32, smallest / len(shards), largest / len(shards))
        loudness = loudness * jnp.repeat(jnp.exp(draws), dims[axis_at] // blocks).reshape((-1,) + (1,) * (len(dims) - 1 - axis_at))
    return loudness


def centred(stream_key, dims, scale, bound, pieces=(), kind=jnp.bfloat16):
    factor_of = shard_levels(stream_key, dims, pieces, -0.22, 0.18) if pieces else 1.0
    drawn = jax.random.normal(stream_key, dims, jnp.float32) * scale * factor_of
    return jnp.minimum(jnp.maximum(drawn, -bound), bound).astype(kind)


def setup_inputs(seed: int = 0) -> dict:
    arg_keys = jax.random.split(jax.random.key(seed), 4)
    magnetization = draw_magnetization(jax.random.fold_in(arg_keys[3], 71), 0)
    easy_axes = centred(arg_keys[1], (3, NX, NY, NZ), 1.0, 6.0, ((1, 16), (2, 2)), jnp.float32)
    pins = centred(arg_keys[2], (2, 3, NY, NZ), 1.0, 4.0, ((2, 2),), jnp.float32)
    return dict(magnetization=magnetization, easy_axes=easy_axes, pins=pins)


diffusion = 4000.0
anisotropy_rate = 0.3
torque_rate = 0.2
exchange_rate = 0.1
norm_floor = 0.5

def line_solve(source):
    count = source.shape[0]
    lower_band = jnp.full((count,), -diffusion, jnp.float32).at[0].set(0.0)
    upper_band = jnp.full((count,), -diffusion, jnp.float32).at[count - 1].set(0.0)
    middle = jnp.full((count,), 1.0 + 2.0 * diffusion, jnp.float32)
    columns = source.reshape(count, -1)
    solved = lax.linalg.tridiagonal_solve(lower_band, middle, upper_band, columns)
    return solved.reshape(source.shape)

def reference(magnetization, easy_axes, pins):
    field = magnetization
    for stepno in range(STEPS):
        for component in range(3):
            projection = lax.optimization_barrier(jnp.sum(field * easy_axes, axis=0))
            source = field[component] + anisotropy_rate * projection * easy_axes[component]
            source = source.at[0].add(diffusion * pins[0, component])
            source = source.at[-1].add(diffusion * pins[1, component])
            field = field.at[component].set(line_solve(source))
        projection = lax.optimization_barrier(jnp.sum(field * easy_axes, axis=0))
        neighbours = jnp.roll(field, 1, 2) + jnp.roll(field, -1, 2) + jnp.roll(field, 1, 3) + jnp.roll(field, -1, 3)
        effective = exchange_rate * (neighbours - 4.0 * field) + projection[None] * easy_axes
        twisted = jnp.cross(field, effective, axis=0)
        rotated = field - torque_rate * twisted
        length = jnp.sqrt(lax.optimization_barrier(jnp.sum(rotated * rotated, axis=0)))
        field = rotated / jnp.maximum(length, norm_floor)[None]
    return field
```

```python
import functools

import jax
import jax.numpy as jnp
import numpy as np
from jax import lax
from jax.experimental import pallas as pl
from jax.experimental.pallas import tpu as pltpu
from jax.sharding import PartitionSpec as P

STEPS = 2
LANES = 128
RHS = 6
COUPLED = 16

diffusion = 4000.0
anisotropy_rate = 0.3
torque_rate = 0.2
exchange_rate = 0.1
norm_floor = 0.5


class Line:
    def __init__(self, planes):
        leading = 1.0 + 2.0 * diffusion
        pivots = [leading]
        for _ in range(1, planes):
            pivots.append(leading - diffusion * diffusion / pivots[-1])
        self.planes = planes
        self.inverse_pivot = [1.0 / p for p in pivots]
        self.factor = [0.0] + [diffusion / p for p in pivots[:-1]]
        block = (
            leading * np.eye(planes)
            - diffusion * np.eye(planes, k=1)
            - diffusion * np.eye(planes, k=-1)
        )
        self.from_low = diffusion * np.linalg.inv(block)[:, 0]
        self.from_high = self.from_low[::-1]

    def solve(self, source):
        planes = self.planes
        carried = [source[0]]
        for i in range(1, planes):
            carried.append(source[i] + self.factor[i] * carried[-1])
        solved = [None] * planes
        solved[-1] = carried[-1] * self.inverse_pivot[-1]
        for i in range(planes - 2, -1, -1):
            solved[i] = carried[i] * self.inverse_pivot[i] + self.factor[i + 1] * solved[i + 1]
        return solved


def ghost_table(line, groups):
    near, far = line.from_low[0], line.from_low[-1]
    link = np.zeros((2 * groups, 2 * groups))
    pick = np.zeros((2 * groups, 2 * groups))
    for d in range(groups):
        if d > 0:
            link[d, groups + d - 1] = near
            link[groups + d, groups + d - 1] = far
            pick[d, groups + d - 1] = 1.0
        if d < groups - 1:
            link[d, d + 1] = far
            link[groups + d, d + 1] = near
            pick[groups + d, d + 1] = 1.0
    return pick @ np.linalg.inv(np.eye(2 * groups) - link)


def row_window(value, values, units, tile, tiles, rows):
    start = (tile // units) * values * units + value * units + tile % units
    return pl.ds(start, rows, stride=tiles * values)


def pinned(source, pins_ref, component, lanes):
    position = lax.axis_index("gx")
    first = jnp.where(position == 0, diffusion, 0.0).astype(jnp.float32)
    last = jnp.where(position == lax.axis_size("gx") - 1, diffusion, 0.0).astype(jnp.float32)
    source[0] = source[0] + first * pins_ref[0, component, :, lanes]
    source[-1] = source[-1] + last * pins_ref[1, component, :, lanes]
    return source


def solve_components(line, field_ref, axes_ref, pins_ref, lanes, ghosts):
    planes = line.planes
    field = [[field_ref[c, i, :, lanes] for i in range(planes)] for c in range(3)]
    axes = [[axes_ref[c, i, :, lanes] for i in range(planes)] for c in range(3)]
    for component in range(3):
        source = []
        for i in range(planes):
            projection = (
                field[0][i] * axes[0][i] + field[1][i] * axes[1][i] + field[2][i] * axes[2][i]
            )
            source.append(
                field[component][i] + (anisotropy_rate * projection) * axes[component][i]
            )
        source = pinned(source, pins_ref, component, lanes)
        if ghosts is not None:
            source[0] = source[0] + diffusion * ghosts[component][0]
            source[-1] = source[-1] + diffusion * ghosts[component][1]
        field[component] = line.solve(source)
    return field


def couplings(line, axes_ref, lanes):
    planes = line.planes
    low, high = line.from_low, line.from_high
    axes = [[axes_ref[c, i, :, lanes] for i in range(planes)] for c in range(3)]
    scaled = [anisotropy_rate * a for a in axes[1]]
    first_second = [axes[0][i] * scaled[i] for i in range(planes)]
    second_third = [axes[2][i] * scaled[i] for i in range(planes)]
    first_third = [(anisotropy_rate * axes[0][i]) * axes[2][i] for i in range(planes)]

    def weighted(terms, weights):
        total = terms[0] * float(weights[0] / diffusion)
        for i in range(1, planes):
            total = total + terms[i] * float(weights[i] / diffusion)
        return total

    found = []
    for product in (first_second, second_third):
        for weights in (low * low, low * high, high * high):
            found.append(weighted(product, weights))
    for ghost in (low, high):
        moved = line.solve([first_second[i] * float(ghost[i]) for i in range(planes)])
        pushed = [
            second_third[i] * moved[i] + first_third[i] * float(ghost[i]) for i in range(planes)
        ]
        found.append(weighted(pushed, low))
        found.append(weighted(pushed, high))
    return found


def send_edges(line, units, coupled, field_ref, axes_ref, pins_ref, out_ref):
    rows, width = field_ref.shape[2], field_ref.shape[3]
    tiles = width // LANES
    values = COUPLED if coupled else RHS
    for tile in range(tiles):
        lanes = slice(tile * LANES, (tile + 1) * LANES)
        solved = solve_components(line, field_ref, axes_ref, pins_ref, lanes, None)
        sent = []
        for component in range(3):
            sent += [solved[component][0], solved[component][-1]]
        if coupled:
            sent += couplings(line, axes_ref, lanes)
        for value in range(values):
            out_ref[row_window(value, values, units, tile, tiles, rows), :] = sent[value]


def reduced_kernel(groups, units, rhs_values, rhs_ref, coupling_ref, table_ref, out_ref):
    def read(ref, values, value):
        parts = [
            ref[pl.ds(value * units + u, groups, stride=values * units), :] for u in range(units)
        ]
        return jnp.concatenate(parts, axis=1) if units > 1 else parts[0]

    table = table_ref[...]

    def ghosts(first, last):
        found = jnp.dot(
            table,
            jnp.concatenate([first, last], axis=0),
            precision=lax.Precision.HIGHEST,
            preferred_element_type=jnp.float32,
        )
        return found[:groups], found[groups:]

    rhs = [read(rhs_ref, rhs_values, v) for v in range(RHS)]
    c = [read(coupling_ref, COUPLED, v) for v in range(RHS, COUPLED)]
    low1, high1 = ghosts(rhs[0], rhs[1])
    low2, high2 = ghosts(
        rhs[2] + c[0] * low1 + c[1] * high1, rhs[3] + c[1] * low1 + c[2] * high1
    )
    low3, high3 = ghosts(
        rhs[4] + c[3] * low2 + c[4] * high2 + c[6] * low1 + c[8] * high1,
        rhs[5] + c[4] * low2 + c[5] * high2 + c[7] * low1 + c[9] * high1,
    )
    for value, found in enumerate((low1, high1, low2, high2, low3, high3)):
        for u in range(units):
            out_ref[pl.ds(value * units + u, groups, stride=RHS * units), :] = found[
                :, u * LANES : (u + 1) * LANES
            ]


def finish_kernel(line, units, field_ref, axes_ref, pins_ref, ghost_ref, out_ref, low_ref, high_ref):
    planes = line.planes
    rows, width = field_ref.shape[2], field_ref.shape[3]
    tiles = width // LANES
    for tile in range(tiles):
        lanes = slice(tile * LANES, (tile + 1) * LANES)
        ghosts = [
            [
                ghost_ref[row_window(2 * c + side, RHS, units, tile, tiles, rows), :]
                for side in range(2)
            ]
            for c in range(3)
        ]
        solved = solve_components(line, field_ref, axes_ref, pins_ref, lanes, ghosts)
        for c in range(3):
            for i in range(planes):
                out_ref[c, i, :, lanes] = solved[c][i]
                low_ref[c * planes + i : c * planes + i + 1, lanes] = solved[c][i][:1]
                high_ref[c * planes + i : c * planes + i + 1, lanes] = solved[c][i][rows - 1 :]


def rotate(field_ref, below_ref, above_ref, axes_ref, out_ref):
    planes, rows, width = field_ref.shape[1:]
    row = lax.broadcasted_iota(jnp.int32, (rows, width), 0)
    for i in range(planes):
        field = [field_ref[c, i] for c in range(3)]
        axes = [axes_ref[c, i] for c in range(3)]
        projection = field[0] * axes[0] + field[1] * axes[1] + field[2] * axes[2]
        effective = []
        for c in range(3):
            at = c * planes + i
            below = jnp.where(
                row == 0, below_ref[at : at + 1, :], pltpu.roll(field[c], 1, 0)
            )
            above = jnp.where(
                row == rows - 1, above_ref[at : at + 1, :], pltpu.roll(field[c], rows - 1, 0)
            )
            beside = pltpu.roll(field[c], 1, 1) + pltpu.roll(field[c], width - 1, 1)
            effective.append(
                exchange_rate * (((above + below) + beside) - 4.0 * field[c])
                + projection * axes[c]
            )
        rotated = []
        for c in range(3):
            d, e = (c + 1) % 3, (c + 2) % 3
            twisted = field[d] * effective[e] - field[e] * effective[d]
            rotated.append(field[c] - torque_rate * twisted)
        square = rotated[0] * rotated[0] + rotated[1] * rotated[1] + rotated[2] * rotated[2]
        scale = jnp.minimum(lax.rsqrt(square), 1.0 / norm_floor)
        for c in range(3):
            out_ref[c, i] = rotated[c] * scale


def rotate_and_send_kernel(
    line, units, field_ref, below_ref, above_ref, axes_ref, pins_ref, out_ref, sent_ref
):
    rotate(field_ref, below_ref, above_ref, axes_ref, out_ref)
    send_edges(line, units, False, out_ref, axes_ref, pins_ref, sent_ref)


VMEM = pl.BlockSpec(memory_space=pltpu.VMEM)
LIMIT = pltpu.CompilerParams(vmem_limit_bytes=32 * 1024 * 1024)


def call(kernel, shapes, *operands):
    shapes = [jax.ShapeDtypeStruct(shape, jnp.float32) for shape in shapes]
    single = len(shapes) == 1
    return pl.pallas_call(
        kernel,
        out_shape=shapes[0] if single else tuple(shapes),
        in_specs=[VMEM] * len(operands),
        out_specs=VMEM if single else (VMEM,) * len(shapes),
        compiler_params=LIMIT,
    )(*operands)


def exchange(block, groups):
    parts = block.reshape(groups, -1, LANES)
    return lax.all_to_all(parts, "gx", split_axis=0, concat_axis=0, tiled=True).reshape(
        block.shape
    )


def to_neighbours(low, high):
    count = lax.axis_size("gy")
    forward = [(i, (i + 1) % count) for i in range(count)]
    backward = [(target, source) for source, target in forward]
    return lax.ppermute(high, "gy", forward), lax.ppermute(low, "gy", backward)


def per_device(magnetization, easy_axes, pins):
    _, planes, rows, width = magnetization.shape
    groups = lax.axis_size("gx")
    units = rows * (width // LANES) // groups
    line = Line(planes)
    table = jnp.asarray(ghost_table(line, groups), jnp.float32)
    whole = magnetization.shape
    edge = (3 * planes, width)
    sent_shape = (groups * RHS * units, LANES)
    coupled_shape = (groups * COUPLED * units, LANES)

    field = magnetization
    sent = call(
        functools.partial(send_edges, line, units, True),
        [coupled_shape],
        field,
        easy_axes,
        pins,
    )
    coupling = None
    for stepno in range(STEPS):
        gathered = exchange(sent, groups)
        if stepno == 0:
            coupling = gathered
        ghosts = call(
            functools.partial(reduced_kernel, groups, units, RHS if stepno else COUPLED),
            [sent_shape],
            gathered,
            coupling,
            table,
        )
        ghosts = exchange(ghosts, groups)
        solved, low, high = call(
            functools.partial(finish_kernel, line, units),
            [whole, edge, edge],
            field,
            easy_axes,
            pins,
            ghosts,
        )
        below, above = to_neighbours(low, high)
        if stepno < STEPS - 1:
            field, sent = call(
                functools.partial(rotate_and_send_kernel, line, units),
                [whole, sent_shape],
                solved,
                below,
                above,
                easy_axes,
                pins,
            )
        else:
            field = call(rotate, [whole], solved, below, above, easy_axes)
    return field


def solution(mesh):
    in_specs = (P(None, "gx", "gy", None), P(None, "gx", "gy", None), P(None, None, "gy", None))
    out_specs = P(None, "gx", "gy", None)
    return jax.shard_map(
        per_device, mesh=mesh, in_specs=in_specs, out_specs=out_specs, check_vma=False
    )
```

```python
import functools

import jax
import jax.numpy as jnp
import numpy as np
from jax import lax
from jax.experimental import pallas as pl
from jax.experimental.pallas import tpu as pltpu
from jax.sharding import PartitionSpec as P

STEPS = 2
LANES = 128
RHS = 6
COUPLED = 16

diffusion = 4000.0
anisotropy_rate = 0.3
torque_rate = 0.2
exchange_rate = 0.1
norm_floor = 0.5


class Line:
    def __init__(self, planes):
        leading = 1.0 + 2.0 * diffusion
        pivots = [leading]
        for _ in range(1, planes):
            pivots.append(leading - diffusion * diffusion / pivots[-1])
        self.planes = planes
        self.inverse_pivot = [1.0 / p for p in pivots]
        self.factor = [0.0] + [diffusion / p for p in pivots[:-1]]
        block = (
            leading * np.eye(planes)
            - diffusion * np.eye(planes, k=1)
            - diffusion * np.eye(planes, k=-1)
        )
        self.from_low = diffusion * np.linalg.inv(block)[:, 0]
        self.from_high = self.from_low[::-1]

    def solve(self, source):
        planes = self.planes
        carried = [source[0]]
        for i in range(1, planes):
            carried.append(source[i] + self.factor[i] * carried[-1])
        solved = [None] * planes
        solved[-1] = carried[-1] * self.inverse_pivot[-1]
        for i in range(planes - 2, -1, -1):
            solved[i] = carried[i] * self.inverse_pivot[i] + self.factor[i + 1] * solved[i + 1]
        return solved


class Level:
    def __init__(self, length, radix, shift, rows):
        self.radix, self.shift, self.rows = radix, shift, rows
        line = Line(length)
        near, far = line.from_low[0], line.from_low[-1]
        count = 2 * radix
        inside = np.kron(np.eye(radix), np.array([[near, far], [far, near]]))
        pick = np.zeros((count, count))
        for r in range(radix):
            if r > 0:
                pick[2 * r, 2 * r - 1] = 1.0
            if r < radix - 1:
                pick[2 * r + 1, 2 * r + 2] = 1.0
        outer = np.zeros((count, 2))
        outer[0, 0] = outer[count - 1, 1] = 1.0
        settle = np.linalg.inv(np.eye(count) - pick @ inside)
        self.ghosts = settle @ pick
        self.passed = settle @ outer
        ends = (np.eye(count) + inside @ self.ghosts)[[0, count - 1]]
        self.ends = ends


def radices_of(groups):
    found = []
    while groups > 1:
        radix = 4 if groups % 4 == 0 else 2
        assert groups % radix == 0
        found.append(radix)
        groups //= radix
    return found


def digit(level):
    return (lax.axis_index("gx") >> level.shift) & (level.radix - 1)


def combine(weights, terms):
    total = None
    for weight, term in zip(weights, terms):
        if weight == 0.0 or term is None:
            continue
        part = term * float(weight)
        total = part if total is None else total + part
    return total


def add(*terms):
    kept = [t for t in terms if t is not None]
    total = kept[0] if kept else None
    for term in kept[1:]:
        total = total + term
    return total


def times(left, right):
    return None if right is None else left * right


def solve_children(level, rhs, coupling, outer):
    radix = level.radix

    def settle(values, component):
        found = []
        for k in range(2 * radix):
            own = combine(level.ghosts[k], values)
            if outer is not None:
                own = add(own, combine(level.passed[k], outer[component]))
            found.append(own)
        return found

    first = rhs[0]
    ghosts1 = settle(first, 0)
    second = []
    for r in range(radix):
        c, low, high = coupling[r], ghosts1[2 * r], ghosts1[2 * r + 1]
        second.append(add(rhs[1][2 * r], times(c[0], low), times(c[1], high)))
        second.append(add(rhs[1][2 * r + 1], times(c[1], low), times(c[2], high)))
    ghosts2 = settle(second, 1)
    third = []
    for r in range(radix):
        c, low1, high1 = coupling[r], ghosts1[2 * r], ghosts1[2 * r + 1]
        low2, high2 = ghosts2[2 * r], ghosts2[2 * r + 1]
        third.append(
            add(
                rhs[2][2 * r],
                times(c[3], low2),
                times(c[4], high2),
                times(c[6], low1),
                times(c[8], high1),
            )
        )
        third.append(
            add(
                rhs[2][2 * r + 1],
                times(c[4], low2),
                times(c[5], high2),
                times(c[7], low1),
                times(c[9], high1),
            )
        )
    return (first, second, third), (ghosts1, ghosts2, third)


def merged_coupling(level, coupling):
    radix = level.radix
    from_first, from_second, across = [], [], []
    for side in range(2):
        passed = level.passed[:, side]
        moved2, moved3 = [], []
        for r in range(radix):
            c, low, high = coupling[r], float(passed[2 * r]), float(passed[2 * r + 1])
            moved2 += [c[0] * low + c[1] * high, c[1] * low + c[2] * high]
            moved3 += [c[3] * low + c[4] * high, c[4] * low + c[5] * high]
        inner = [combine(level.ghosts[k], moved2) for k in range(2 * radix)]
        through = []
        for r in range(radix):
            c, low, high = coupling[r], float(passed[2 * r]), float(passed[2 * r + 1])
            k_low, k_high = inner[2 * r], inner[2 * r + 1]
            through.append(
                add(c[6] * low + c[8] * high, times(c[3], k_low), times(c[4], k_high))
            )
            through.append(
                add(c[7] * low + c[9] * high, times(c[4], k_low), times(c[5], k_high))
            )
        for end in range(2):
            if side <= end:
                from_first.append(combine(level.ends[end], moved2))
                from_second.append(combine(level.ends[end], moved3))
            across.append(combine(level.ends[end], through))
    return from_first + from_second + across


def gather_children(level, received, ordered_ref):
    position = digit(level)
    for s in range(level.radix):
        ordered_ref[position ^ s] = received[s][...]


def read_children(level, rhs_ref, coupling_ref):
    rows, radix = level.rows, level.radix

    def value(ref, r, v):
        return ref[r, v * rows : (v + 1) * rows, :]

    rhs = [
        [value(rhs_ref, k // 2, 2 * component + k % 2) for k in range(2 * radix)]
        for component in range(3)
    ]
    coupling = [
        [value(coupling_ref, r, v) for v in range(RHS, COUPLED)] for r in range(radix)
    ]
    return rhs, coupling


def up_kernel(level, above, coupled, *refs):
    radix, rows = level.radix, above.rows
    received, refs = refs[:radix], refs[radix:]
    if coupled:
        outs, (ordered_ref, staged_ref) = refs[:-2], refs[-2:]
        coupling_ref = ordered_ref
    else:
        coupling_ref, refs = refs[0], refs[1:]
        outs, (ordered_ref, staged_ref) = refs[:-2], refs[-2:]
    gather_children(level, received, ordered_ref)
    rhs, coupling = read_children(level, ordered_ref, coupling_ref)
    seen, _ = solve_children(level, rhs, coupling, None)
    sent = []
    for component in range(3):
        for end in range(2):
            sent.append(combine(level.ends[end], seen[component]))
    if coupled:
        sent += merged_coupling(level, coupling)
    for v, value in enumerate(sent):
        for chunk in range(above.radix):
            staged_ref[chunk, v * rows : (v + 1) * rows, :] = value[
                chunk * rows : (chunk + 1) * rows
            ]
    position = digit(above)
    for s in range(above.radix):
        outs[s][...] = staged_ref[position ^ s]


def send_down(level, rhs, coupling, outer, outs, staged_ref):
    rows = level.rows
    _, (ghosts1, ghosts2, third) = solve_children(level, rhs, coupling, outer)
    ghosts3 = []
    for k in range(2 * level.radix):
        own = combine(level.ghosts[k], third)
        if outer is not None:
            own = add(own, combine(level.passed[k], outer[2]))
        ghosts3.append(own)
    for component, ghosts in enumerate((ghosts1, ghosts2, ghosts3)):
        for k, ghost in enumerate(ghosts):
            v = 2 * component + k % 2
            if ghost is None:
                ghost = jnp.zeros((rows, LANES), jnp.float32)
            staged_ref[k // 2, v * rows : (v + 1) * rows, :] = ghost
    position = digit(level)
    for s in range(level.radix):
        outs[s][...] = staged_ref[position ^ s]


def top_kernel(level, coupled, *refs):
    radix = level.radix
    received, refs = refs[:radix], refs[radix:]
    if coupled:
        outs, (ordered_ref, staged_ref) = refs[:-2], refs[-2:]
        coupling_ref = ordered_ref
    else:
        coupling_ref, refs = refs[0], refs[1:]
        outs, (ordered_ref, staged_ref) = refs[:-2], refs[-2:]
    gather_children(level, received, ordered_ref)
    rhs, coupling = read_children(level, ordered_ref, coupling_ref)
    send_down(level, rhs, coupling, None, outs, staged_ref)


def down_kernel(level, above, *refs):
    radix, rows = above.radix, above.rows
    received, refs = refs[:radix], refs[radix:]
    rhs_ref, coupling_ref, refs = refs[0], refs[1], refs[2:]
    outs, (ordered_ref, staged_ref) = refs[:-2], refs[-2:]
    gather_children(above, received, ordered_ref)
    outer = [
        [
            jnp.concatenate(
                [
                    ordered_ref[chunk, v * rows : (v + 1) * rows, :]
                    for chunk in range(above.radix)
                ],
                axis=0,
            )
            for v in (2 * component, 2 * component + 1)
        ]
        for component in range(3)
    ]
    rhs, coupling = read_children(level, rhs_ref, coupling_ref)
    send_down(level, rhs, coupling, outer, outs, staged_ref)


def chunk_tiles(level, width):
    per = width // LANES // level.radix
    position = digit(level)
    for s in range(level.radix):
        for k in range(per):
            tile = (position ^ s) * per + k
            yield s, k, pl.ds(pl.multiple_of(tile * LANES, LANES), LANES)


def pinned(source, pins_ref, component, lanes):
    position = lax.axis_index("gx")
    first = jnp.where(position == 0, diffusion, 0.0).astype(jnp.float32)
    last = jnp.where(position == lax.axis_size("gx") - 1, diffusion, 0.0).astype(jnp.float32)
    source[0] = source[0] + first * pins_ref[0, component, :, lanes]
    source[-1] = source[-1] + last * pins_ref[1, component, :, lanes]
    return source


def solve_components(line, field_ref, axes_ref, pins_ref, lanes, ghosts):
    planes = line.planes
    field = [[field_ref[c, i, :, lanes] for i in range(planes)] for c in range(3)]
    axes = [[axes_ref[c, i, :, lanes] for i in range(planes)] for c in range(3)]
    for component in range(3):
        source = []
        for i in range(planes):
            projection = (
                field[0][i] * axes[0][i] + field[1][i] * axes[1][i] + field[2][i] * axes[2][i]
            )
            source.append(
                field[component][i] + (anisotropy_rate * projection) * axes[component][i]
            )
        source = pinned(source, pins_ref, component, lanes)
        if ghosts is not None:
            source[0] = source[0] + diffusion * ghosts[component][0]
            source[-1] = source[-1] + diffusion * ghosts[component][1]
        field[component] = line.solve(source)
    return field


def couplings(line, axes_ref, lanes):
    planes = line.planes
    low, high = line.from_low, line.from_high
    axes = [[axes_ref[c, i, :, lanes] for i in range(planes)] for c in range(3)]
    scaled = [anisotropy_rate * a for a in axes[1]]
    first_second = [axes[0][i] * scaled[i] for i in range(planes)]
    second_third = [axes[2][i] * scaled[i] for i in range(planes)]
    first_third = [(anisotropy_rate * axes[0][i]) * axes[2][i] for i in range(planes)]

    def weighted(terms, weights):
        total = terms[0] * float(weights[0] / diffusion)
        for i in range(1, planes):
            total = total + terms[i] * float(weights[i] / diffusion)
        return total

    found = []
    for product in (first_second, second_third):
        for weights in (low * low, low * high, high * high):
            found.append(weighted(product, weights))
    for ghost in (low, high):
        moved = line.solve([first_second[i] * float(ghost[i]) for i in range(planes)])
        pushed = [
            second_third[i] * moved[i] + first_third[i] * float(ghost[i]) for i in range(planes)
        ]
        found.append(weighted(pushed, low))
        found.append(weighted(pushed, high))
    return found


def send_edges(line, level, coupled, field_ref, axes_ref, pins_ref, outs):
    rows, width = field_ref.shape[2:]
    for s, k, lanes in chunk_tiles(level, width):
        solved = solve_components(line, field_ref, axes_ref, pins_ref, lanes, None)
        sent = []
        for component in range(3):
            sent += [solved[component][0], solved[component][-1]]
        if coupled:
            sent += couplings(line, axes_ref, lanes)
        for v, value in enumerate(sent):
            start = v * level.rows + k * rows
            outs[s][start : start + rows, :] = value


def send_kernel(line, level, field_ref, axes_ref, pins_ref, *outs):
    send_edges(line, level, True, field_ref, axes_ref, pins_ref, outs)


def finish_kernel(line, level, *refs):
    radix, planes = level.radix, line.planes
    received, refs = refs[:radix], refs[radix:]
    field_ref, axes_ref, pins_ref, out_ref, low_ref, high_ref = refs
    rows, width = field_ref.shape[2:]
    for s, k, lanes in chunk_tiles(level, width):
        ghosts = []
        for component in range(3):
            starts = [(2 * component + side) * level.rows + k * rows for side in range(2)]
            ghosts.append([received[s][start : start + rows, :] for start in starts])
        solved = solve_components(line, field_ref, axes_ref, pins_ref, lanes, ghosts)
        for c in range(3):
            for i in range(planes):
                at = c * planes + i
                out_ref[c, i, :, lanes] = solved[c][i]
                low_ref[at : at + 1, lanes] = solved[c][i][:1]
                high_ref[at : at + 1, lanes] = solved[c][i][rows - 1 :]


def rotate(field_ref, below_ref, above_ref, axes_ref, out_ref):
    planes, rows, width = field_ref.shape[1:]
    row = lax.broadcasted_iota(jnp.int32, (rows, width), 0)
    for i in range(planes):
        field = [field_ref[c, i] for c in range(3)]
        axes = [axes_ref[c, i] for c in range(3)]
        projection = field[0] * axes[0] + field[1] * axes[1] + field[2] * axes[2]
        effective = []
        for c in range(3):
            at = c * planes + i
            below = jnp.where(
                row == 0, below_ref[at : at + 1, :], pltpu.roll(field[c], 1, 0)
            )
            above = jnp.where(
                row == rows - 1, above_ref[at : at + 1, :], pltpu.roll(field[c], rows - 1, 0)
            )
            beside = pltpu.roll(field[c], 1, 1) + pltpu.roll(field[c], width - 1, 1)
            effective.append(
                exchange_rate * (((above + below) + beside) - 4.0 * field[c])
                + projection * axes[c]
            )
        rotated = []
        for c in range(3):
            d, e = (c + 1) % 3, (c + 2) % 3
            twisted = field[d] * effective[e] - field[e] * effective[d]
            rotated.append(field[c] - torque_rate * twisted)
        square = rotated[0] * rotated[0] + rotated[1] * rotated[1] + rotated[2] * rotated[2]
        scale = jnp.minimum(lax.rsqrt(square), 1.0 / norm_floor)
        for c in range(3):
            out_ref[c, i] = rotated[c] * scale


def rotate_and_send_kernel(
    line, level, field_ref, below_ref, above_ref, axes_ref, pins_ref, out_ref, *outs
):
    rotate(field_ref, below_ref, above_ref, axes_ref, out_ref)
    send_edges(line, level, False, out_ref, axes_ref, pins_ref, outs)


VMEM = pl.BlockSpec(memory_space=pltpu.VMEM)
LIMIT = pltpu.CompilerParams(vmem_limit_bytes=32 * 1024 * 1024)


def call(kernel, shapes, *operands, scratch=()):
    shapes = [jax.ShapeDtypeStruct(shape, jnp.float32) for shape in shapes]
    return pl.pallas_call(
        kernel,
        out_shape=tuple(shapes),
        in_specs=[VMEM] * len(operands),
        out_specs=(VMEM,) * len(shapes),
        scratch_shapes=[pltpu.VMEM(shape, jnp.float32) for shape in scratch],
        compiler_params=LIMIT,
    )(*operands)


def exchange(level, blocks):
    groups = lax.axis_size("gx")
    received = [blocks[0]]
    for s in range(1, level.radix):
        pairs = [(i, i ^ (s << level.shift)) for i in range(groups)]
        received.append(lax.ppermute(blocks[s], "gx", pairs))
    return received


def to_neighbours(low, high):
    count = lax.axis_size("gy")
    forward = [(i, (i + 1) % count) for i in range(count)]
    backward = [(target, source) for source, target in forward]
    return lax.ppermute(high, "gy", forward), lax.ppermute(low, "gy", backward)


def make_levels(planes, lines, groups):
    found = []
    length, rows, shift = planes, lines // LANES, 0
    for radix in radices_of(groups):
        rows //= radix
        found.append(Level(length, radix, shift, rows))
        length *= radix
        shift += radix.bit_length() - 1
    return found


def settle_ghosts(levels, blocks, coupled, kept):
    values = COUPLED if coupled else RHS
    orders = []
    for at, level in enumerate(levels):
        received = exchange(level, blocks)
        extra = [] if coupled else [kept[at]]
        ordered = (level.radix, values * level.rows, LANES)
        down = (RHS * level.rows, LANES)
        if at + 1 < len(levels):
            above = levels[at + 1]
            up = (values * above.rows, LANES)
            found = call(
                functools.partial(up_kernel, level, above, coupled),
                [up] * above.radix + [ordered],
                *received,
                *extra,
                scratch=[(above.radix, values * above.rows, LANES)],
            )
        else:
            found = call(
                functools.partial(top_kernel, level, coupled),
                [down] * level.radix + [ordered],
                *received,
                *extra,
                scratch=[(level.radix, RHS * level.rows, LANES)],
            )
        blocks, ordered = found[:-1], found[-1]
        orders.append(ordered)
    if coupled:
        kept = orders
    for at in range(len(levels) - 1, -1, -1):
        received = exchange(levels[at], blocks)
        if at == 0:
            return received, kept
        level, above = levels[at - 1], levels[at]
        down = (RHS * level.rows, LANES)
        blocks = call(
            functools.partial(down_kernel, level, above),
            [down] * level.radix,
            *received,
            orders[at - 1],
            kept[at - 1],
            scratch=[
                (above.radix, RHS * above.rows, LANES),
                (level.radix, RHS * level.rows, LANES),
            ],
        )


def per_device(magnetization, easy_axes, pins):
    _, planes, rows, width = magnetization.shape
    groups = lax.axis_size("gx")
    line = Line(planes)
    levels = make_levels(planes, rows * width, groups)
    lowest = levels[0]
    whole = magnetization.shape
    edge = (3 * planes, width)

    field = magnetization
    blocks = call(
        functools.partial(send_kernel, line, lowest),
        [(COUPLED * lowest.rows, LANES)] * lowest.radix,
        field,
        easy_axes,
        pins,
    )
    kept = None
    for stepno in range(STEPS):
        ghosts, kept = settle_ghosts(levels, blocks, stepno == 0, kept)
        solved, low, high = call(
            functools.partial(finish_kernel, line, lowest),
            [whole, edge, edge],
            *ghosts,
            field,
            easy_axes,
            pins,
        )
        below, above = to_neighbours(low, high)
        if stepno < STEPS - 1:
            field, *blocks = call(
                functools.partial(rotate_and_send_kernel, line, lowest),
                [whole] + [(RHS * lowest.rows, LANES)] * lowest.radix,
                solved,
                below,
                above,
                easy_axes,
                pins,
            )
        else:
            (field,) = call(rotate, [whole], solved, below, above, easy_axes)
    return field


def solution(mesh):
    in_specs = (P(None, "gx", "gy", None), P(None, "gx", "gy", None), P(None, None, "gy", None))
    out_specs = P(None, "gx", "gy", None)
    return jax.shard_map(
        per_device, mesh=mesh, in_specs=in_specs, out_specs=out_specs, check_vma=False
    )
```

```python
import functools

import jax
import jax.numpy as jnp
import numpy as np
from jax import lax
from jax.experimental import pallas as pl
from jax.experimental.pallas import tpu as pltpu
from jax.sharding import PartitionSpec as P

STEPS = 2
LANES = 128
RHS = 6
COUPLED = 16

diffusion = 4000.0
anisotropy_rate = 0.3
torque_rate = 0.2
exchange_rate = 0.1
norm_floor = 0.5


class Line:
    def __init__(self, planes):
        leading = 1.0 + 2.0 * diffusion
        pivots = [leading]
        for _ in range(1, planes):
            pivots.append(leading - diffusion * diffusion / pivots[-1])
        self.planes = planes
        self.inverse_pivot = [1.0 / p for p in pivots]
        self.factor = [0.0] + [diffusion / p for p in pivots[:-1]]
        block = (
            leading * np.eye(planes)
            - diffusion * np.eye(planes, k=1)
            - diffusion * np.eye(planes, k=-1)
        )
        self.from_low = diffusion * np.linalg.inv(block)[:, 0]
        self.from_high = self.from_low[::-1]

    def solve(self, source):
        planes = self.planes
        carried = [source[0]]
        for i in range(1, planes):
            carried.append(source[i] + self.factor[i] * carried[-1])
        solved = [None] * planes
        solved[-1] = carried[-1] * self.inverse_pivot[-1]
        for i in range(planes - 2, -1, -1):
            solved[i] = carried[i] * self.inverse_pivot[i] + self.factor[i + 1] * solved[i + 1]
        return solved


class Level:
    def __init__(self, length, radix, shift, rows):
        self.radix, self.shift, self.rows = radix, shift, rows
        line = Line(length)
        near, far = line.from_low[0], line.from_low[-1]
        count = 2 * radix
        inside = np.kron(np.eye(radix), np.array([[near, far], [far, near]]))
        pick = np.zeros((count, count))
        for r in range(radix):
            if r > 0:
                pick[2 * r, 2 * r - 1] = 1.0
            if r < radix - 1:
                pick[2 * r + 1, 2 * r + 2] = 1.0
        outer = np.zeros((count, 2))
        outer[0, 0] = outer[count - 1, 1] = 1.0
        settle = np.linalg.inv(np.eye(count) - pick @ inside)
        self.ghosts = settle @ pick
        self.passed = settle @ outer
        ends = (np.eye(count) + inside @ self.ghosts)[[0, count - 1]]
        self.ends = ends


def radices_of(groups):
    found = []
    while groups > 1:
        radix = 4 if groups % 4 == 0 else 2
        assert groups % radix == 0
        found.append(radix)
        groups //= radix
    return found


def combine(weights, terms):
    total = None
    for weight, term in zip(weights, terms):
        if weight == 0.0 or term is None:
            continue
        part = term * float(weight)
        total = part if total is None else total + part
    return total


def add(*terms):
    kept = [t for t in terms if t is not None]
    total = kept[0] if kept else None
    for term in kept[1:]:
        total = total + term
    return total


def times(left, right):
    return None if right is None else left * right


def solve_children(level, rhs, coupling, outer):
    radix = level.radix

    def settle(values, component):
        found = []
        for k in range(2 * radix):
            own = combine(level.ghosts[k], values)
            if outer is not None:
                own = add(own, combine(level.passed[k], outer[component]))
            found.append(own)
        return found

    first = rhs[0]
    ghosts1 = settle(first, 0)
    second = []
    for r in range(radix):
        c, low, high = coupling[r], ghosts1[2 * r], ghosts1[2 * r + 1]
        second.append(add(rhs[1][2 * r], times(c[0], low), times(c[1], high)))
        second.append(add(rhs[1][2 * r + 1], times(c[1], low), times(c[2], high)))
    ghosts2 = settle(second, 1)
    third = []
    for r in range(radix):
        c, low1, high1 = coupling[r], ghosts1[2 * r], ghosts1[2 * r + 1]
        low2, high2 = ghosts2[2 * r], ghosts2[2 * r + 1]
        third.append(
            add(
                rhs[2][2 * r],
                times(c[3], low2),
                times(c[4], high2),
                times(c[6], low1),
                times(c[8], high1),
            )
        )
        third.append(
            add(
                rhs[2][2 * r + 1],
                times(c[4], low2),
                times(c[5], high2),
                times(c[7], low1),
                times(c[9], high1),
            )
        )
    return (first, second, third), (ghosts1, ghosts2, third)


def merged_coupling(level, coupling):
    radix = level.radix
    from_first, from_second, across = [], [], []
    for side in range(2):
        passed = level.passed[:, side]
        moved2, moved3 = [], []
        for r in range(radix):
            c, low, high = coupling[r], float(passed[2 * r]), float(passed[2 * r + 1])
            moved2 += [c[0] * low + c[1] * high, c[1] * low + c[2] * high]
            moved3 += [c[3] * low + c[4] * high, c[4] * low + c[5] * high]
        inner = [combine(level.ghosts[k], moved2) for k in range(2 * radix)]
        through = []
        for r in range(radix):
            c, low, high = coupling[r], float(passed[2 * r]), float(passed[2 * r + 1])
            k_low, k_high = inner[2 * r], inner[2 * r + 1]
            through.append(
                add(c[6] * low + c[8] * high, times(c[3], k_low), times(c[4], k_high))
            )
            through.append(
                add(c[7] * low + c[9] * high, times(c[4], k_low), times(c[5], k_high))
            )
        for end in range(2):
            if side <= end:
                from_first.append(combine(level.ends[end], moved2))
                from_second.append(combine(level.ends[end], moved3))
            across.append(combine(level.ends[end], through))
    return from_first + from_second + across


def read_children(level, rhs_ref, coupling_ref):
    rows, radix = level.rows, level.radix

    def value(ref, r, v):
        return ref[r, v * rows : (v + 1) * rows, :]

    rhs = [
        [value(rhs_ref, k // 2, 2 * component + k % 2) for k in range(2 * radix)]
        for component in range(3)
    ]
    coupling = [
        [value(coupling_ref, r, v) for v in range(RHS, COUPLED)] for r in range(radix)
    ]
    return rhs, coupling


def up_kernel(level, above, coupled, rhs_ref, coupling_ref, out_ref):
    rows = above.rows
    rhs, coupling = read_children(level, rhs_ref, coupling_ref)
    seen, _ = solve_children(level, rhs, coupling, None)
    sent = []
    for component in range(3):
        for end in range(2):
            sent.append(combine(level.ends[end], seen[component]))
    if coupled:
        sent += merged_coupling(level, coupling)
    for v, value in enumerate(sent):
        for chunk in range(above.radix):
            out_ref[chunk, v * rows : (v + 1) * rows, :] = value[
                chunk * rows : (chunk + 1) * rows
            ]


def send_down(level, rhs, coupling, outer, out_ref):
    rows = level.rows
    _, (ghosts1, ghosts2, third) = solve_children(level, rhs, coupling, outer)
    ghosts3 = []
    for k in range(2 * level.radix):
        own = combine(level.ghosts[k], third)
        if outer is not None:
            own = add(own, combine(level.passed[k], outer[2]))
        ghosts3.append(own)
    for component, ghosts in enumerate((ghosts1, ghosts2, ghosts3)):
        for k, ghost in enumerate(ghosts):
            v = 2 * component + k % 2
            if ghost is None:
                ghost = jnp.zeros((rows, LANES), jnp.float32)
            out_ref[k // 2, v * rows : (v + 1) * rows, :] = ghost


def top_kernel(level, rhs_ref, coupling_ref, out_ref):
    rhs, coupling = read_children(level, rhs_ref, coupling_ref)
    send_down(level, rhs, coupling, None, out_ref)


def down_kernel(level, above, outer_ref, rhs_ref, coupling_ref, out_ref):
    rows = above.rows
    outer = [
        [
            jnp.concatenate(
                [
                    outer_ref[chunk, v * rows : (v + 1) * rows, :]
                    for chunk in range(above.radix)
                ],
                axis=0,
            )
            for v in (2 * component, 2 * component + 1)
        ]
        for component in range(3)
    ]
    rhs, coupling = read_children(level, rhs_ref, coupling_ref)
    send_down(level, rhs, coupling, outer, out_ref)


def chunk_tiles(level, width):
    per = width // LANES // level.radix
    for chunk in range(level.radix):
        for k in range(per):
            tile = chunk * per + k
            yield chunk, k, slice(tile * LANES, (tile + 1) * LANES)


def pinned(source, pins_ref, component, lanes):
    position = lax.axis_index("gx")
    first = jnp.where(position == 0, diffusion, 0.0).astype(jnp.float32)
    last = jnp.where(position == lax.axis_size("gx") - 1, diffusion, 0.0).astype(jnp.float32)
    source[0] = source[0] + first * pins_ref[0, component, :, lanes]
    source[-1] = source[-1] + last * pins_ref[1, component, :, lanes]
    return source


def solve_components(line, field_ref, axes_ref, pins_ref, lanes, ghosts):
    planes = line.planes
    field = [[field_ref[c, i, :, lanes] for i in range(planes)] for c in range(3)]
    axes = [[axes_ref[c, i, :, lanes] for i in range(planes)] for c in range(3)]
    for component in range(3):
        source = []
        for i in range(planes):
            projection = (
                field[0][i] * axes[0][i] + field[1][i] * axes[1][i] + field[2][i] * axes[2][i]
            )
            source.append(
                field[component][i] + (anisotropy_rate * projection) * axes[component][i]
            )
        source = pinned(source, pins_ref, component, lanes)
        if ghosts is not None:
            source[0] = source[0] + diffusion * ghosts[component][0]
            source[-1] = source[-1] + diffusion * ghosts[component][1]
        field[component] = line.solve(source)
    return field


def couplings(line, axes_ref, lanes):
    planes = line.planes
    low, high = line.from_low, line.from_high
    axes = [[axes_ref[c, i, :, lanes] for i in range(planes)] for c in range(3)]
    scaled = [anisotropy_rate * a for a in axes[1]]
    first_second = [axes[0][i] * scaled[i] for i in range(planes)]
    second_third = [axes[2][i] * scaled[i] for i in range(planes)]
    first_third = [(anisotropy_rate * axes[0][i]) * axes[2][i] for i in range(planes)]

    def weighted(terms, weights):
        total = terms[0] * float(weights[0] / diffusion)
        for i in range(1, planes):
            total = total + terms[i] * float(weights[i] / diffusion)
        return total

    found = []
    for product in (first_second, second_third):
        for weights in (low * low, low * high, high * high):
            found.append(weighted(product, weights))
    for ghost in (low, high):
        moved = line.solve([first_second[i] * float(ghost[i]) for i in range(planes)])
        pushed = [
            second_third[i] * moved[i] + first_third[i] * float(ghost[i]) for i in range(planes)
        ]
        found.append(weighted(pushed, low))
        found.append(weighted(pushed, high))
    return found


def send_edges(line, level, coupled, field_ref, axes_ref, pins_ref, out_ref):
    rows, width = field_ref.shape[2:]
    for chunk, k, lanes in chunk_tiles(level, width):
        solved = solve_components(line, field_ref, axes_ref, pins_ref, lanes, None)
        sent = []
        for component in range(3):
            sent += [solved[component][0], solved[component][-1]]
        if coupled:
            sent += couplings(line, axes_ref, lanes)
        for v, value in enumerate(sent):
            start = v * level.rows + k * rows
            out_ref[chunk, start : start + rows, :] = value


def send_kernel(line, level, field_ref, axes_ref, pins_ref, out_ref):
    send_edges(line, level, True, field_ref, axes_ref, pins_ref, out_ref)


def finish_kernel(
    line, level, ghost_ref, field_ref, axes_ref, pins_ref, out_ref, low_ref, high_ref
):
    planes = line.planes
    rows, width = field_ref.shape[2:]
    for chunk, k, lanes in chunk_tiles(level, width):
        ghosts = []
        for component in range(3):
            starts = [(2 * component + side) * level.rows + k * rows for side in range(2)]
            ghosts.append([ghost_ref[chunk, start : start + rows, :] for start in starts])
        solved = solve_components(line, field_ref, axes_ref, pins_ref, lanes, ghosts)
        for c in range(3):
            for i in range(planes):
                at = c * planes + i
                out_ref[c, i, :, lanes] = solved[c][i]
                low_ref[at : at + 1, lanes] = solved[c][i][:1]
                high_ref[at : at + 1, lanes] = solved[c][i][rows - 1 :]


def rotate(field_ref, below_ref, above_ref, axes_ref, out_ref):
    planes, rows, width = field_ref.shape[1:]
    row = lax.broadcasted_iota(jnp.int32, (rows, width), 0)
    for i in range(planes):
        field = [field_ref[c, i] for c in range(3)]
        axes = [axes_ref[c, i] for c in range(3)]
        projection = field[0] * axes[0] + field[1] * axes[1] + field[2] * axes[2]
        effective = []
        for c in range(3):
            at = c * planes + i
            below = jnp.where(
                row == 0, below_ref[at : at + 1, :], pltpu.roll(field[c], 1, 0)
            )
            above = jnp.where(
                row == rows - 1, above_ref[at : at + 1, :], pltpu.roll(field[c], rows - 1, 0)
            )
            beside = pltpu.roll(field[c], 1, 1) + pltpu.roll(field[c], width - 1, 1)
            effective.append(
                exchange_rate * (((above + below) + beside) - 4.0 * field[c])
                + projection * axes[c]
            )
        rotated = []
        for c in range(3):
            d, e = (c + 1) % 3, (c + 2) % 3
            twisted = field[d] * effective[e] - field[e] * effective[d]
            rotated.append(field[c] - torque_rate * twisted)
        square = rotated[0] * rotated[0] + rotated[1] * rotated[1] + rotated[2] * rotated[2]
        scale = jnp.minimum(lax.rsqrt(square), 1.0 / norm_floor)
        for c in range(3):
            out_ref[c, i] = rotated[c] * scale


def rotate_and_send_kernel(
    line, level, field_ref, below_ref, above_ref, axes_ref, pins_ref, out_ref, sent_ref
):
    rotate(field_ref, below_ref, above_ref, axes_ref, out_ref)
    send_edges(line, level, False, out_ref, axes_ref, pins_ref, sent_ref)


VMEM = pl.BlockSpec(memory_space=pltpu.VMEM)
LIMIT = pltpu.CompilerParams(vmem_limit_bytes=32 * 1024 * 1024)


def call(kernel, shapes, *operands, scratch=()):
    shapes = [jax.ShapeDtypeStruct(shape, jnp.float32) for shape in shapes]
    return pl.pallas_call(
        kernel,
        out_shape=tuple(shapes),
        in_specs=[VMEM] * len(operands),
        out_specs=(VMEM,) * len(shapes),
        scratch_shapes=[pltpu.VMEM(shape, jnp.float32) for shape in scratch],
        compiler_params=LIMIT,
    )(*operands)


def exchange(level, block):
    count = lax.axis_size("gx")
    step, span = 1 << level.shift, level.radix << level.shift
    members = [
        [start + low + step * r for r in range(level.radix)]
        for start in range(0, count, span)
        for low in range(step)
    ]
    return lax.all_to_all(
        block, "gx", split_axis=0, concat_axis=0, axis_index_groups=members, tiled=True
    )


def to_neighbours(low, high):
    count = lax.axis_size("gy")
    forward = [(i, (i + 1) % count) for i in range(count)]
    backward = [(target, source) for source, target in forward]
    return lax.ppermute(high, "gy", forward), lax.ppermute(low, "gy", backward)


def make_levels(planes, lines, groups):
    found = []
    length, rows, shift = planes, lines // LANES, 0
    for radix in radices_of(groups):
        rows //= radix
        found.append(Level(length, radix, shift, rows))
        length *= radix
        shift += radix.bit_length() - 1
    return found


def settle_ghosts(levels, block, coupled, kept):
    values = COUPLED if coupled else RHS
    orders = []
    for at, level in enumerate(levels):
        ordered = exchange(level, block)
        orders.append(ordered)
        coupling = ordered if coupled else kept[at]
        if at + 1 < len(levels):
            above = levels[at + 1]
            (block,) = call(
                functools.partial(up_kernel, level, above, coupled),
                [(above.radix, values * above.rows, LANES)],
                ordered,
                coupling,
            )
        else:
            (block,) = call(
                functools.partial(top_kernel, level),
                [(level.radix, RHS * level.rows, LANES)],
                ordered,
                coupling,
            )
    if coupled:
        kept = orders
    for at in range(len(levels) - 1, -1, -1):
        received = exchange(levels[at], block)
        if at == 0:
            return received, kept
        level, above = levels[at - 1], levels[at]
        (block,) = call(
            functools.partial(down_kernel, level, above),
            [(level.radix, RHS * level.rows, LANES)],
            received,
            orders[at - 1],
            kept[at - 1],
        )


def per_device(magnetization, easy_axes, pins):
    _, planes, rows, width = magnetization.shape
    groups = lax.axis_size("gx")
    line = Line(planes)
    levels = make_levels(planes, rows * width, groups)
    lowest = levels[0]
    whole = magnetization.shape
    edge = (3 * planes, width)

    field = magnetization
    (block,) = call(
        functools.partial(send_kernel, line, lowest),
        [(lowest.radix, COUPLED * lowest.rows, LANES)],
        field,
        easy_axes,
        pins,
    )
    kept = None
    for stepno in range(STEPS):
        ghosts, kept = settle_ghosts(levels, block, stepno == 0, kept)
        solved, low, high = call(
            functools.partial(finish_kernel, line, lowest),
            [whole, edge, edge],
            ghosts,
            field,
            easy_axes,
            pins,
        )
        below, above = to_neighbours(low, high)
        if stepno < STEPS - 1:
            field, block = call(
                functools.partial(rotate_and_send_kernel, line, lowest),
                [whole, (lowest.radix, RHS * lowest.rows, LANES)],
                solved,
                below,
                above,
                easy_axes,
                pins,
            )
        else:
            (field,) = call(rotate, [whole], solved, below, above, easy_axes)
    return field


def solution(mesh):
    in_specs = (P(None, "gx", "gy", None), P(None, "gx", "gy", None), P(None, None, "gy", None))
    out_specs = P(None, "gx", "gy", None)
    return jax.shard_map(
        per_device, mesh=mesh, in_specs=in_specs, out_specs=out_specs, check_vma=False
    )
```

```python
import functools

import jax
import jax.numpy as jnp
import numpy as np
from jax import lax
from jax.experimental import pallas as pl
from jax.experimental.pallas import tpu as pltpu
from jax.sharding import PartitionSpec as P

STEPS = 2
LANES = 128
RHS = 6
COUPLED = 16

diffusion = 4000.0
anisotropy_rate = 0.3
torque_rate = 0.2
exchange_rate = 0.1
norm_floor = 0.5


class Line:
    def __init__(self, planes):
        leading = 1.0 + 2.0 * diffusion
        pivots = [leading]
        for _ in range(1, planes):
            pivots.append(leading - diffusion * diffusion / pivots[-1])
        self.planes = planes
        self.inverse_pivot = [1.0 / p for p in pivots]
        self.factor = [0.0] + [diffusion / p for p in pivots[:-1]]
        block = (
            leading * np.eye(planes)
            - diffusion * np.eye(planes, k=1)
            - diffusion * np.eye(planes, k=-1)
        )
        self.from_low = diffusion * np.linalg.inv(block)[:, 0]
        self.from_high = self.from_low[::-1]

    def solve(self, source):
        planes = self.planes
        carried = [source[0]]
        for i in range(1, planes):
            carried.append(source[i] + self.factor[i] * carried[-1])
        solved = [None] * planes
        solved[-1] = carried[-1] * self.inverse_pivot[-1]
        for i in range(planes - 2, -1, -1):
            solved[i] = carried[i] * self.inverse_pivot[i] + self.factor[i + 1] * solved[i + 1]
        return solved


class Level:
    def __init__(self, length, radix):
        self.radix = radix
        line = Line(length)
        near, far = line.from_low[0], line.from_low[-1]
        count = 2 * radix
        inside = np.kron(np.eye(radix), np.array([[near, far], [far, near]]))
        pick = np.zeros((count, count))
        for r in range(radix):
            if r > 0:
                pick[2 * r, 2 * r - 1] = 1.0
            if r < radix - 1:
                pick[2 * r + 1, 2 * r + 2] = 1.0
        outer = np.zeros((count, 2))
        outer[0, 0] = outer[count - 1, 1] = 1.0
        settle = np.linalg.inv(np.eye(count) - pick @ inside)
        self.ghosts = settle @ pick
        self.passed = settle @ outer
        ends = (np.eye(count) + inside @ self.ghosts)[[0, count - 1]]
        self.ends = ends


def radices_of(groups):
    found = []
    while groups > 1:
        radix = 4 if groups % 4 == 0 else 2
        assert groups % radix == 0
        found.append(radix)
        groups //= radix
    return found


def combine(weights, terms):
    total = None
    for weight, term in zip(weights, terms):
        if weight == 0.0 or term is None:
            continue
        part = term * float(weight)
        total = part if total is None else total + part
    return total


def make_levels(planes, groups):
    found = []
    for radix in radices_of(groups):
        found.append(Level(planes, radix))
        planes *= radix
    return found


def settle(levels, ends):
    level, count = levels[0], 2 * levels[0].radix
    if len(levels) == 1:
        return [combine(weights, ends) for weights in level.ghosts]
    joined = []
    for start in range(0, len(ends), count):
        part = ends[start : start + count]
        joined += [combine(weights, part) for weights in level.ends]
    outer = settle(levels[1:], joined)
    found = []
    for at, start in enumerate(range(0, len(ends), count)):
        part = list(ends[start : start + count]) + [outer[2 * at], outer[2 * at + 1]]
        for inside, passed in zip(level.ghosts, level.passed):
            found.append(combine(list(inside) + list(passed), part))
    return found


def plus(total, weight, term):
    return total if term is None else total + weight * term


def row_window(value, values, units, tile, tiles, rows):
    start = (tile // units) * values * units + value * units + tile % units
    return pl.ds(start, rows, stride=tiles * values)


def pinned(source, pins_ref, component, lanes):
    position = lax.axis_index("gx")
    first = jnp.where(position == 0, diffusion, 0.0).astype(jnp.float32)
    last = jnp.where(position == lax.axis_size("gx") - 1, diffusion, 0.0).astype(jnp.float32)
    source[0] = source[0] + first * pins_ref[0, component, :, lanes]
    source[-1] = source[-1] + last * pins_ref[1, component, :, lanes]
    return source


def solve_components(line, field_ref, axes_ref, pins_ref, lanes, ghosts):
    planes = line.planes
    field = [[field_ref[c, i, :, lanes] for i in range(planes)] for c in range(3)]
    axes = [[axes_ref[c, i, :, lanes] for i in range(planes)] for c in range(3)]
    for component in range(3):
        source = []
        for i in range(planes):
            projection = (
                field[0][i] * axes[0][i] + field[1][i] * axes[1][i] + field[2][i] * axes[2][i]
            )
            source.append(
                field[component][i] + (anisotropy_rate * projection) * axes[component][i]
            )
        source = pinned(source, pins_ref, component, lanes)
        if ghosts is not None:
            source[0] = source[0] + diffusion * ghosts[component][0]
            source[-1] = source[-1] + diffusion * ghosts[component][1]
        field[component] = line.solve(source)
    return field


def couplings(line, axes_ref, lanes):
    planes = line.planes
    low, high = line.from_low, line.from_high
    axes = [[axes_ref[c, i, :, lanes] for i in range(planes)] for c in range(3)]
    scaled = [anisotropy_rate * a for a in axes[1]]
    first_second = [axes[0][i] * scaled[i] for i in range(planes)]
    second_third = [axes[2][i] * scaled[i] for i in range(planes)]
    first_third = [(anisotropy_rate * axes[0][i]) * axes[2][i] for i in range(planes)]

    def weighted(terms, weights):
        total = terms[0] * float(weights[0] / diffusion)
        for i in range(1, planes):
            total = total + terms[i] * float(weights[i] / diffusion)
        return total

    found = []
    for product in (first_second, second_third):
        for weights in (low * low, low * high, high * high):
            found.append(weighted(product, weights))
    for ghost in (low, high):
        moved = line.solve([first_second[i] * float(ghost[i]) for i in range(planes)])
        pushed = [
            second_third[i] * moved[i] + first_third[i] * float(ghost[i]) for i in range(planes)
        ]
        found.append(weighted(pushed, low))
        found.append(weighted(pushed, high))
    return found


def send_tile(line, units, coupled, field_ref, axes_ref, pins_ref, out_ref, tile):
    rows, width = field_ref.shape[2], field_ref.shape[3]
    tiles = width // LANES
    values = COUPLED if coupled else RHS
    lanes = slice(tile * LANES, (tile + 1) * LANES)
    solved = solve_components(line, field_ref, axes_ref, pins_ref, lanes, None)
    sent = []
    for component in range(3):
        sent += [solved[component][0], solved[component][-1]]
    if coupled:
        sent += couplings(line, axes_ref, lanes)
    for value in range(values):
        out_ref[row_window(value, values, units, tile, tiles, rows), :] = sent[value]


def first_kernel(
    line, units, field_hbm, axes_hbm, pins_hbm, out_ref, field_ref, axes_ref, pins_ref, sems, pin_sem
):
    tiles = field_ref.shape[3] // LANES
    pin_copy = pltpu.make_async_copy(pins_hbm, pins_ref, pin_sem)
    copies = []
    for tile in range(tiles):
        lanes = pl.ds(tile * LANES, LANES)
        at = (slice(None), slice(None), slice(None), lanes)
        copies.append(
            (
                pltpu.make_async_copy(axes_hbm.at[at], axes_ref.at[at], sems.at[0, tile]),
                pltpu.make_async_copy(field_hbm.at[at], field_ref.at[at], sems.at[1, tile]),
            )
        )
        for copy in copies[-1]:
            copy.start()
        if tile == 0:
            pin_copy.start()
    for tile in range(tiles):
        for copy in copies[tile]:
            copy.wait()
        if tile == 0:
            pin_copy.wait()
        send_tile(line, units, True, field_ref, axes_ref, pins_ref, out_ref, tile)


def reduced_kernel(levels, groups, units, rhs_values, rhs_ref, coupling_ref, out_ref):
    def read(ref, values, d, value):
        start = (d * values + value) * units
        return ref[start : start + units, :]

    rhs = [
        [read(rhs_ref, rhs_values, k // 2, 2 * c + k % 2) for k in range(2 * groups)]
        for c in range(3)
    ]

    def coupling(d, value):
        return read(coupling_ref, COUPLED, d, RHS + value)

    first = settle(levels, rhs[0])
    for d in range(groups):
        low, high = first[2 * d], first[2 * d + 1]
        mixed = coupling(d, 1)
        rhs[1][2 * d] = plus(plus(rhs[1][2 * d], coupling(d, 0), low), mixed, high)
        rhs[1][2 * d + 1] = plus(plus(rhs[1][2 * d + 1], mixed, low), coupling(d, 2), high)
    second = settle(levels, rhs[1])
    for d in range(groups):
        low1, high1 = first[2 * d], first[2 * d + 1]
        low2, high2 = second[2 * d], second[2 * d + 1]
        mixed = coupling(d, 4)
        total = plus(plus(rhs[2][2 * d], coupling(d, 3), low2), mixed, high2)
        rhs[2][2 * d] = plus(plus(total, coupling(d, 6), low1), coupling(d, 8), high1)
        total = plus(plus(rhs[2][2 * d + 1], mixed, low2), coupling(d, 5), high2)
        rhs[2][2 * d + 1] = plus(plus(total, coupling(d, 7), low1), coupling(d, 9), high1)
    third = settle(levels, rhs[2])
    for c, ghosts in enumerate((first, second, third)):
        for k, ghost in enumerate(ghosts):
            start = (k // 2 * RHS + 2 * c + k % 2) * units
            if ghost is None:
                ghost = jnp.zeros((units, LANES), jnp.float32)
            out_ref[start : start + units, :] = ghost


def finish_kernel(line, units, field_ref, axes_ref, pins_ref, ghost_ref, out_ref, edge_ref):
    planes = line.planes
    rows, width = field_ref.shape[2], field_ref.shape[3]
    tiles = width // LANES
    for tile in range(tiles):
        lanes = slice(tile * LANES, (tile + 1) * LANES)
        ghosts = [
            [
                ghost_ref[row_window(2 * c + side, RHS, units, tile, tiles, rows), :]
                for side in range(2)
            ]
            for c in range(3)
        ]
        solved = solve_components(line, field_ref, axes_ref, pins_ref, lanes, ghosts)
        for c in range(3):
            for i in range(planes):
                out_ref[c, i, :, lanes] = solved[c][i]
                at = c * planes + i
                edge_ref[0, at : at + 1, lanes] = solved[c][i][:1]
                edge_ref[1, at : at + 1, lanes] = solved[c][i][rows - 1 :]


def rotate(field_ref, beyond_ref, axes_ref, out_ref, finished=None):
    planes, rows, width = field_ref.shape[1:]
    row = lax.broadcasted_iota(jnp.int32, (rows, width), 0)
    for i in range(planes):
        field = [field_ref[c, i] for c in range(3)]
        axes = [axes_ref[c, i] for c in range(3)]
        projection = field[0] * axes[0] + field[1] * axes[1] + field[2] * axes[2]
        effective = []
        for c in range(3):
            at = c * planes + i
            below = jnp.where(
                row == 0, beyond_ref[1, at : at + 1, :], pltpu.roll(field[c], 1, 0)
            )
            above = jnp.where(
                row == rows - 1, beyond_ref[0, at : at + 1, :], pltpu.roll(field[c], rows - 1, 0)
            )
            beside = pltpu.roll(field[c], 1, 1) + pltpu.roll(field[c], width - 1, 1)
            effective.append(
                exchange_rate * (((above + below) + beside) - 4.0 * field[c])
                + projection * axes[c]
            )
        rotated = []
        for c in range(3):
            d, e = (c + 1) % 3, (c + 2) % 3
            twisted = field[d] * effective[e] - field[e] * effective[d]
            rotated.append(field[c] - torque_rate * twisted)
        square = rotated[0] * rotated[0] + rotated[1] * rotated[1] + rotated[2] * rotated[2]
        scale = jnp.minimum(lax.rsqrt(square), 1.0 / norm_floor)
        for c in range(3):
            out_ref[c, i] = rotated[c] * scale
        if finished is not None:
            finished(i)


def rotate_and_send_kernel(
    line, units, field_ref, beyond_ref, axes_ref, pins_ref, out_ref, sent_ref
):
    rotate(field_ref, beyond_ref, axes_ref, out_ref)
    for tile in range(field_ref.shape[3] // LANES):
        send_tile(line, units, False, out_ref, axes_ref, pins_ref, sent_ref, tile)


def last_kernel(field_ref, beyond_ref, axes_ref, out_hbm, out_ref, sems):
    def copy(i):
        return pltpu.make_async_copy(out_ref.at[:, i], out_hbm.at[:, i], sems.at[i])

    rotate(field_ref, beyond_ref, axes_ref, out_ref, lambda i: copy(i).start())
    for i in range(field_ref.shape[1]):
        copy(i).wait()


VMEM = pl.BlockSpec(memory_space=pltpu.VMEM)
HBM = pl.BlockSpec(memory_space=pltpu.HBM)
SMALL = 32 * 1024 * 1024
LARGE = 63 * 1024 * 1024


def call(kernel, shapes, *operands, read=VMEM, written=VMEM, scratch=(), limit=SMALL):
    shapes = [jax.ShapeDtypeStruct(shape, jnp.float32) for shape in shapes]
    return pl.pallas_call(
        kernel,
        out_shape=tuple(shapes),
        in_specs=[read] * len(operands),
        out_specs=(written,) * len(shapes),
        scratch_shapes=scratch,
        compiler_params=pltpu.CompilerParams(vmem_limit_bytes=limit),
    )(*operands)


def exchange(block, groups):
    parts = block.reshape(groups, -1, LANES)
    return lax.all_to_all(parts, "gx", split_axis=0, concat_axis=0, tiled=True).reshape(
        block.shape
    )


def from_neighbours(edges):
    count = lax.axis_size("gy")
    forward = [(i, (i + 1) % count) for i in range(count)]
    if count == 2:
        return lax.ppermute(edges, "gy", forward)
    backward = [(target, source) for source, target in forward]
    return jnp.stack(
        [lax.ppermute(edges[0], "gy", backward), lax.ppermute(edges[1], "gy", forward)]
    )


def per_device(magnetization, easy_axes, pins):
    _, planes, rows, width = magnetization.shape
    groups = lax.axis_size("gx")
    tiles = width // LANES
    units = rows * tiles // groups
    line = Line(planes)
    levels = make_levels(planes, groups)
    whole = magnetization.shape
    sent_shape = (groups * RHS * units, LANES)

    field = magnetization
    (sent,) = call(
        functools.partial(first_kernel, line, units),
        [(groups * COUPLED * units, LANES)],
        field,
        easy_axes,
        pins,
        read=HBM,
        scratch=[
            pltpu.VMEM(whole, jnp.float32),
            pltpu.VMEM(whole, jnp.float32),
            pltpu.VMEM(pins.shape, jnp.float32),
            pltpu.SemaphoreType.DMA((2, tiles)),
            pltpu.SemaphoreType.DMA,
        ],
        limit=LARGE,
    )
    coupling = None
    for stepno in range(STEPS):
        gathered = exchange(sent, groups)
        if stepno == 0:
            coupling = gathered
        (ghosts,) = call(
            functools.partial(reduced_kernel, levels, groups, units, RHS if stepno else COUPLED),
            [sent_shape],
            gathered,
            coupling,
        )
        ghosts = exchange(ghosts, groups)
        solved, edges = call(
            functools.partial(finish_kernel, line, units),
            [whole, (2, 3 * planes, width)],
            field,
            easy_axes,
            pins,
            ghosts,
        )
        beyond = from_neighbours(edges)
        if stepno < STEPS - 1:
            field, sent = call(
                functools.partial(rotate_and_send_kernel, line, units),
                [whole, sent_shape],
                solved,
                beyond,
                easy_axes,
                pins,
            )
        else:
            (field,) = call(
                last_kernel,
                [whole],
                solved,
                beyond,
                easy_axes,
                written=HBM,
                scratch=[pltpu.VMEM(whole, jnp.float32), pltpu.SemaphoreType.DMA((planes,))],
            )
    return field


def solution(mesh):
    in_specs = (P(None, "gx", "gy", None), P(None, "gx", "gy", None), P(None, None, "gy", None))
    out_specs = P(None, "gx", "gy", None)
    return jax.shard_map(
        per_device, mesh=mesh, in_specs=in_specs, out_specs=out_specs, check_vma=False
    )
```

```python
import functools

import jax
import jax.numpy as jnp
import numpy as np
from jax import lax
from jax.experimental import pallas as pl
from jax.experimental.pallas import tpu as pltpu
from jax.sharding import PartitionSpec as P

STEPS = 2
LANES = 128
RHS = 6
COUPLED = 16

diffusion = 4000.0
anisotropy_rate = 0.3
torque_rate = 0.2
exchange_rate = 0.1
norm_floor = 0.5


class Line:
    def __init__(self, planes):
        leading = 1.0 + 2.0 * diffusion
        pivots = [leading]
        for _ in range(1, planes):
            pivots.append(leading - diffusion * diffusion / pivots[-1])
        self.planes = planes
        self.inverse_pivot = [1.0 / p for p in pivots]
        self.factor = [0.0] + [diffusion / p for p in pivots[:-1]]
        block = (
            leading * np.eye(planes)
            - diffusion * np.eye(planes, k=1)
            - diffusion * np.eye(planes, k=-1)
        )
        self.from_low = diffusion * np.linalg.inv(block)[:, 0]
        self.from_high = self.from_low[::-1]

    def solve(self, source):
        planes = self.planes
        carried = [source[0]]
        for i in range(1, planes):
            carried.append(source[i] + self.factor[i] * carried[-1])
        solved = [None] * planes
        solved[-1] = carried[-1] * self.inverse_pivot[-1]
        for i in range(planes - 2, -1, -1):
            solved[i] = carried[i] * self.inverse_pivot[i] + self.factor[i + 1] * solved[i + 1]
        return solved


class Level:
    def __init__(self, length, radix):
        self.radix = radix
        line = Line(length)
        near, far = line.from_low[0], line.from_low[-1]
        count = 2 * radix
        inside = np.kron(np.eye(radix), np.array([[near, far], [far, near]]))
        pick = np.zeros((count, count))
        for r in range(radix):
            if r > 0:
                pick[2 * r, 2 * r - 1] = 1.0
            if r < radix - 1:
                pick[2 * r + 1, 2 * r + 2] = 1.0
        outer = np.zeros((count, 2))
        outer[0, 0] = outer[count - 1, 1] = 1.0
        settle = np.linalg.inv(np.eye(count) - pick @ inside)
        self.ghosts = settle @ pick
        self.passed = settle @ outer
        ends = (np.eye(count) + inside @ self.ghosts)[[0, count - 1]]
        self.ends = ends


def radices_of(groups):
    found = []
    while groups > 1:
        radix = 4 if groups % 4 == 0 else 2
        assert groups % radix == 0
        found.append(radix)
        groups //= radix
    return found


def combine(weights, terms):
    total = None
    for weight, term in zip(weights, terms):
        if weight == 0.0 or term is None:
            continue
        part = term * float(weight)
        total = part if total is None else total + part
    return total


def make_levels(planes, groups):
    found = []
    for radix in radices_of(groups):
        found.append(Level(planes, radix))
        planes *= radix
    return found


def settle(levels, ends):
    level, count = levels[0], 2 * levels[0].radix
    if len(levels) == 1:
        return [combine(weights, ends) for weights in level.ghosts]
    joined = []
    for start in range(0, len(ends), count):
        part = ends[start : start + count]
        joined += [combine(weights, part) for weights in level.ends]
    outer = settle(levels[1:], joined)
    found = []
    for at, start in enumerate(range(0, len(ends), count)):
        part = list(ends[start : start + count]) + [outer[2 * at], outer[2 * at + 1]]
        for inside, passed in zip(level.ghosts, level.passed):
            found.append(combine(list(inside) + list(passed), part))
    return found


def plus(total, weight, term):
    return total if term is None else total + weight * term


def row_window(value, values, units, tile, tiles, rows):
    start = (tile // units) * values * units + value * units + tile % units
    return pl.ds(start, rows, stride=tiles * values)


def pinned(source, pins_ref, component, lanes):
    position = lax.axis_index("gx")
    first = jnp.where(position == 0, diffusion, 0.0).astype(jnp.float32)
    last = jnp.where(position == lax.axis_size("gx") - 1, diffusion, 0.0).astype(jnp.float32)
    source[0] = source[0] + first * pins_ref[0, component, :, lanes]
    source[-1] = source[-1] + last * pins_ref[1, component, :, lanes]
    return source


def solve_components(line, field_ref, axes_ref, pins_ref, lanes, ghosts):
    planes = line.planes
    field = [[field_ref[c, i, :, lanes] for i in range(planes)] for c in range(3)]
    axes = [[axes_ref[c, i, :, lanes] for i in range(planes)] for c in range(3)]
    for component in range(3):
        source = []
        for i in range(planes):
            projection = (
                field[0][i] * axes[0][i] + field[1][i] * axes[1][i] + field[2][i] * axes[2][i]
            )
            source.append(
                field[component][i] + (anisotropy_rate * projection) * axes[component][i]
            )
        source = pinned(source, pins_ref, component, lanes)
        if ghosts is not None:
            source[0] = source[0] + diffusion * ghosts[component][0]
            source[-1] = source[-1] + diffusion * ghosts[component][1]
        field[component] = line.solve(source)
    return field


def couplings(line, axes_ref, lanes):
    planes = line.planes
    low, high = line.from_low, line.from_high
    axes = [[axes_ref[c, i, :, lanes] for i in range(planes)] for c in range(3)]
    scaled = [anisotropy_rate * a for a in axes[1]]
    first_second = [axes[0][i] * scaled[i] for i in range(planes)]
    second_third = [axes[2][i] * scaled[i] for i in range(planes)]
    first_third = [(anisotropy_rate * axes[0][i]) * axes[2][i] for i in range(planes)]

    def weighted(terms, weights):
        total = terms[0] * float(weights[0] / diffusion)
        for i in range(1, planes):
            total = total + terms[i] * float(weights[i] / diffusion)
        return total

    found = []
    for product in (first_second, second_third):
        for weights in (low * low, low * high, high * high):
            found.append(weighted(product, weights))
    for ghost in (low, high):
        moved = line.solve([first_second[i] * float(ghost[i]) for i in range(planes)])
        pushed = [
            second_third[i] * moved[i] + first_third[i] * float(ghost[i]) for i in range(planes)
        ]
        found.append(weighted(pushed, low))
        found.append(weighted(pushed, high))
    return found


def send_tile(line, units, values, field_ref, axes_ref, pins_ref, out_ref, tile):
    rows, width = field_ref.shape[2], field_ref.shape[3]
    tiles = width // LANES
    lanes = slice(tile * LANES, (tile + 1) * LANES)
    solved = solve_components(line, field_ref, axes_ref, pins_ref, lanes, None)
    for component in range(3):
        for side, end in enumerate((0, -1)):
            at = row_window(2 * component + side, values, units, tile, tiles, rows)
            out_ref[at, :] = solved[component][end]


def coupling_kernel(line, units, axes_ref, out_ref):
    rows, width = axes_ref.shape[2:]
    tiles = width // LANES
    for tile in range(tiles):
        found = couplings(line, axes_ref, slice(tile * LANES, (tile + 1) * LANES))
        for value, one in enumerate(found):
            out_ref[row_window(value, COUPLED - RHS, units, tile, tiles, rows), :] = one


def first_kernel(line, groups, units, coupling_ref, field_ref, axes_ref, pins_ref, out_ref):
    extra = (COUPLED - RHS) * units
    for d in range(groups):
        start = (d * COUPLED + RHS) * units
        out_ref[start : start + extra, :] = coupling_ref[d * extra : (d + 1) * extra, :]
    for tile in range(field_ref.shape[3] // LANES):
        send_tile(line, units, COUPLED, field_ref, axes_ref, pins_ref, out_ref, tile)


def reduced_kernel(levels, groups, units, rhs_values, rhs_ref, coupling_ref, out_ref):
    def read(ref, values, d, value):
        start = (d * values + value) * units
        return ref[start : start + units, :]

    rhs = [
        [read(rhs_ref, rhs_values, k // 2, 2 * c + k % 2) for k in range(2 * groups)]
        for c in range(3)
    ]

    def coupling(d, value):
        return read(coupling_ref, COUPLED, d, RHS + value)

    first = settle(levels, rhs[0])
    for d in range(groups):
        low, high = first[2 * d], first[2 * d + 1]
        mixed = coupling(d, 1)
        rhs[1][2 * d] = plus(plus(rhs[1][2 * d], coupling(d, 0), low), mixed, high)
        rhs[1][2 * d + 1] = plus(plus(rhs[1][2 * d + 1], mixed, low), coupling(d, 2), high)
    second = settle(levels, rhs[1])
    for d in range(groups):
        low1, high1 = first[2 * d], first[2 * d + 1]
        low2, high2 = second[2 * d], second[2 * d + 1]
        mixed = coupling(d, 4)
        total = plus(plus(rhs[2][2 * d], coupling(d, 3), low2), mixed, high2)
        rhs[2][2 * d] = plus(plus(total, coupling(d, 6), low1), coupling(d, 8), high1)
        total = plus(plus(rhs[2][2 * d + 1], mixed, low2), coupling(d, 5), high2)
        rhs[2][2 * d + 1] = plus(plus(total, coupling(d, 7), low1), coupling(d, 9), high1)
    third = settle(levels, rhs[2])
    for c, ghosts in enumerate((first, second, third)):
        for k, ghost in enumerate(ghosts):
            start = (k // 2 * RHS + 2 * c + k % 2) * units
            if ghost is None:
                ghost = jnp.zeros((units, LANES), jnp.float32)
            out_ref[start : start + units, :] = ghost


def finish_kernel(line, units, field_ref, axes_ref, pins_ref, ghost_ref, out_ref, edge_ref):
    planes = line.planes
    rows, width = field_ref.shape[2], field_ref.shape[3]
    tiles = width // LANES
    for tile in range(tiles):
        lanes = slice(tile * LANES, (tile + 1) * LANES)
        ghosts = [
            [
                ghost_ref[row_window(2 * c + side, RHS, units, tile, tiles, rows), :]
                for side in range(2)
            ]
            for c in range(3)
        ]
        solved = solve_components(line, field_ref, axes_ref, pins_ref, lanes, ghosts)
        for c in range(3):
            for i in range(planes):
                out_ref[c, i, :, lanes] = solved[c][i]
                at = c * planes + i
                edge_ref[0, at : at + 1, lanes] = solved[c][i][:1]
                edge_ref[1, at : at + 1, lanes] = solved[c][i][rows - 1 :]


def rotate(field_ref, beyond_ref, axes_ref, out_ref, finished=None):
    planes, rows, width = field_ref.shape[1:]
    row = lax.broadcasted_iota(jnp.int32, (rows, width), 0)
    for i in range(planes):
        field = [field_ref[c, i] for c in range(3)]
        axes = [axes_ref[c, i] for c in range(3)]
        projection = field[0] * axes[0] + field[1] * axes[1] + field[2] * axes[2]
        effective = []
        for c in range(3):
            at = c * planes + i
            below = jnp.where(
                row == 0, beyond_ref[1, at : at + 1, :], pltpu.roll(field[c], 1, 0)
            )
            above = jnp.where(
                row == rows - 1, beyond_ref[0, at : at + 1, :], pltpu.roll(field[c], rows - 1, 0)
            )
            beside = pltpu.roll(field[c], 1, 1) + pltpu.roll(field[c], width - 1, 1)
            effective.append(
                exchange_rate * (((above + below) + beside) - 4.0 * field[c])
                + projection * axes[c]
            )
        rotated = []
        for c in range(3):
            d, e = (c + 1) % 3, (c + 2) % 3
            twisted = field[d] * effective[e] - field[e] * effective[d]
            rotated.append(field[c] - torque_rate * twisted)
        square = rotated[0] * rotated[0] + rotated[1] * rotated[1] + rotated[2] * rotated[2]
        scale = jnp.minimum(lax.rsqrt(square), 1.0 / norm_floor)
        for c in range(3):
            out_ref[c, i] = rotated[c] * scale
        if finished is not None:
            finished(i)


def rotate_and_send_kernel(
    line, units, field_ref, beyond_ref, axes_ref, pins_ref, out_ref, sent_ref
):
    rotate(field_ref, beyond_ref, axes_ref, out_ref)
    for tile in range(field_ref.shape[3] // LANES):
        send_tile(line, units, RHS, out_ref, axes_ref, pins_ref, sent_ref, tile)


def last_kernel(field_ref, beyond_ref, axes_ref, out_hbm, out_ref, sems):
    def copy(i):
        return pltpu.make_async_copy(out_ref.at[:, i], out_hbm.at[:, i], sems.at[i])

    rotate(field_ref, beyond_ref, axes_ref, out_ref, lambda i: copy(i).start())
    for i in range(field_ref.shape[1]):
        copy(i).wait()


VMEM = pl.BlockSpec(memory_space=pltpu.VMEM)
HBM = pl.BlockSpec(memory_space=pltpu.HBM)
LIMIT = 32 * 1024 * 1024


def call(kernel, shapes, *operands, written=VMEM, scratch=()):
    shapes = [jax.ShapeDtypeStruct(shape, jnp.float32) for shape in shapes]
    return pl.pallas_call(
        kernel,
        out_shape=tuple(shapes),
        in_specs=[VMEM] * len(operands),
        out_specs=(written,) * len(shapes),
        scratch_shapes=scratch,
        compiler_params=pltpu.CompilerParams(vmem_limit_bytes=LIMIT),
    )(*operands)


def exchange(block, groups):
    parts = block.reshape(groups, -1, LANES)
    return lax.all_to_all(parts, "gx", split_axis=0, concat_axis=0, tiled=True).reshape(
        block.shape
    )


def from_neighbours(edges):
    count = lax.axis_size("gy")
    forward = [(i, (i + 1) % count) for i in range(count)]
    if count == 2:
        return lax.ppermute(edges, "gy", forward)
    backward = [(target, source) for source, target in forward]
    return jnp.stack(
        [lax.ppermute(edges[0], "gy", backward), lax.ppermute(edges[1], "gy", forward)]
    )


def per_device(magnetization, easy_axes, pins):
    _, planes, rows, width = magnetization.shape
    groups = lax.axis_size("gx")
    tiles = width // LANES
    units = rows * tiles // groups
    line = Line(planes)
    levels = make_levels(planes, groups)
    whole = magnetization.shape
    sent_shape = (groups * RHS * units, LANES)

    field = magnetization
    (coupling,) = call(
        functools.partial(coupling_kernel, line, units),
        [(groups * (COUPLED - RHS) * units, LANES)],
        easy_axes,
    )
    (sent,) = call(
        functools.partial(first_kernel, line, groups, units),
        [(groups * COUPLED * units, LANES)],
        coupling,
        field,
        easy_axes,
        pins,
    )
    coupling = None
    for stepno in range(STEPS):
        gathered = exchange(sent, groups)
        if stepno == 0:
            coupling = gathered
        (ghosts,) = call(
            functools.partial(reduced_kernel, levels, groups, units, RHS if stepno else COUPLED),
            [sent_shape],
            gathered,
            coupling,
        )
        ghosts = exchange(ghosts, groups)
        solved, edges = call(
            functools.partial(finish_kernel, line, units),
            [whole, (2, 3 * planes, width)],
            field,
            easy_axes,
            pins,
            ghosts,
        )
        beyond = from_neighbours(edges)
        if stepno < STEPS - 1:
            field, sent = call(
                functools.partial(rotate_and_send_kernel, line, units),
                [whole, sent_shape],
                solved,
                beyond,
                easy_axes,
                pins,
            )
        else:
            (field,) = call(
                last_kernel,
                [whole],
                solved,
                beyond,
                easy_axes,
                written=HBM,
                scratch=[pltpu.VMEM(whole, jnp.float32), pltpu.SemaphoreType.DMA((planes,))],
            )
    return field


def solution(mesh):
    in_specs = (P(None, "gx", "gy", None), P(None, "gx", "gy", None), P(None, None, "gy", None))
    out_specs = P(None, "gx", "gy", None)
    return jax.shard_map(
        per_device, mesh=mesh, in_specs=in_specs, out_specs=out_specs, check_vma=False
    )
```

```python
import functools

import jax
import jax.numpy as jnp
import numpy as np
from jax import lax
from jax.experimental import pallas as pl
from jax.experimental.pallas import tpu as pltpu
from jax.sharding import PartitionSpec as P

STEPS = 2
LANES = 128
RHS = 6
COUPLED = 16

diffusion = 4000.0
anisotropy_rate = 0.3
torque_rate = 0.2
exchange_rate = 0.1
norm_floor = 0.5


class Line:
    def __init__(self, planes):
        leading = 1.0 + 2.0 * diffusion
        pivots = [leading]
        for _ in range(1, planes):
            pivots.append(leading - diffusion * diffusion / pivots[-1])
        self.planes = planes
        self.inverse_pivot = [1.0 / p for p in pivots]
        self.factor = [0.0] + [diffusion / p for p in pivots[:-1]]
        block = (
            leading * np.eye(planes)
            - diffusion * np.eye(planes, k=1)
            - diffusion * np.eye(planes, k=-1)
        )
        self.from_low = diffusion * np.linalg.inv(block)[:, 0]
        self.from_high = self.from_low[::-1]

    def solve(self, source):
        planes = self.planes
        carried = [source[0]]
        for i in range(1, planes):
            carried.append(source[i] + self.factor[i] * carried[-1])
        solved = [None] * planes
        solved[-1] = carried[-1] * self.inverse_pivot[-1]
        for i in range(planes - 2, -1, -1):
            solved[i] = carried[i] * self.inverse_pivot[i] + self.factor[i + 1] * solved[i + 1]
        return solved


class Level:
    def __init__(self, length, radix):
        self.radix = radix
        line = Line(length)
        near, far = line.from_low[0], line.from_low[-1]
        count = 2 * radix
        inside = np.kron(np.eye(radix), np.array([[near, far], [far, near]]))
        pick = np.zeros((count, count))
        for r in range(radix):
            if r > 0:
                pick[2 * r, 2 * r - 1] = 1.0
            if r < radix - 1:
                pick[2 * r + 1, 2 * r + 2] = 1.0
        outer = np.zeros((count, 2))
        outer[0, 0] = outer[count - 1, 1] = 1.0
        settle = np.linalg.inv(np.eye(count) - pick @ inside)
        self.ghosts = settle @ pick
        self.passed = settle @ outer
        ends = (np.eye(count) + inside @ self.ghosts)[[0, count - 1]]
        self.ends = ends


def radices_of(groups):
    found = []
    while groups > 1:
        radix = 4 if groups % 4 == 0 else 2
        assert groups % radix == 0
        found.append(radix)
        groups //= radix
    return found


def combine(weights, terms):
    total = None
    for weight, term in zip(weights, terms):
        if weight == 0.0 or term is None:
            continue
        part = term * float(weight)
        total = part if total is None else total + part
    return total


def make_levels(planes, groups):
    found = []
    for radix in radices_of(groups):
        found.append(Level(planes, radix))
        planes *= radix
    return found


def settle(levels, ends):
    level, count = levels[0], 2 * levels[0].radix
    if len(levels) == 1:
        return [combine(weights, ends) for weights in level.ghosts]
    joined = []
    for start in range(0, len(ends), count):
        part = ends[start : start + count]
        joined += [combine(weights, part) for weights in level.ends]
    outer = settle(levels[1:], joined)
    found = []
    for at, start in enumerate(range(0, len(ends), count)):
        part = list(ends[start : start + count]) + [outer[2 * at], outer[2 * at + 1]]
        for inside, passed in zip(level.ghosts, level.passed):
            found.append(combine(list(inside) + list(passed), part))
    return found


def plus(total, weight, term):
    return total if term is None else total + weight * term


def row_window(value, values, units, tile, tiles, rows):
    start = (tile // units) * values * units + value * units + tile % units
    return pl.ds(start, rows, stride=tiles * values)


def pinned(source, pins_ref, component, lanes):
    position = lax.axis_index("gx")
    first = jnp.where(position == 0, diffusion, 0.0).astype(jnp.float32)
    last = jnp.where(position == lax.axis_size("gx") - 1, diffusion, 0.0).astype(jnp.float32)
    source[0] = source[0] + first * pins_ref[0, component, :, lanes]
    source[-1] = source[-1] + last * pins_ref[1, component, :, lanes]
    return source


def read_field(field_ref, lanes):
    planes = field_ref.shape[1]
    return [[field_ref[c, i, :, lanes] for i in range(planes)] for c in range(3)]


def solve_components(line, field, axes_ref, pins_ref, lanes, ghosts):
    planes = line.planes
    axes = [[axes_ref[c, i, :, lanes] for i in range(planes)] for c in range(3)]
    for component in range(3):
        source = []
        for i in range(planes):
            projection = (
                field[0][i] * axes[0][i] + field[1][i] * axes[1][i] + field[2][i] * axes[2][i]
            )
            source.append(
                field[component][i] + (anisotropy_rate * projection) * axes[component][i]
            )
        source = pinned(source, pins_ref, component, lanes)
        if ghosts is not None:
            source[0] = source[0] + diffusion * ghosts[component][0]
            source[-1] = source[-1] + diffusion * ghosts[component][1]
        field[component] = line.solve(source)
    return field


def couplings(line, axes_ref, lanes):
    planes = line.planes
    low, high = line.from_low, line.from_high
    axes = [[axes_ref[c, i, :, lanes] for i in range(planes)] for c in range(3)]
    scaled = [anisotropy_rate * a for a in axes[1]]
    first_second = [axes[0][i] * scaled[i] for i in range(planes)]
    second_third = [axes[2][i] * scaled[i] for i in range(planes)]
    first_third = [(anisotropy_rate * axes[0][i]) * axes[2][i] for i in range(planes)]

    def weighted(terms, weights):
        total = terms[0] * float(weights[0] / diffusion)
        for i in range(1, planes):
            total = total + terms[i] * float(weights[i] / diffusion)
        return total

    found = []
    for product in (first_second, second_third):
        for weights in (low * low, low * high, high * high):
            found.append(weighted(product, weights))
    for ghost in (low, high):
        moved = line.solve([first_second[i] * float(ghost[i]) for i in range(planes)])
        pushed = [
            second_third[i] * moved[i] + first_third[i] * float(ghost[i]) for i in range(planes)
        ]
        found.append(weighted(pushed, low))
        found.append(weighted(pushed, high))
    return found


def send_tile(line, units, values, field, axes_ref, pins_ref, out_ref, tile):
    rows, width = axes_ref.shape[2:]
    tiles = width // LANES
    lanes = slice(tile * LANES, (tile + 1) * LANES)
    solved = solve_components(line, field, axes_ref, pins_ref, lanes, None)
    for component in range(3):
        for side, end in enumerate((0, -1)):
            at = row_window(2 * component + side, values, units, tile, tiles, rows)
            out_ref[at, :] = solved[component][end]


def coupling_kernel(line, units, axes_ref, out_ref):
    rows, width = axes_ref.shape[2:]
    tiles = width // LANES
    for tile in range(tiles):
        found = couplings(line, axes_ref, slice(tile * LANES, (tile + 1) * LANES))
        for value, one in enumerate(found):
            out_ref[row_window(value, COUPLED - RHS, units, tile, tiles, rows), :] = one


def first_kernel(line, groups, units, coupling_ref, field_ref, axes_ref, pins_ref, out_ref):
    extra = (COUPLED - RHS) * units
    for d in range(groups):
        start = (d * COUPLED + RHS) * units
        out_ref[start : start + extra, :] = coupling_ref[d * extra : (d + 1) * extra, :]
    for tile in range(field_ref.shape[3] // LANES):
        field = read_field(field_ref, slice(tile * LANES, (tile + 1) * LANES))
        send_tile(line, units, COUPLED, field, axes_ref, pins_ref, out_ref, tile)


def reduced_kernel(levels, groups, units, rhs_values, rhs_ref, coupling_ref, out_ref):
    def read(ref, values, d, value):
        start = (d * values + value) * units
        return ref[start : start + units, :]

    rhs = [
        [read(rhs_ref, rhs_values, k // 2, 2 * c + k % 2) for k in range(2 * groups)]
        for c in range(3)
    ]

    def coupling(d, value):
        return read(coupling_ref, COUPLED, d, RHS + value)

    first = settle(levels, rhs[0])
    for d in range(groups):
        low, high = first[2 * d], first[2 * d + 1]
        mixed = coupling(d, 1)
        rhs[1][2 * d] = plus(plus(rhs[1][2 * d], coupling(d, 0), low), mixed, high)
        rhs[1][2 * d + 1] = plus(plus(rhs[1][2 * d + 1], mixed, low), coupling(d, 2), high)
    second = settle(levels, rhs[1])
    for d in range(groups):
        low1, high1 = first[2 * d], first[2 * d + 1]
        low2, high2 = second[2 * d], second[2 * d + 1]
        mixed = coupling(d, 4)
        total = plus(plus(rhs[2][2 * d], coupling(d, 3), low2), mixed, high2)
        rhs[2][2 * d] = plus(plus(total, coupling(d, 6), low1), coupling(d, 8), high1)
        total = plus(plus(rhs[2][2 * d + 1], mixed, low2), coupling(d, 5), high2)
        rhs[2][2 * d + 1] = plus(plus(total, coupling(d, 7), low1), coupling(d, 9), high1)
    third = settle(levels, rhs[2])
    for c, ghosts in enumerate((first, second, third)):
        for k, ghost in enumerate(ghosts):
            start = (k // 2 * RHS + 2 * c + k % 2) * units
            if ghost is None:
                ghost = jnp.zeros((units, LANES), jnp.float32)
            out_ref[start : start + units, :] = ghost


def finish_kernel(line, units, field_ref, axes_ref, pins_ref, ghost_ref, out_ref, edge_ref):
    planes = line.planes
    rows, width = field_ref.shape[2], field_ref.shape[3]
    tiles = width // LANES
    for tile in range(tiles):
        lanes = slice(tile * LANES, (tile + 1) * LANES)
        ghosts = [
            [
                ghost_ref[row_window(2 * c + side, RHS, units, tile, tiles, rows), :]
                for side in range(2)
            ]
            for c in range(3)
        ]
        field = read_field(field_ref, lanes)
        solved = solve_components(line, field, axes_ref, pins_ref, lanes, ghosts)
        for c in range(3):
            for i in range(planes):
                out_ref[c, i, :, lanes] = solved[c][i]
                at = c * planes + i
                edge_ref[0, at : at + 1, lanes] = solved[c][i][:1]
                edge_ref[1, at : at + 1, lanes] = solved[c][i][rows - 1 :]


def unit_scale(parts):
    square = parts[0] * parts[0] + parts[1] * parts[1] + parts[2] * parts[2]
    return jnp.minimum(lax.rsqrt(square), 1.0 / norm_floor)


def turn_kernel(field_ref, axes_ref, out_ref, raw_ref):
    planes, rows, width = field_ref.shape[1:]
    row = lax.broadcasted_iota(jnp.int32, (rows, width), 0)
    for i in range(planes):
        field = [field_ref[c, i] for c in range(3)]
        axes = [axes_ref[c, i] for c in range(3)]
        projection = field[0] * axes[0] + field[1] * axes[1] + field[2] * axes[2]
        effective = []
        for c in range(3):
            below = jnp.where(row == 0, 0.0, pltpu.roll(field[c], 1, 0))
            above = jnp.where(row == rows - 1, 0.0, pltpu.roll(field[c], rows - 1, 0))
            beside = pltpu.roll(field[c], 1, 1) + pltpu.roll(field[c], width - 1, 1)
            effective.append(
                exchange_rate * (((above + below) + beside) - 4.0 * field[c])
                + projection * axes[c]
            )
        rotated = []
        for c in range(3):
            d, e = (c + 1) % 3, (c + 2) % 3
            twisted = field[d] * effective[e] - field[e] * effective[d]
            rotated.append(field[c] - torque_rate * twisted)
        scale = unit_scale(rotated)
        for c in range(3):
            at = c * planes + i
            out_ref[c, i] = rotated[c] * scale
            raw_ref[0, at : at + 1, :] = rotated[c][:1]
            raw_ref[1, at : at + 1, :] = rotated[c][rows - 1 :]


def mend_edges(edge_ref, raw_ref, beyond_ref, mended_ref):
    planes = edge_ref.shape[1] // 3
    for side in range(2):
        parts = [slice(c * planes, (c + 1) * planes) for c in range(3)]
        field = [edge_ref[side, part, :] for part in parts]
        beyond = [beyond_ref[1 - side, part, :] for part in parts]
        rotated = []
        for c in range(3):
            d, e = (c + 1) % 3, (c + 2) % 3
            twisted = field[d] * beyond[e] - field[e] * beyond[d]
            rotated.append(raw_ref[side, parts[c], :] - (torque_rate * exchange_rate) * twisted)
        scale = unit_scale(rotated)
        for c in range(3):
            mended_ref[side, parts[c], :] = rotated[c] * scale


def mended(turned, mended_ref, at, lanes):
    rows = turned.shape[0]
    row = lax.broadcasted_iota(jnp.int32, turned.shape, 0)
    turned = jnp.where(row == 0, mended_ref[0, at : at + 1, lanes], turned)
    return jnp.where(row == rows - 1, mended_ref[1, at : at + 1, lanes], turned)


def mend_and_send_kernel(
    line,
    units,
    turned_ref,
    edge_ref,
    raw_ref,
    beyond_ref,
    axes_ref,
    pins_ref,
    out_ref,
    sent_ref,
    mended_ref,
):
    planes = line.planes
    mend_edges(edge_ref, raw_ref, beyond_ref, mended_ref)
    for tile in range(turned_ref.shape[3] // LANES):
        lanes = slice(tile * LANES, (tile + 1) * LANES)
        field = read_field(turned_ref, lanes)
        for c in range(3):
            for i in range(planes):
                field[c][i] = mended(field[c][i], mended_ref, c * planes + i, lanes)
                out_ref[c, i, :, lanes] = field[c][i]
        send_tile(line, units, RHS, field, axes_ref, pins_ref, sent_ref, tile)


def last_kernel(turned_ref, edge_ref, raw_ref, beyond_ref, out_hbm, out_ref, mended_ref, sems):
    planes = turned_ref.shape[1]

    def copy(i):
        return pltpu.make_async_copy(out_ref.at[:, i], out_hbm.at[:, i], sems.at[i])

    mend_edges(edge_ref, raw_ref, beyond_ref, mended_ref)
    for i in range(planes):
        for c in range(3):
            out_ref[c, i] = mended(turned_ref[c, i], mended_ref, c * planes + i, slice(None))
        copy(i).start()
    for i in range(planes):
        copy(i).wait()


VMEM = pl.BlockSpec(memory_space=pltpu.VMEM)
HBM = pl.BlockSpec(memory_space=pltpu.HBM)
LIMIT = 32 * 1024 * 1024


def call(kernel, shapes, *operands, written=VMEM, scratch=()):
    shapes = [jax.ShapeDtypeStruct(shape, jnp.float32) for shape in shapes]
    return pl.pallas_call(
        kernel,
        out_shape=tuple(shapes),
        in_specs=[VMEM] * len(operands),
        out_specs=(written,) * len(shapes),
        scratch_shapes=scratch,
        compiler_params=pltpu.CompilerParams(vmem_limit_bytes=LIMIT),
    )(*operands)


def exchange(block, groups):
    parts = block.reshape(groups, -1, LANES)
    return lax.all_to_all(parts, "gx", split_axis=0, concat_axis=0, tiled=True).reshape(
        block.shape
    )


def from_neighbours(edges):
    count = lax.axis_size("gy")
    forward = [(i, (i + 1) % count) for i in range(count)]
    if count == 2:
        return lax.ppermute(edges, "gy", forward)
    backward = [(target, source) for source, target in forward]
    return jnp.stack(
        [lax.ppermute(edges[0], "gy", backward), lax.ppermute(edges[1], "gy", forward)]
    )


def per_device(magnetization, easy_axes, pins):
    _, planes, rows, width = magnetization.shape
    groups = lax.axis_size("gx")
    tiles = width // LANES
    units = rows * tiles // groups
    line = Line(planes)
    levels = make_levels(planes, groups)
    whole = magnetization.shape
    sent_shape = (groups * RHS * units, LANES)
    edge_shape = (2, 3 * planes, width)

    field = magnetization
    (coupling,) = call(
        functools.partial(coupling_kernel, line, units),
        [(groups * (COUPLED - RHS) * units, LANES)],
        easy_axes,
    )
    (sent,) = call(
        functools.partial(first_kernel, line, groups, units),
        [(groups * COUPLED * units, LANES)],
        coupling,
        field,
        easy_axes,
        pins,
    )
    coupling = None
    for stepno in range(STEPS):
        gathered = exchange(sent, groups)
        if stepno == 0:
            coupling = gathered
        (ghosts,) = call(
            functools.partial(reduced_kernel, levels, groups, units, RHS if stepno else COUPLED),
            [sent_shape],
            gathered,
            coupling,
        )
        ghosts = exchange(ghosts, groups)
        solved, edges = call(
            functools.partial(finish_kernel, line, units),
            [whole, edge_shape],
            field,
            easy_axes,
            pins,
            ghosts,
        )
        beyond = from_neighbours(edges)
        turned, raw = call(turn_kernel, [whole, edge_shape], solved, easy_axes)
        if stepno < STEPS - 1:
            field, sent = call(
                functools.partial(mend_and_send_kernel, line, units),
                [whole, sent_shape],
                turned,
                edges,
                raw,
                beyond,
                easy_axes,
                pins,
                scratch=[pltpu.VMEM(edge_shape, jnp.float32)],
            )
        else:
            (field,) = call(
                last_kernel,
                [whole],
                turned,
                edges,
                raw,
                beyond,
                written=HBM,
                scratch=[
                    pltpu.VMEM(whole, jnp.float32),
                    pltpu.VMEM(edge_shape, jnp.float32),
                    pltpu.SemaphoreType.DMA((planes,)),
                ],
            )
    return field


def solution(mesh):
    in_specs = (P(None, "gx", "gy", None), P(None, "gx", "gy", None), P(None, None, "gy", None))
    out_specs = P(None, "gx", "gy", None)
    return jax.shard_map(
        per_device, mesh=mesh, in_specs=in_specs, out_specs=out_specs, check_vma=False
    )
```

```python
import functools

import jax
import jax.numpy as jnp
import numpy as np
from jax import lax
from jax.experimental import pallas as pl
from jax.experimental.pallas import tpu as pltpu
from jax.sharding import PartitionSpec as P

STEPS = 2
LANES = 128
RHS = 6
COUPLED = 16

diffusion = 4000.0
anisotropy_rate = 0.3
torque_rate = 0.2
exchange_rate = 0.1
norm_floor = 0.5


class Line:
    def __init__(self, planes):
        leading = 1.0 + 2.0 * diffusion
        pivots = [leading]
        for _ in range(1, planes):
            pivots.append(leading - diffusion * diffusion / pivots[-1])
        self.planes = planes
        self.inverse_pivot = [1.0 / p for p in pivots]
        self.factor = [0.0] + [diffusion / p for p in pivots[:-1]]
        block = (
            leading * np.eye(planes)
            - diffusion * np.eye(planes, k=1)
            - diffusion * np.eye(planes, k=-1)
        )
        self.from_low = diffusion * np.linalg.inv(block)[:, 0]
        self.from_high = self.from_low[::-1]

    def solve(self, source):
        planes = self.planes
        carried = [source[0]]
        for i in range(1, planes):
            carried.append(source[i] + self.factor[i] * carried[-1])
        solved = [None] * planes
        solved[-1] = carried[-1] * self.inverse_pivot[-1]
        for i in range(planes - 2, -1, -1):
            solved[i] = carried[i] * self.inverse_pivot[i] + self.factor[i + 1] * solved[i + 1]
        return solved


class Level:
    def __init__(self, length, radix):
        self.radix = radix
        line = Line(length)
        near, far = line.from_low[0], line.from_low[-1]
        count = 2 * radix
        inside = np.kron(np.eye(radix), np.array([[near, far], [far, near]]))
        pick = np.zeros((count, count))
        for r in range(radix):
            if r > 0:
                pick[2 * r, 2 * r - 1] = 1.0
            if r < radix - 1:
                pick[2 * r + 1, 2 * r + 2] = 1.0
        outer = np.zeros((count, 2))
        outer[0, 0] = outer[count - 1, 1] = 1.0
        settle = np.linalg.inv(np.eye(count) - pick @ inside)
        self.ghosts = settle @ pick
        self.passed = settle @ outer
        ends = (np.eye(count) + inside @ self.ghosts)[[0, count - 1]]
        self.ends = ends


def radices_of(groups):
    found = []
    while groups > 1:
        radix = 4 if groups % 4 == 0 else 2
        assert groups % radix == 0
        found.append(radix)
        groups //= radix
    return found


def combine(weights, terms):
    total = None
    for weight, term in zip(weights, terms):
        if weight == 0.0 or term is None:
            continue
        part = term * float(weight)
        total = part if total is None else total + part
    return total


def make_levels(planes, groups):
    found = []
    for radix in radices_of(groups):
        found.append(Level(planes, radix))
        planes *= radix
    return found


def settle(levels, ends):
    level, count = levels[0], 2 * levels[0].radix
    if len(levels) == 1:
        return [combine(weights, ends) for weights in level.ghosts]
    joined = []
    for start in range(0, len(ends), count):
        part = ends[start : start + count]
        joined += [combine(weights, part) for weights in level.ends]
    outer = settle(levels[1:], joined)
    found = []
    for at, start in enumerate(range(0, len(ends), count)):
        part = list(ends[start : start + count]) + [outer[2 * at], outer[2 * at + 1]]
        for inside, passed in zip(level.ghosts, level.passed):
            found.append(combine(list(inside) + list(passed), part))
    return found


def plus(total, weight, term):
    return total if term is None else total + weight * term


def pieces(value, values, units, tile, rows):
    step = min(units, rows)
    for start in range(0, rows, step):
        at = tile * rows + start
        to = (at // units * values + value) * units + at % units
        yield slice(start, start + step), slice(to, to + step)


def pinned(source, pins_ref, component, lanes):
    position = lax.axis_index("gx")
    first = jnp.where(position == 0, diffusion, 0.0).astype(jnp.float32)
    last = jnp.where(position == lax.axis_size("gx") - 1, diffusion, 0.0).astype(jnp.float32)
    source[0] = source[0] + first * pins_ref[0, component, :, lanes]
    source[-1] = source[-1] + last * pins_ref[1, component, :, lanes]
    return source


def read_field(field_ref, lanes):
    planes = field_ref.shape[1]
    return [[field_ref[c, i, :, lanes] for i in range(planes)] for c in range(3)]


def solve_components(line, field, axes_ref, pins_ref, lanes, ghosts):
    planes = line.planes
    axes = [[axes_ref[c, i, :, lanes] for i in range(planes)] for c in range(3)]
    for component in range(3):
        source = []
        for i in range(planes):
            projection = (
                field[0][i] * axes[0][i] + field[1][i] * axes[1][i] + field[2][i] * axes[2][i]
            )
            source.append(
                field[component][i] + (anisotropy_rate * projection) * axes[component][i]
            )
        source = pinned(source, pins_ref, component, lanes)
        if ghosts is not None:
            source[0] = source[0] + diffusion * ghosts[component][0]
            source[-1] = source[-1] + diffusion * ghosts[component][1]
        field[component] = line.solve(source)
    return field


def couplings(line, axes_ref, lanes):
    planes = line.planes
    low, high = line.from_low, line.from_high
    axes = [[axes_ref[c, i, :, lanes] for i in range(planes)] for c in range(3)]
    scaled = [anisotropy_rate * a for a in axes[1]]
    first_second = [axes[0][i] * scaled[i] for i in range(planes)]
    second_third = [axes[2][i] * scaled[i] for i in range(planes)]
    first_third = [(anisotropy_rate * axes[0][i]) * axes[2][i] for i in range(planes)]

    def weighted(terms, weights):
        total = terms[0] * float(weights[0] / diffusion)
        for i in range(1, planes):
            total = total + terms[i] * float(weights[i] / diffusion)
        return total

    found = []
    for product in (first_second, second_third):
        for weights in (low * low, low * high, high * high):
            found.append(weighted(product, weights))
    for ghost in (low, high):
        moved = line.solve([first_second[i] * float(ghost[i]) for i in range(planes)])
        pushed = [
            second_third[i] * moved[i] + first_third[i] * float(ghost[i]) for i in range(planes)
        ]
        found.append(weighted(pushed, low))
        found.append(weighted(pushed, high))
    return found


def send_tile(line, units, values, field, axes_ref, pins_ref, out_ref, tile):
    rows = axes_ref.shape[2]
    lanes = slice(tile * LANES, (tile + 1) * LANES)
    solved = solve_components(line, field, axes_ref, pins_ref, lanes, None)
    for component in range(3):
        for side, end in enumerate((0, -1)):
            value = 2 * component + side
            for source, target in pieces(value, values, units, tile, rows):
                out_ref[target, :] = solved[component][end][source]


def coupling_kernel(line, units, axes_ref, out_ref):
    rows, width = axes_ref.shape[2:]
    tiles = width // LANES
    for tile in range(tiles):
        found = couplings(line, axes_ref, slice(tile * LANES, (tile + 1) * LANES))
        for value, one in enumerate(found):
            for source, target in pieces(value, COUPLED - RHS, units, tile, rows):
                out_ref[target, :] = one[source]


def first_kernel(line, groups, units, coupling_ref, field_ref, axes_ref, pins_ref, out_ref):
    extra = (COUPLED - RHS) * units
    for d in range(groups):
        start = (d * COUPLED + RHS) * units
        out_ref[start : start + extra, :] = coupling_ref[d * extra : (d + 1) * extra, :]
    for tile in range(field_ref.shape[3] // LANES):
        field = read_field(field_ref, slice(tile * LANES, (tile + 1) * LANES))
        send_tile(line, units, COUPLED, field, axes_ref, pins_ref, out_ref, tile)


def solve_children(level, levels, rhs, coupling, outer):
    def ghosts(ends, component):
        found = settle(levels, ends)
        if outer is None:
            return found
        low, high = outer[component]
        moved = []
        for ghost, passed in zip(found, level.passed):
            terms = combine(passed, [low, high])
            moved.append(terms if ghost is None else ghost if terms is None else ghost + terms)
        return moved

    first = ghosts(rhs[0], 0)
    middle = []
    for d in range(level.radix):
        c, low, high = coupling[d], first[2 * d], first[2 * d + 1]
        middle.append(plus(plus(rhs[1][2 * d], c[0], low), c[1], high))
        middle.append(plus(plus(rhs[1][2 * d + 1], c[1], low), c[2], high))
    second = ghosts(middle, 1)
    last = []
    for d in range(level.radix):
        c, low1, high1 = coupling[d], first[2 * d], first[2 * d + 1]
        low2, high2 = second[2 * d], second[2 * d + 1]
        total = plus(plus(rhs[2][2 * d], c[3], low2), c[4], high2)
        last.append(plus(plus(total, c[6], low1), c[8], high1))
        total = plus(plus(rhs[2][2 * d + 1], c[4], low2), c[5], high2)
        last.append(plus(plus(total, c[7], low1), c[9], high1))
    return (first, second, ghosts(last, 2)), (rhs[0], middle, last)


def merged_coupling(level, levels, coupling):
    radix = level.radix
    from_first, from_second, across = [], [], []
    for side in range(2):
        passed = level.passed[:, side]
        moved2, moved3 = [], []
        for r in range(radix):
            c, low, high = coupling[r], float(passed[2 * r]), float(passed[2 * r + 1])
            moved2 += [c[0] * low + c[1] * high, c[1] * low + c[2] * high]
            moved3 += [c[3] * low + c[4] * high, c[4] * low + c[5] * high]
        inner = settle(levels, moved2)
        through = []
        for r in range(radix):
            c, low, high = coupling[r], float(passed[2 * r]), float(passed[2 * r + 1])
            k_low, k_high = inner[2 * r], inner[2 * r + 1]
            total = plus(c[6] * low + c[8] * high, c[3], k_low)
            through.append(plus(total, c[4], k_high))
            total = plus(c[7] * low + c[9] * high, c[4], k_low)
            through.append(plus(total, c[5], k_high))
        for end in range(2):
            if side <= end:
                from_first.append(combine(level.ends[end], moved2))
                from_second.append(combine(level.ends[end], moved3))
            across.append(combine(level.ends[end], through))
    return from_first + from_second + across


def read_children(level, units, rhs_values, rhs_ref, coupling_ref):
    def read(ref, values, d, value):
        start = (d * values + value) * units
        return ref[start : start + units, :]

    rhs = [
        [read(rhs_ref, rhs_values, k // 2, 2 * c + k % 2) for k in range(2 * level.radix)]
        for c in range(3)
    ]
    coupling = [
        [read(coupling_ref, COUPLED, d, v) for v in range(RHS, COUPLED)]
        for d in range(level.radix)
    ]
    return rhs, coupling


def join_kernel(level, levels, units, coupled, rhs_ref, coupling_ref, out_ref):
    values = COUPLED if coupled else RHS
    rhs, coupling = read_children(level, units, values, rhs_ref, coupling_ref)
    _, seen = solve_children(level, levels, rhs, coupling, None)
    joined = [combine(weights, seen[c]) for c in range(3) for weights in level.ends]
    if coupled:
        joined += merged_coupling(level, levels, coupling)
    for value, one in enumerate(joined):
        out_ref[value * units : (value + 1) * units, :] = one


def part_kernel(
    level,
    levels,
    pair,
    units,
    coupled,
    own_ref,
    other_ref,
    own_coupling_ref,
    other_coupling_ref,
    rhs_ref,
    coupling_ref,
    out_ref,
):
    upper = lax.axis_index("gx") >= level.radix

    def halves(own, other, value):
        at = slice(value * units, (value + 1) * units)
        mine, theirs = own[at, :], other[at, :]
        return jnp.where(upper, theirs, mine), jnp.where(upper, mine, theirs)

    both = [halves(own_ref, other_ref, v) for v in range(RHS)]
    ends = [
        [both[2 * c + side][half] for half in range(2) for side in range(2)] for c in range(3)
    ]
    across = [halves(own_coupling_ref, other_coupling_ref, v) for v in range(RHS, COUPLED)]
    found, _ = solve_children(
        pair, [pair], ends, [[one[half] for one in across] for half in range(2)], None
    )
    outer = []
    zero = jnp.zeros((units, LANES), jnp.float32)
    for ghosts in found:
        ghosts = [zero if ghost is None else ghost for ghost in ghosts]
        outer.append([jnp.where(upper, ghosts[2 + side], ghosts[side]) for side in range(2)])
    values = COUPLED if coupled else RHS
    rhs, coupling = read_children(level, units, values, rhs_ref, coupling_ref)
    found, _ = solve_children(level, levels, rhs, coupling, outer)
    for c, ghosts in enumerate(found):
        for k, ghost in enumerate(ghosts):
            start = (k // 2 * RHS + 2 * c + k % 2) * units
            out_ref[start : start + units, :] = ghost


def finish_kernel(line, units, field_ref, axes_ref, pins_ref, ghost_ref, out_ref, edge_ref):
    planes = line.planes
    rows, width = field_ref.shape[2], field_ref.shape[3]
    tiles = width // LANES
    for tile in range(tiles):
        lanes = slice(tile * LANES, (tile + 1) * LANES)
        ghosts = [
            [
                jnp.concatenate(
                    [
                        ghost_ref[target, :]
                        for _, target in pieces(2 * c + side, RHS, units, tile, rows)
                    ],
                    axis=0,
                )
                for side in range(2)
            ]
            for c in range(3)
        ]
        field = read_field(field_ref, lanes)
        solved = solve_components(line, field, axes_ref, pins_ref, lanes, ghosts)
        for c in range(3):
            for i in range(planes):
                out_ref[c, i, :, lanes] = solved[c][i]
                at = c * planes + i
                edge_ref[0, at : at + 1, lanes] = solved[c][i][:1]
                edge_ref[1, at : at + 1, lanes] = solved[c][i][rows - 1 :]


def unit_scale(parts):
    square = parts[0] * parts[0] + parts[1] * parts[1] + parts[2] * parts[2]
    return jnp.minimum(lax.rsqrt(square), 1.0 / norm_floor)


def turn_kernel(field_ref, axes_ref, out_ref, raw_ref):
    planes, rows, width = field_ref.shape[1:]
    row = lax.broadcasted_iota(jnp.int32, (rows, width), 0)
    for i in range(planes):
        field = [field_ref[c, i] for c in range(3)]
        axes = [axes_ref[c, i] for c in range(3)]
        projection = field[0] * axes[0] + field[1] * axes[1] + field[2] * axes[2]
        effective = []
        for c in range(3):
            below = jnp.where(row == 0, 0.0, pltpu.roll(field[c], 1, 0))
            above = jnp.where(row == rows - 1, 0.0, pltpu.roll(field[c], rows - 1, 0))
            beside = pltpu.roll(field[c], 1, 1) + pltpu.roll(field[c], width - 1, 1)
            effective.append(
                exchange_rate * (((above + below) + beside) - 4.0 * field[c])
                + projection * axes[c]
            )
        rotated = []
        for c in range(3):
            d, e = (c + 1) % 3, (c + 2) % 3
            twisted = field[d] * effective[e] - field[e] * effective[d]
            rotated.append(field[c] - torque_rate * twisted)
        scale = unit_scale(rotated)
        for c in range(3):
            at = c * planes + i
            out_ref[c, i] = rotated[c] * scale
            raw_ref[0, at : at + 1, :] = rotated[c][:1]
            raw_ref[1, at : at + 1, :] = rotated[c][rows - 1 :]


def mend_edges(edge_ref, raw_ref, beyond_ref, mended_ref):
    planes = edge_ref.shape[1] // 3
    for side in range(2):
        parts = [slice(c * planes, (c + 1) * planes) for c in range(3)]
        field = [edge_ref[side, part, :] for part in parts]
        beyond = [beyond_ref[1 - side, part, :] for part in parts]
        rotated = []
        for c in range(3):
            d, e = (c + 1) % 3, (c + 2) % 3
            twisted = field[d] * beyond[e] - field[e] * beyond[d]
            rotated.append(raw_ref[side, parts[c], :] - (torque_rate * exchange_rate) * twisted)
        scale = unit_scale(rotated)
        for c in range(3):
            mended_ref[side, parts[c], :] = rotated[c] * scale


def mended(turned, mended_ref, at, lanes):
    rows = turned.shape[0]
    row = lax.broadcasted_iota(jnp.int32, turned.shape, 0)
    turned = jnp.where(row == 0, mended_ref[0, at : at + 1, lanes], turned)
    return jnp.where(row == rows - 1, mended_ref[1, at : at + 1, lanes], turned)


def mend_and_send_kernel(
    line,
    units,
    turned_ref,
    edge_ref,
    raw_ref,
    beyond_ref,
    axes_ref,
    pins_ref,
    out_ref,
    sent_ref,
    mended_ref,
):
    planes = line.planes
    mend_edges(edge_ref, raw_ref, beyond_ref, mended_ref)
    for tile in range(turned_ref.shape[3] // LANES):
        lanes = slice(tile * LANES, (tile + 1) * LANES)
        field = read_field(turned_ref, lanes)
        for c in range(3):
            for i in range(planes):
                field[c][i] = mended(field[c][i], mended_ref, c * planes + i, lanes)
                out_ref[c, i, :, lanes] = field[c][i]
        send_tile(line, units, RHS, field, axes_ref, pins_ref, sent_ref, tile)


def last_kernel(turned_ref, edge_ref, raw_ref, beyond_ref, out_hbm, out_ref, mended_ref, sems):
    planes = turned_ref.shape[1]

    def copy(i):
        return pltpu.make_async_copy(out_ref.at[:, i], out_hbm.at[:, i], sems.at[i])

    mend_edges(edge_ref, raw_ref, beyond_ref, mended_ref)
    for i in range(planes):
        for c in range(3):
            out_ref[c, i] = mended(turned_ref[c, i], mended_ref, c * planes + i, slice(None))
        copy(i).start()
    for i in range(planes):
        copy(i).wait()


VMEM = pl.BlockSpec(memory_space=pltpu.VMEM)
HBM = pl.BlockSpec(memory_space=pltpu.HBM)
LIMIT = 32 * 1024 * 1024


def call(kernel, shapes, *operands, written=VMEM, scratch=()):
    shapes = [jax.ShapeDtypeStruct(shape, jnp.float32) for shape in shapes]
    return pl.pallas_call(
        kernel,
        out_shape=tuple(shapes),
        in_specs=[VMEM] * len(operands),
        out_specs=(written,) * len(shapes),
        scratch_shapes=scratch,
        compiler_params=pltpu.CompilerParams(vmem_limit_bytes=LIMIT),
    )(*operands)


def exchange(block, groups):
    parts = block.reshape(groups, -1, LANES)
    members = [
        list(range(start, start + groups)) for start in range(0, lax.axis_size("gx"), groups)
    ]
    return lax.all_to_all(
        parts, "gx", split_axis=0, concat_axis=0, axis_index_groups=members, tiled=True
    ).reshape(block.shape)


def swap_halves(block, groups):
    pairs = [(i, (i + groups) % (2 * groups)) for i in range(2 * groups)]
    return lax.ppermute(block, "gx", pairs)


def from_neighbours(edges):
    count = lax.axis_size("gy")
    forward = [(i, (i + 1) % count) for i in range(count)]
    if count == 2:
        return lax.ppermute(edges, "gy", forward)
    backward = [(target, source) for source, target in forward]
    return jnp.stack(
        [lax.ppermute(edges[0], "gy", backward), lax.ppermute(edges[1], "gy", forward)]
    )


def per_device(magnetization, easy_axes, pins):
    _, planes, rows, width = magnetization.shape
    groups = lax.axis_size("gx") // 2
    units = rows * (width // LANES) // groups
    line = Line(planes)
    levels = make_levels(planes, groups)
    level, pair = Level(planes, groups), Level(planes * groups, 2)
    whole = magnetization.shape
    sent_shape = (groups * RHS * units, LANES)
    edge_shape = (2, 3 * planes, width)

    field = magnetization
    (coupling,) = call(
        functools.partial(coupling_kernel, line, units),
        [(groups * (COUPLED - RHS) * units, LANES)],
        easy_axes,
    )
    (sent,) = call(
        functools.partial(first_kernel, line, groups, units),
        [(groups * COUPLED * units, LANES)],
        coupling,
        field,
        easy_axes,
        pins,
    )
    coupling = None
    for stepno in range(STEPS):
        gathered = exchange(sent, groups)
        coupled = stepno == 0
        if coupled:
            coupling = gathered
        (joined,) = call(
            functools.partial(join_kernel, level, levels, units, coupled),
            [((COUPLED if coupled else RHS) * units, LANES)],
            gathered,
            coupling,
        )
        swapped = swap_halves(joined, groups)
        if coupled:
            across = (joined, swapped)
        (ghosts,) = call(
            functools.partial(part_kernel, level, levels, pair, units, coupled),
            [sent_shape],
            joined,
            swapped,
            *across,
            gathered,
            coupling,
        )
        ghosts = exchange(ghosts, groups)
        solved, edges = call(
            functools.partial(finish_kernel, line, units),
            [whole, edge_shape],
            field,
            easy_axes,
            pins,
            ghosts,
        )
        beyond = from_neighbours(edges)
        turned, raw = call(turn_kernel, [whole, edge_shape], solved, easy_axes)
        if stepno < STEPS - 1:
            field, sent = call(
                functools.partial(mend_and_send_kernel, line, units),
                [whole, sent_shape],
                turned,
                edges,
                raw,
                beyond,
                easy_axes,
                pins,
                scratch=[pltpu.VMEM(edge_shape, jnp.float32)],
            )
        else:
            (field,) = call(
                last_kernel,
                [whole],
                turned,
                edges,
                raw,
                beyond,
                written=HBM,
                scratch=[
                    pltpu.VMEM(whole, jnp.float32),
                    pltpu.VMEM(edge_shape, jnp.float32),
                    pltpu.SemaphoreType.DMA((planes,)),
                ],
            )
    return field


def solution(mesh):
    in_specs = (P(None, "gx", "gy", None), P(None, "gx", "gy", None), P(None, None, "gy", None))
    out_specs = P(None, "gx", "gy", None)
    return jax.shard_map(
        per_device, mesh=mesh, in_specs=in_specs, out_specs=out_specs, check_vma=False
    )
```

```python
import functools

import jax
import jax.numpy as jnp
import numpy as np
from jax import lax
from jax.experimental import pallas as pl
from jax.experimental.pallas import tpu as pltpu
from jax.sharding import PartitionSpec as P

STEPS = 2
LANES = 128
RHS = 6
COUPLED = 16

diffusion = 4000.0
anisotropy_rate = 0.3
torque_rate = 0.2
exchange_rate = 0.1
norm_floor = 0.5


class Line:
    def __init__(self, planes):
        leading = 1.0 + 2.0 * diffusion
        pivots = [leading]
        for _ in range(1, planes):
            pivots.append(leading - diffusion * diffusion / pivots[-1])
        self.planes = planes
        self.inverse_pivot = [1.0 / p for p in pivots]
        self.factor = [0.0] + [diffusion / p for p in pivots[:-1]]
        block = (
            leading * np.eye(planes)
            - diffusion * np.eye(planes, k=1)
            - diffusion * np.eye(planes, k=-1)
        )
        self.from_low = diffusion * np.linalg.inv(block)[:, 0]
        self.from_high = self.from_low[::-1]

    def solve(self, source):
        planes = self.planes
        carried = [source[0]]
        for i in range(1, planes):
            carried.append(source[i] + self.factor[i] * carried[-1])
        solved = [None] * planes
        solved[-1] = carried[-1] * self.inverse_pivot[-1]
        for i in range(planes - 2, -1, -1):
            solved[i] = carried[i] * self.inverse_pivot[i] + self.factor[i + 1] * solved[i + 1]
        return solved


class Level:
    def __init__(self, length, radix):
        self.radix = radix
        line = Line(length)
        near, far = line.from_low[0], line.from_low[-1]
        count = 2 * radix
        inside = np.kron(np.eye(radix), np.array([[near, far], [far, near]]))
        pick = np.zeros((count, count))
        for r in range(radix):
            if r > 0:
                pick[2 * r, 2 * r - 1] = 1.0
            if r < radix - 1:
                pick[2 * r + 1, 2 * r + 2] = 1.0
        outer = np.zeros((count, 2))
        outer[0, 0] = outer[count - 1, 1] = 1.0
        settle = np.linalg.inv(np.eye(count) - pick @ inside)
        self.ghosts = settle @ pick
        self.passed = settle @ outer
        ends = (np.eye(count) + inside @ self.ghosts)[[0, count - 1]]
        self.ends = ends


def radices_of(groups):
    found = []
    while groups > 1:
        radix = 4 if groups % 4 == 0 else 2
        assert groups % radix == 0
        found.append(radix)
        groups //= radix
    return found


def combine(weights, terms):
    total = None
    for weight, term in zip(weights, terms):
        if weight == 0.0 or term is None:
            continue
        part = term * float(weight)
        total = part if total is None else total + part
    return total


def make_levels(planes, groups):
    found = []
    for radix in radices_of(groups):
        found.append(Level(planes, radix))
        planes *= radix
    return found


def settle(levels, ends):
    level, count = levels[0], 2 * levels[0].radix
    if len(levels) == 1:
        return [combine(weights, ends) for weights in level.ghosts]
    joined = []
    for start in range(0, len(ends), count):
        part = ends[start : start + count]
        joined += [combine(weights, part) for weights in level.ends]
    outer = settle(levels[1:], joined)
    found = []
    for at, start in enumerate(range(0, len(ends), count)):
        part = list(ends[start : start + count]) + [outer[2 * at], outer[2 * at + 1]]
        for inside, passed in zip(level.ghosts, level.passed):
            found.append(combine(list(inside) + list(passed), part))
    return found


def plus(total, weight, term):
    return total if term is None else total + weight * term


def pieces(value, values, units, tile, rows):
    step = min(units, rows)
    for start in range(0, rows, step):
        at = tile * rows + start
        to = (at // units * values + value) * units + at % units
        yield slice(start, start + step), slice(to, to + step)


def pinned(source, pins_ref, component, lanes):
    position = lax.axis_index("gx")
    first = jnp.where(position == 0, diffusion, 0.0).astype(jnp.float32)
    last = jnp.where(position == lax.axis_size("gx") - 1, diffusion, 0.0).astype(jnp.float32)
    source[0] = source[0] + first * pins_ref[0, component, :, lanes]
    source[-1] = source[-1] + last * pins_ref[1, component, :, lanes]
    return source


def read_field(field_ref, lanes):
    planes = field_ref.shape[1]
    return [[field_ref[c, i, :, lanes] for i in range(planes)] for c in range(3)]


def solve_components(line, field, axes_ref, pins_ref, lanes, ghosts):
    planes = line.planes
    axes = [[axes_ref[c, i, :, lanes] for i in range(planes)] for c in range(3)]
    for component in range(3):
        source = []
        for i in range(planes):
            projection = (
                field[0][i] * axes[0][i] + field[1][i] * axes[1][i] + field[2][i] * axes[2][i]
            )
            source.append(
                field[component][i] + (anisotropy_rate * projection) * axes[component][i]
            )
        source = pinned(source, pins_ref, component, lanes)
        if ghosts is not None:
            source[0] = source[0] + diffusion * ghosts[component][0]
            source[-1] = source[-1] + diffusion * ghosts[component][1]
        field[component] = line.solve(source)
    return field


def couplings(line, axes_ref, lanes):
    planes = line.planes
    low, high = line.from_low, line.from_high
    axes = [[axes_ref[c, i, :, lanes] for i in range(planes)] for c in range(3)]
    scaled = [anisotropy_rate * a for a in axes[1]]
    first_second = [axes[0][i] * scaled[i] for i in range(planes)]
    second_third = [axes[2][i] * scaled[i] for i in range(planes)]
    first_third = [(anisotropy_rate * axes[0][i]) * axes[2][i] for i in range(planes)]

    def weighted(terms, weights):
        total = terms[0] * float(weights[0] / diffusion)
        for i in range(1, planes):
            total = total + terms[i] * float(weights[i] / diffusion)
        return total

    found = []
    for product in (first_second, second_third):
        for weights in (low * low, low * high, high * high):
            found.append(weighted(product, weights))
    for ghost in (low, high):
        moved = line.solve([first_second[i] * float(ghost[i]) for i in range(planes)])
        pushed = [
            second_third[i] * moved[i] + first_third[i] * float(ghost[i]) for i in range(planes)
        ]
        found.append(weighted(pushed, low))
        found.append(weighted(pushed, high))
    return found


def send_tile(line, units, values, field, axes_ref, pins_ref, out_ref, tile):
    rows = axes_ref.shape[2]
    lanes = slice(tile * LANES, (tile + 1) * LANES)
    solved = solve_components(line, field, axes_ref, pins_ref, lanes, None)
    for component in range(3):
        for side, end in enumerate((0, -1)):
            value = 2 * component + side
            for source, target in pieces(value, values, units, tile, rows):
                out_ref[target, :] = solved[component][end][source]


def coupling_kernel(line, units, axes_ref, out_ref):
    rows, width = axes_ref.shape[2:]
    tiles = width // LANES
    for tile in range(tiles):
        found = couplings(line, axes_ref, slice(tile * LANES, (tile + 1) * LANES))
        for value, one in enumerate(found):
            for source, target in pieces(value, COUPLED - RHS, units, tile, rows):
                out_ref[target, :] = one[source]


def first_kernel(line, groups, units, coupling_ref, field_ref, axes_ref, pins_ref, out_ref):
    extra = (COUPLED - RHS) * units
    for d in range(groups):
        start = (d * COUPLED + RHS) * units
        out_ref[start : start + extra, :] = coupling_ref[d * extra : (d + 1) * extra, :]
    for tile in range(field_ref.shape[3] // LANES):
        field = read_field(field_ref, slice(tile * LANES, (tile + 1) * LANES))
        send_tile(line, units, COUPLED, field, axes_ref, pins_ref, out_ref, tile)


def solve_children(level, levels, rhs, coupling, outer):
    def ghosts(ends, component):
        found = settle(levels, ends)
        if outer is None:
            return found
        low, high = outer[component]
        moved = []
        for ghost, passed in zip(found, level.passed):
            terms = combine(passed, [low, high])
            moved.append(terms if ghost is None else ghost if terms is None else ghost + terms)
        return moved

    first = ghosts(rhs[0], 0)
    middle = []
    for d in range(level.radix):
        c, low, high = coupling[d], first[2 * d], first[2 * d + 1]
        middle.append(plus(plus(rhs[1][2 * d], c[0], low), c[1], high))
        middle.append(plus(plus(rhs[1][2 * d + 1], c[1], low), c[2], high))
    second = ghosts(middle, 1)
    last = []
    for d in range(level.radix):
        c, low1, high1 = coupling[d], first[2 * d], first[2 * d + 1]
        low2, high2 = second[2 * d], second[2 * d + 1]
        total = plus(plus(rhs[2][2 * d], c[3], low2), c[4], high2)
        last.append(plus(plus(total, c[6], low1), c[8], high1))
        total = plus(plus(rhs[2][2 * d + 1], c[4], low2), c[5], high2)
        last.append(plus(plus(total, c[7], low1), c[9], high1))
    return (first, second, ghosts(last, 2)), (rhs[0], middle, last)


def facing_coupling(level, levels, coupling, side):
    passed = level.passed[:, side]
    moved2, moved3 = [], []
    for r in range(level.radix):
        c, low, high = coupling[r], float(passed[2 * r]), float(passed[2 * r + 1])
        moved2 += [c[0] * low + c[1] * high, c[1] * low + c[2] * high]
        moved3 += [c[3] * low + c[4] * high, c[4] * low + c[5] * high]
    inner = settle(levels, moved2)
    through = []
    for r in range(level.radix):
        c, low, high = coupling[r], float(passed[2 * r]), float(passed[2 * r + 1])
        k_low, k_high = inner[2 * r], inner[2 * r + 1]
        total = plus(c[6] * low + c[8] * high, c[3], k_low)
        through.append(plus(total, c[4], k_high))
        total = plus(c[7] * low + c[9] * high, c[4], k_low)
        through.append(plus(total, c[5], k_high))
    return [combine(level.ends[side], moved) for moved in (moved2, moved3, through)]


def read_children(level, units, rhs_values, rhs_ref, coupling_ref):
    def read(ref, values, d, value):
        start = (d * values + value) * units
        return ref[start : start + units, :]

    rhs = [
        [read(rhs_ref, rhs_values, k // 2, 2 * c + k % 2) for k in range(2 * level.radix)]
        for c in range(3)
    ]
    coupling = [
        [read(coupling_ref, COUPLED, d, v) for v in range(RHS, COUPLED)]
        for d in range(level.radix)
    ]
    return rhs, coupling


def join_kernel(level, levels, units, coupled, rhs_ref, coupling_ref, out_ref):
    upper = lax.axis_index("gx") >= level.radix
    values = COUPLED if coupled else RHS
    rhs, coupling = read_children(level, units, values, rhs_ref, coupling_ref)
    _, seen = solve_children(level, levels, rhs, coupling, None)
    ends = [[combine(level.ends[side], seen[c]) for c in range(3)] for side in range(2)]
    if coupled:
        for side in range(2):
            ends[side] += facing_coupling(level, levels, coupling, side)
    for value, (first, last) in enumerate(zip(*ends)):
        out_ref[value * units : (value + 1) * units, :] = jnp.where(upper, first, last)


def part_kernel(
    level,
    levels,
    near,
    units,
    coupled,
    own_ref,
    other_ref,
    own_coupling_ref,
    other_coupling_ref,
    rhs_ref,
    coupling_ref,
    out_ref,
):
    upper = lax.axis_index("gx") >= level.radix

    def read(ref, value):
        return ref[value * units : (value + 1) * units, :]

    settled = 1.0 / (1.0 - near * near)

    def meet(own, other):
        beyond = other * settled + own * (near * settled)
        return beyond, own * settled + other * (near * settled)

    own = [read(own_ref, c) for c in range(3)]
    other = [read(other_ref, c) for c in range(3)]
    own_c = [read(own_coupling_ref, 3 + v) for v in range(3)]
    other_c = [read(other_coupling_ref, 3 + v) for v in range(3)]
    beyond1, back1 = meet(own[0], other[0])
    beyond2, back2 = meet(own[1] + own_c[0] * beyond1, other[1] + other_c[0] * back1)
    beyond3, _ = meet(
        own[2] + own_c[1] * beyond2 + own_c[2] * beyond1,
        other[2] + other_c[1] * back2 + other_c[2] * back1,
    )
    outer = [
        [jnp.where(upper, beyond, 0.0), jnp.where(upper, 0.0, beyond)]
        for beyond in (beyond1, beyond2, beyond3)
    ]
    values = COUPLED if coupled else RHS
    rhs, coupling = read_children(level, units, values, rhs_ref, coupling_ref)
    found, _ = solve_children(level, levels, rhs, coupling, outer)
    for c, ghosts in enumerate(found):
        for k, ghost in enumerate(ghosts):
            start = (k // 2 * RHS + 2 * c + k % 2) * units
            out_ref[start : start + units, :] = ghost


def finish_kernel(line, units, field_ref, axes_ref, pins_ref, ghost_ref, out_ref, edge_ref):
    planes = line.planes
    rows, width = field_ref.shape[2], field_ref.shape[3]
    tiles = width // LANES
    for tile in range(tiles):
        lanes = slice(tile * LANES, (tile + 1) * LANES)
        ghosts = [
            [
                jnp.concatenate(
                    [
                        ghost_ref[target, :]
                        for _, target in pieces(2 * c + side, RHS, units, tile, rows)
                    ],
                    axis=0,
                )
                for side in range(2)
            ]
            for c in range(3)
        ]
        field = read_field(field_ref, lanes)
        solved = solve_components(line, field, axes_ref, pins_ref, lanes, ghosts)
        for c in range(3):
            for i in range(planes):
                out_ref[c, i, :, lanes] = solved[c][i]
                at = c * planes + i
                edge_ref[0, at : at + 1, lanes] = solved[c][i][:1]
                edge_ref[1, at : at + 1, lanes] = solved[c][i][rows - 1 :]


def unit_scale(parts):
    square = parts[0] * parts[0] + parts[1] * parts[1] + parts[2] * parts[2]
    return jnp.minimum(lax.rsqrt(square), 1.0 / norm_floor)


def turn_kernel(field_ref, axes_ref, out_ref, raw_ref):
    planes, rows, width = field_ref.shape[1:]
    row = lax.broadcasted_iota(jnp.int32, (rows, width), 0)
    for i in range(planes):
        field = [field_ref[c, i] for c in range(3)]
        axes = [axes_ref[c, i] for c in range(3)]
        projection = field[0] * axes[0] + field[1] * axes[1] + field[2] * axes[2]
        effective = []
        for c in range(3):
            below = jnp.where(row == 0, 0.0, pltpu.roll(field[c], 1, 0))
            above = jnp.where(row == rows - 1, 0.0, pltpu.roll(field[c], rows - 1, 0))
            beside = pltpu.roll(field[c], 1, 1) + pltpu.roll(field[c], width - 1, 1)
            effective.append(
                exchange_rate * (((above + below) + beside) - 4.0 * field[c])
                + projection * axes[c]
            )
        rotated = []
        for c in range(3):
            d, e = (c + 1) % 3, (c + 2) % 3
            twisted = field[d] * effective[e] - field[e] * effective[d]
            rotated.append(field[c] - torque_rate * twisted)
        scale = unit_scale(rotated)
        for c in range(3):
            at = c * planes + i
            out_ref[c, i] = rotated[c] * scale
            raw_ref[0, at : at + 1, :] = rotated[c][:1]
            raw_ref[1, at : at + 1, :] = rotated[c][rows - 1 :]


def mend_edges(edge_ref, raw_ref, beyond_ref, mended_ref):
    planes = edge_ref.shape[1] // 3
    for side in range(2):
        parts = [slice(c * planes, (c + 1) * planes) for c in range(3)]
        field = [edge_ref[side, part, :] for part in parts]
        beyond = [beyond_ref[1 - side, part, :] for part in parts]
        rotated = []
        for c in range(3):
            d, e = (c + 1) % 3, (c + 2) % 3
            twisted = field[d] * beyond[e] - field[e] * beyond[d]
            rotated.append(raw_ref[side, parts[c], :] - (torque_rate * exchange_rate) * twisted)
        scale = unit_scale(rotated)
        for c in range(3):
            mended_ref[side, parts[c], :] = rotated[c] * scale


def mended(turned, mended_ref, at, lanes):
    rows = turned.shape[0]
    row = lax.broadcasted_iota(jnp.int32, turned.shape, 0)
    turned = jnp.where(row == 0, mended_ref[0, at : at + 1, lanes], turned)
    return jnp.where(row == rows - 1, mended_ref[1, at : at + 1, lanes], turned)


def mend_and_send_kernel(
    line,
    units,
    turned_ref,
    edge_ref,
    raw_ref,
    beyond_ref,
    axes_ref,
    pins_ref,
    out_ref,
    sent_ref,
    mended_ref,
):
    planes = line.planes
    mend_edges(edge_ref, raw_ref, beyond_ref, mended_ref)
    for tile in range(turned_ref.shape[3] // LANES):
        lanes = slice(tile * LANES, (tile + 1) * LANES)
        field = read_field(turned_ref, lanes)
        for c in range(3):
            for i in range(planes):
                field[c][i] = mended(field[c][i], mended_ref, c * planes + i, lanes)
                out_ref[c, i, :, lanes] = field[c][i]
        send_tile(line, units, RHS, field, axes_ref, pins_ref, sent_ref, tile)


def last_kernel(turned_ref, edge_ref, raw_ref, beyond_ref, out_hbm, out_ref, mended_ref, sems):
    planes = turned_ref.shape[1]

    def copy(i):
        return pltpu.make_async_copy(out_ref.at[:, i], out_hbm.at[:, i], sems.at[i])

    mend_edges(edge_ref, raw_ref, beyond_ref, mended_ref)
    for i in range(planes):
        for c in range(3):
            out_ref[c, i] = mended(turned_ref[c, i], mended_ref, c * planes + i, slice(None))
        copy(i).start()
    for i in range(planes):
        copy(i).wait()


VMEM = pl.BlockSpec(memory_space=pltpu.VMEM)
HBM = pl.BlockSpec(memory_space=pltpu.HBM)
LIMIT = 32 * 1024 * 1024


def call(kernel, shapes, *operands, written=VMEM, scratch=()):
    shapes = [jax.ShapeDtypeStruct(shape, jnp.float32) for shape in shapes]
    return pl.pallas_call(
        kernel,
        out_shape=tuple(shapes),
        in_specs=[VMEM] * len(operands),
        out_specs=(written,) * len(shapes),
        scratch_shapes=scratch,
        compiler_params=pltpu.CompilerParams(vmem_limit_bytes=LIMIT),
    )(*operands)


def exchange(block, groups):
    parts = block.reshape(groups, -1, LANES)
    members = [
        list(range(start, start + groups)) for start in range(0, lax.axis_size("gx"), groups)
    ]
    return lax.all_to_all(
        parts, "gx", split_axis=0, concat_axis=0, axis_index_groups=members, tiled=True
    ).reshape(block.shape)


def swap_halves(block, groups):
    pairs = [(i, (i + groups) % (2 * groups)) for i in range(2 * groups)]
    return lax.ppermute(block, "gx", pairs)


def from_neighbours(edges):
    count = lax.axis_size("gy")
    forward = [(i, (i + 1) % count) for i in range(count)]
    if count == 2:
        return lax.ppermute(edges, "gy", forward)
    backward = [(target, source) for source, target in forward]
    return jnp.stack(
        [lax.ppermute(edges[0], "gy", backward), lax.ppermute(edges[1], "gy", forward)]
    )


def per_device(magnetization, easy_axes, pins):
    _, planes, rows, width = magnetization.shape
    groups = lax.axis_size("gx") // 2
    units = rows * (width // LANES) // groups
    line = Line(planes)
    levels = make_levels(planes, groups)
    level = Level(planes, groups)
    near = float(Line(planes * groups).from_low[0])
    whole = magnetization.shape
    sent_shape = (groups * RHS * units, LANES)
    edge_shape = (2, 3 * planes, width)

    field = magnetization
    (coupling,) = call(
        functools.partial(coupling_kernel, line, units),
        [(groups * (COUPLED - RHS) * units, LANES)],
        easy_axes,
    )
    (sent,) = call(
        functools.partial(first_kernel, line, groups, units),
        [(groups * COUPLED * units, LANES)],
        coupling,
        field,
        easy_axes,
        pins,
    )
    coupling = None
    for stepno in range(STEPS):
        gathered = exchange(sent, groups)
        coupled = stepno == 0
        if coupled:
            coupling = gathered
        (joined,) = call(
            functools.partial(join_kernel, level, levels, units, coupled),
            [((6 if coupled else 3) * units, LANES)],
            gathered,
            coupling,
        )
        swapped = swap_halves(joined, groups)
        if coupled:
            across = (joined, swapped)
        (ghosts,) = call(
            functools.partial(part_kernel, level, levels, near, units, coupled),
            [sent_shape],
            joined,
            swapped,
            *across,
            gathered,
            coupling,
        )
        ghosts = exchange(ghosts, groups)
        solved, edges = call(
            functools.partial(finish_kernel, line, units),
            [whole, edge_shape],
            field,
            easy_axes,
            pins,
            ghosts,
        )
        beyond = from_neighbours(edges)
        turned, raw = call(turn_kernel, [whole, edge_shape], solved, easy_axes)
        if stepno < STEPS - 1:
            field, sent = call(
                functools.partial(mend_and_send_kernel, line, units),
                [whole, sent_shape],
                turned,
                edges,
                raw,
                beyond,
                easy_axes,
                pins,
                scratch=[pltpu.VMEM(edge_shape, jnp.float32)],
            )
        else:
            (field,) = call(
                last_kernel,
                [whole],
                turned,
                edges,
                raw,
                beyond,
                written=HBM,
                scratch=[
                    pltpu.VMEM(whole, jnp.float32),
                    pltpu.VMEM(edge_shape, jnp.float32),
                    pltpu.SemaphoreType.DMA((planes,)),
                ],
            )
    return field


def solution(mesh):
    in_specs = (P(None, "gx", "gy", None), P(None, "gx", "gy", None), P(None, None, "gy", None))
    out_specs = P(None, "gx", "gy", None)
    return jax.shard_map(
        per_device, mesh=mesh, in_specs=in_specs, out_specs=out_specs, check_vma=False
    )
```

```python
import functools

import jax
import jax.numpy as jnp
import numpy as np
from jax import lax
from jax.experimental import pallas as pl
from jax.experimental.pallas import tpu as pltpu
from jax.sharding import PartitionSpec as P

STEPS = 2
LANES = 128
RHS = 6
COUPLED = 16

diffusion = 4000.0
anisotropy_rate = 0.3
torque_rate = 0.2
exchange_rate = 0.1
norm_floor = 0.5


class Line:
    def __init__(self, planes):
        leading = 1.0 + 2.0 * diffusion
        pivots = [leading]
        for _ in range(1, planes):
            pivots.append(leading - diffusion * diffusion / pivots[-1])
        self.planes = planes
        self.inverse_pivot = [1.0 / p for p in pivots]
        self.factor = [0.0] + [diffusion / p for p in pivots[:-1]]
        block = (
            leading * np.eye(planes)
            - diffusion * np.eye(planes, k=1)
            - diffusion * np.eye(planes, k=-1)
        )
        self.from_low = diffusion * np.linalg.inv(block)[:, 0]
        self.from_high = self.from_low[::-1]

    def solve(self, source):
        planes = self.planes
        carried = [source[0]]
        for i in range(1, planes):
            carried.append(source[i] + self.factor[i] * carried[-1])
        solved = [None] * planes
        solved[-1] = carried[-1] * self.inverse_pivot[-1]
        for i in range(planes - 2, -1, -1):
            solved[i] = carried[i] * self.inverse_pivot[i] + self.factor[i + 1] * solved[i + 1]
        return solved


class Level:
    def __init__(self, length, radix):
        self.radix = radix
        line = Line(length)
        near, far = line.from_low[0], line.from_low[-1]
        count = 2 * radix
        inside = np.kron(np.eye(radix), np.array([[near, far], [far, near]]))
        pick = np.zeros((count, count))
        for r in range(radix):
            if r > 0:
                pick[2 * r, 2 * r - 1] = 1.0
            if r < radix - 1:
                pick[2 * r + 1, 2 * r + 2] = 1.0
        outer = np.zeros((count, 2))
        outer[0, 0] = outer[count - 1, 1] = 1.0
        settle = np.linalg.inv(np.eye(count) - pick @ inside)
        self.ghosts = settle @ pick
        self.passed = settle @ outer
        ends = (np.eye(count) + inside @ self.ghosts)[[0, count - 1]]
        self.ends = ends


def radices_of(groups):
    found = []
    while groups > 1:
        radix = 4 if groups % 4 == 0 else 2
        assert groups % radix == 0
        found.append(radix)
        groups //= radix
    return found


def combine(weights, terms):
    total = None
    for weight, term in zip(weights, terms):
        if weight == 0.0 or term is None:
            continue
        part = term * float(weight)
        total = part if total is None else total + part
    return total


def make_levels(planes, groups):
    found = []
    for radix in radices_of(groups):
        found.append(Level(planes, radix))
        planes *= radix
    return found


def settle(levels, ends):
    level, count = levels[0], 2 * levels[0].radix
    if len(levels) == 1:
        return [combine(weights, ends) for weights in level.ghosts]
    joined = []
    for start in range(0, len(ends), count):
        part = ends[start : start + count]
        joined += [combine(weights, part) for weights in level.ends]
    outer = settle(levels[1:], joined)
    found = []
    for at, start in enumerate(range(0, len(ends), count)):
        part = list(ends[start : start + count]) + [outer[2 * at], outer[2 * at + 1]]
        for inside, passed in zip(level.ghosts, level.passed):
            found.append(combine(list(inside) + list(passed), part))
    return found


def plus(total, weight, term):
    return total if term is None else total + weight * term


def pieces(value, values, units, tile, rows):
    step = min(units, rows)
    for start in range(0, rows, step):
        at = tile * rows + start
        to = (at // units * values + value) * units + at % units
        yield slice(start, start + step), slice(to, to + step)


def pinned(source, pins_ref, component, lanes):
    position = lax.axis_index("gx")
    first = jnp.where(position == 0, diffusion, 0.0).astype(jnp.float32)
    last = jnp.where(position == lax.axis_size("gx") - 1, diffusion, 0.0).astype(jnp.float32)
    source[0] = source[0] + first * pins_ref[0, component, :, lanes]
    source[-1] = source[-1] + last * pins_ref[1, component, :, lanes]
    return source


def read_field(field_ref, lanes):
    planes = field_ref.shape[1]
    return [[field_ref[c, i, :, lanes] for i in range(planes)] for c in range(3)]


def solve_components(line, field, scaled_ref, pins_ref, lanes, ghosts):
    planes = line.planes
    scaled = [[scaled_ref[c, i, :, lanes] for i in range(planes)] for c in range(3)]
    projection = [
        field[0][i] * scaled[0][i] + field[1][i] * scaled[1][i] + field[2][i] * scaled[2][i]
        for i in range(planes)
    ]
    for component in range(3):
        source = [
            field[component][i] + projection[i] * scaled[component][i] for i in range(planes)
        ]
        source = pinned(source, pins_ref, component, lanes)
        if ghosts is not None:
            source[0] = source[0] + diffusion * ghosts[component][0]
            source[-1] = source[-1] + diffusion * ghosts[component][1]
        solved = line.solve(source)
        if component < 2:
            projection = [
                projection[i] + (solved[i] - field[component][i]) * scaled[component][i]
                for i in range(planes)
            ]
        field[component] = solved
    return field


def couplings(line, scaled):
    planes = line.planes
    low, high = line.from_low, line.from_high
    first_second = [scaled[0][i] * scaled[1][i] for i in range(planes)]
    second_third = [scaled[1][i] * scaled[2][i] for i in range(planes)]
    first_third = [scaled[0][i] * scaled[2][i] for i in range(planes)]

    def weighted(terms, weights):
        total = terms[0] * float(weights[0] / diffusion)
        for i in range(1, planes):
            total = total + terms[i] * float(weights[i] / diffusion)
        return total

    found = []
    for product in (first_second, second_third):
        for weights in (low * low, low * high, high * high):
            found.append(weighted(product, weights))
    for ghost in (low, high):
        moved = line.solve([first_second[i] * float(ghost[i]) for i in range(planes)])
        pushed = [
            second_third[i] * moved[i] + first_third[i] * float(ghost[i]) for i in range(planes)
        ]
        found.append(weighted(pushed, low))
        found.append(weighted(pushed, high))
    return found


def send_tile(line, units, values, field, scaled_ref, pins_ref, out_ref, tile):
    rows = scaled_ref.shape[2]
    lanes = slice(tile * LANES, (tile + 1) * LANES)
    solved = solve_components(line, field, scaled_ref, pins_ref, lanes, None)
    for component in range(3):
        for side, end in enumerate((0, -1)):
            value = 2 * component + side
            for source, target in pieces(value, values, units, tile, rows):
                out_ref[target, :] = solved[component][end][source]


def scaled_tile(axes_ref, lanes):
    root = float(np.sqrt(anisotropy_rate))
    planes = axes_ref.shape[1]
    return [[root * axes_ref[c, i, :, lanes] for i in range(planes)] for c in range(3)]


def coupling_kernel(line, units, axes_ref, out_ref):
    rows, width = axes_ref.shape[2:]
    for tile in range(width // LANES):
        lanes = slice(tile * LANES, (tile + 1) * LANES)
        for value, one in enumerate(couplings(line, scaled_tile(axes_ref, lanes))):
            for source, target in pieces(value, COUPLED - RHS, units, tile, rows):
                out_ref[target, :] = one[source]


def first_kernel(
    line, groups, units, coupling_ref, field_ref, axes_ref, pins_ref, out_ref, scaled_ref
):
    extra = (COUPLED - RHS) * units
    for d in range(groups):
        start = (d * COUPLED + RHS) * units
        out_ref[start : start + extra, :] = coupling_ref[d * extra : (d + 1) * extra, :]
    for tile in range(field_ref.shape[3] // LANES):
        lanes = slice(tile * LANES, (tile + 1) * LANES)
        for c, parts in enumerate(scaled_tile(axes_ref, lanes)):
            for i, part in enumerate(parts):
                scaled_ref[c, i, :, lanes] = part
        field = read_field(field_ref, lanes)
        send_tile(line, units, COUPLED, field, scaled_ref, pins_ref, out_ref, tile)


def solve_children(level, levels, rhs, coupling, outer):
    def ghosts(ends, component):
        found = settle(levels, ends)
        if outer is None:
            return found
        low, high = outer[component]
        moved = []
        for ghost, passed in zip(found, level.passed):
            terms = combine(passed, [low, high])
            moved.append(terms if ghost is None else ghost if terms is None else ghost + terms)
        return moved

    first = ghosts(rhs[0], 0)
    middle = []
    for d in range(level.radix):
        c, low, high = coupling[d], first[2 * d], first[2 * d + 1]
        middle.append(plus(plus(rhs[1][2 * d], c[0], low), c[1], high))
        middle.append(plus(plus(rhs[1][2 * d + 1], c[1], low), c[2], high))
    second = ghosts(middle, 1)
    last = []
    for d in range(level.radix):
        c, low1, high1 = coupling[d], first[2 * d], first[2 * d + 1]
        low2, high2 = second[2 * d], second[2 * d + 1]
        total = plus(plus(rhs[2][2 * d], c[3], low2), c[4], high2)
        last.append(plus(plus(total, c[6], low1), c[8], high1))
        total = plus(plus(rhs[2][2 * d + 1], c[4], low2), c[5], high2)
        last.append(plus(plus(total, c[7], low1), c[9], high1))
    return (first, second, ghosts(last, 2)), (rhs[0], middle, last)


def facing_coupling(level, levels, coupling, side):
    passed = level.passed[:, side]
    moved2, moved3 = [], []
    for r in range(level.radix):
        c, low, high = coupling[r], float(passed[2 * r]), float(passed[2 * r + 1])
        moved2 += [c[0] * low + c[1] * high, c[1] * low + c[2] * high]
        moved3 += [c[3] * low + c[4] * high, c[4] * low + c[5] * high]
    inner = settle(levels, moved2)
    through = []
    for r in range(level.radix):
        c, low, high = coupling[r], float(passed[2 * r]), float(passed[2 * r + 1])
        k_low, k_high = inner[2 * r], inner[2 * r + 1]
        total = plus(c[6] * low + c[8] * high, c[3], k_low)
        through.append(plus(total, c[4], k_high))
        total = plus(c[7] * low + c[9] * high, c[4], k_low)
        through.append(plus(total, c[5], k_high))
    return [combine(level.ends[side], moved) for moved in (moved2, moved3, through)]


def read_children(level, units, rhs_values, rhs_ref, coupling_ref):
    def read(ref, values, d, value):
        start = (d * values + value) * units
        return ref[start : start + units, :]

    rhs = [
        [read(rhs_ref, rhs_values, k // 2, 2 * c + k % 2) for k in range(2 * level.radix)]
        for c in range(3)
    ]
    coupling = [
        [read(coupling_ref, COUPLED, d, v) for v in range(RHS, COUPLED)]
        for d in range(level.radix)
    ]
    return rhs, coupling


def join_kernel(level, levels, units, coupled, rhs_ref, coupling_ref, out_ref):
    upper = lax.axis_index("gx") >= level.radix
    values = COUPLED if coupled else RHS
    rhs, coupling = read_children(level, units, values, rhs_ref, coupling_ref)
    _, seen = solve_children(level, levels, rhs, coupling, None)
    ends = [[combine(level.ends[side], seen[c]) for c in range(3)] for side in range(2)]
    if coupled:
        for side in range(2):
            ends[side] += facing_coupling(level, levels, coupling, side)
    for value, (first, last) in enumerate(zip(*ends)):
        out_ref[value * units : (value + 1) * units, :] = jnp.where(upper, first, last)


def part_kernel(
    level,
    levels,
    near,
    units,
    coupled,
    own_ref,
    other_ref,
    own_coupling_ref,
    other_coupling_ref,
    rhs_ref,
    coupling_ref,
    out_ref,
):
    upper = lax.axis_index("gx") >= level.radix

    def read(ref, value):
        return ref[value * units : (value + 1) * units, :]

    settled = 1.0 / (1.0 - near * near)

    def meet(own, other):
        beyond = other * settled + own * (near * settled)
        return beyond, own * settled + other * (near * settled)

    own = [read(own_ref, c) for c in range(3)]
    other = [read(other_ref, c) for c in range(3)]
    own_c = [read(own_coupling_ref, 3 + v) for v in range(3)]
    other_c = [read(other_coupling_ref, 3 + v) for v in range(3)]
    beyond1, back1 = meet(own[0], other[0])
    beyond2, back2 = meet(own[1] + own_c[0] * beyond1, other[1] + other_c[0] * back1)
    beyond3, _ = meet(
        own[2] + own_c[1] * beyond2 + own_c[2] * beyond1,
        other[2] + other_c[1] * back2 + other_c[2] * back1,
    )
    outer = [
        [jnp.where(upper, beyond, 0.0), jnp.where(upper, 0.0, beyond)]
        for beyond in (beyond1, beyond2, beyond3)
    ]
    values = COUPLED if coupled else RHS
    rhs, coupling = read_children(level, units, values, rhs_ref, coupling_ref)
    found, _ = solve_children(level, levels, rhs, coupling, outer)
    for c, ghosts in enumerate(found):
        for k, ghost in enumerate(ghosts):
            start = (k // 2 * RHS + 2 * c + k % 2) * units
            out_ref[start : start + units, :] = ghost


def finish_kernel(line, units, field_ref, scaled_ref, pins_ref, ghost_ref, out_ref, edge_ref):
    planes = line.planes
    rows, width = field_ref.shape[2], field_ref.shape[3]
    tiles = width // LANES
    for tile in range(tiles):
        lanes = slice(tile * LANES, (tile + 1) * LANES)
        ghosts = [
            [
                jnp.concatenate(
                    [
                        ghost_ref[target, :]
                        for _, target in pieces(2 * c + side, RHS, units, tile, rows)
                    ],
                    axis=0,
                )
                for side in range(2)
            ]
            for c in range(3)
        ]
        field = read_field(field_ref, lanes)
        solved = solve_components(line, field, scaled_ref, pins_ref, lanes, ghosts)
        for c in range(3):
            for i in range(planes):
                out_ref[c, i, :, lanes] = solved[c][i]
                at = c * planes + i
                edge_ref[0, at : at + 1, lanes] = solved[c][i][:1]
                edge_ref[1, at : at + 1, lanes] = solved[c][i][rows - 1 :]


def unit_scale(parts):
    square = parts[0] * parts[0] + parts[1] * parts[1] + parts[2] * parts[2]
    return jnp.minimum(lax.rsqrt(square), 1.0 / norm_floor)


def turn_kernel(field_ref, scaled_ref, out_ref, raw_ref):
    planes, rows, width = field_ref.shape[1:]
    row = lax.broadcasted_iota(jnp.int32, (rows, width), 0)
    for i in range(planes):
        field = [field_ref[c, i] for c in range(3)]
        scaled = [scaled_ref[c, i] for c in range(3)]
        projection = field[0] * scaled[0] + field[1] * scaled[1] + field[2] * scaled[2]
        projection = projection * (1.0 / anisotropy_rate)
        effective = []
        for c in range(3):
            below = jnp.where(row == 0, 0.0, pltpu.roll(field[c], 1, 0))
            above = jnp.where(row == rows - 1, 0.0, pltpu.roll(field[c], rows - 1, 0))
            beside = pltpu.roll(field[c], 1, 1) + pltpu.roll(field[c], width - 1, 1)
            effective.append(
                exchange_rate * (((above + below) + beside) - 4.0 * field[c])
                + projection * scaled[c]
            )
        rotated = []
        for c in range(3):
            d, e = (c + 1) % 3, (c + 2) % 3
            twisted = field[d] * effective[e] - field[e] * effective[d]
            rotated.append(field[c] - torque_rate * twisted)
        scale = unit_scale(rotated)
        for c in range(3):
            at = c * planes + i
            out_ref[c, i] = rotated[c] * scale
            raw_ref[0, at : at + 1, :] = rotated[c][:1]
            raw_ref[1, at : at + 1, :] = rotated[c][rows - 1 :]


def mend_edges(edge_ref, raw_ref, beyond_ref, mended_ref):
    planes = edge_ref.shape[1] // 3
    for side in range(2):
        parts = [slice(c * planes, (c + 1) * planes) for c in range(3)]
        field = [edge_ref[side, part, :] for part in parts]
        beyond = [beyond_ref[1 - side, part, :] for part in parts]
        rotated = []
        for c in range(3):
            d, e = (c + 1) % 3, (c + 2) % 3
            twisted = field[d] * beyond[e] - field[e] * beyond[d]
            rotated.append(raw_ref[side, parts[c], :] - (torque_rate * exchange_rate) * twisted)
        scale = unit_scale(rotated)
        for c in range(3):
            mended_ref[side, parts[c], :] = rotated[c] * scale


def mended(turned, mended_ref, at, lanes):
    rows = turned.shape[0]
    row = lax.broadcasted_iota(jnp.int32, turned.shape, 0)
    turned = jnp.where(row == 0, mended_ref[0, at : at + 1, lanes], turned)
    return jnp.where(row == rows - 1, mended_ref[1, at : at + 1, lanes], turned)


def mend_and_send_kernel(
    line,
    units,
    turned_ref,
    edge_ref,
    raw_ref,
    beyond_ref,
    scaled_ref,
    pins_ref,
    out_ref,
    sent_ref,
    mended_ref,
):
    planes = line.planes
    mend_edges(edge_ref, raw_ref, beyond_ref, mended_ref)
    for tile in range(turned_ref.shape[3] // LANES):
        lanes = slice(tile * LANES, (tile + 1) * LANES)
        field = read_field(turned_ref, lanes)
        for c in range(3):
            for i in range(planes):
                field[c][i] = mended(field[c][i], mended_ref, c * planes + i, lanes)
                out_ref[c, i, :, lanes] = field[c][i]
        send_tile(line, units, RHS, field, scaled_ref, pins_ref, sent_ref, tile)


def last_kernel(turned_ref, edge_ref, raw_ref, beyond_ref, out_hbm, out_ref, mended_ref, sems):
    planes = turned_ref.shape[1]

    def copy(i):
        return pltpu.make_async_copy(out_ref.at[:, i], out_hbm.at[:, i], sems.at[i])

    mend_edges(edge_ref, raw_ref, beyond_ref, mended_ref)
    for i in range(planes):
        for c in range(3):
            out_ref[c, i] = mended(turned_ref[c, i], mended_ref, c * planes + i, slice(None))
        copy(i).start()
    for i in range(planes):
        copy(i).wait()


VMEM = pl.BlockSpec(memory_space=pltpu.VMEM)
HBM = pl.BlockSpec(memory_space=pltpu.HBM)
LIMIT = 32 * 1024 * 1024


def call(kernel, shapes, *operands, written=VMEM, scratch=()):
    shapes = [jax.ShapeDtypeStruct(shape, jnp.float32) for shape in shapes]
    return pl.pallas_call(
        kernel,
        out_shape=tuple(shapes),
        in_specs=[VMEM] * len(operands),
        out_specs=(written,) * len(shapes),
        scratch_shapes=scratch,
        compiler_params=pltpu.CompilerParams(vmem_limit_bytes=LIMIT),
    )(*operands)


def exchange(block, groups):
    parts = block.reshape(groups, -1, LANES)
    members = [
        list(range(start, start + groups)) for start in range(0, lax.axis_size("gx"), groups)
    ]
    return lax.all_to_all(
        parts, "gx", split_axis=0, concat_axis=0, axis_index_groups=members, tiled=True
    ).reshape(block.shape)


def swap_halves(block, groups):
    pairs = [(i, (i + groups) % (2 * groups)) for i in range(2 * groups)]
    return lax.ppermute(block, "gx", pairs)


def from_neighbours(edges):
    count = lax.axis_size("gy")
    forward = [(i, (i + 1) % count) for i in range(count)]
    if count == 2:
        return lax.ppermute(edges, "gy", forward)
    backward = [(target, source) for source, target in forward]
    return jnp.stack(
        [lax.ppermute(edges[0], "gy", backward), lax.ppermute(edges[1], "gy", forward)]
    )


def per_device(magnetization, easy_axes, pins):
    _, planes, rows, width = magnetization.shape
    groups = lax.axis_size("gx") // 2
    units = rows * (width // LANES) // groups
    line = Line(planes)
    levels = make_levels(planes, groups)
    level = Level(planes, groups)
    near = float(Line(planes * groups).from_low[0])
    whole = magnetization.shape
    sent_shape = (groups * RHS * units, LANES)
    edge_shape = (2, 3 * planes, width)

    field = magnetization
    (coupling,) = call(
        functools.partial(coupling_kernel, line, units),
        [(groups * (COUPLED - RHS) * units, LANES)],
        easy_axes,
    )
    sent, scaled = call(
        functools.partial(first_kernel, line, groups, units),
        [(groups * COUPLED * units, LANES), whole],
        coupling,
        field,
        easy_axes,
        pins,
    )
    coupling = None
    for stepno in range(STEPS):
        gathered = exchange(sent, groups)
        coupled = stepno == 0
        if coupled:
            coupling = gathered
        (joined,) = call(
            functools.partial(join_kernel, level, levels, units, coupled),
            [((6 if coupled else 3) * units, LANES)],
            gathered,
            coupling,
        )
        swapped = swap_halves(joined, groups)
        if coupled:
            across = (joined, swapped)
        (ghosts,) = call(
            functools.partial(part_kernel, level, levels, near, units, coupled),
            [sent_shape],
            joined,
            swapped,
            *across,
            gathered,
            coupling,
        )
        ghosts = exchange(ghosts, groups)
        solved, edges = call(
            functools.partial(finish_kernel, line, units),
            [whole, edge_shape],
            field,
            scaled,
            pins,
            ghosts,
        )
        beyond = from_neighbours(edges)
        turned, raw = call(turn_kernel, [whole, edge_shape], solved, scaled)
        if stepno < STEPS - 1:
            field, sent = call(
                functools.partial(mend_and_send_kernel, line, units),
                [whole, sent_shape],
                turned,
                edges,
                raw,
                beyond,
                scaled,
                pins,
                scratch=[pltpu.VMEM(edge_shape, jnp.float32)],
            )
        else:
            (field,) = call(
                last_kernel,
                [whole],
                turned,
                edges,
                raw,
                beyond,
                written=HBM,
                scratch=[
                    pltpu.VMEM(whole, jnp.float32),
                    pltpu.VMEM(edge_shape, jnp.float32),
                    pltpu.SemaphoreType.DMA((planes,)),
                ],
            )
    return field


def solution(mesh):
    in_specs = (P(None, "gx", "gy", None), P(None, "gx", "gy", None), P(None, None, "gy", None))
    out_specs = P(None, "gx", "gy", None)
    return jax.shard_map(
        per_device, mesh=mesh, in_specs=in_specs, out_specs=out_specs, check_vma=False
    )
```

```python
import functools

import jax
import jax.numpy as jnp
import numpy as np
from jax import lax
from jax.experimental import pallas as pl
from jax.experimental.pallas import tpu as pltpu
from jax.sharding import PartitionSpec as P

STEPS = 2
LANES = 128
RHS = 6
COUPLED = 16

diffusion = 4000.0
anisotropy_rate = 0.3
torque_rate = 0.2
exchange_rate = 0.1
norm_floor = 0.5


class Line:
    def __init__(self, planes):
        leading = 1.0 + 2.0 * diffusion
        pivots = [leading]
        for _ in range(1, planes):
            pivots.append(leading - diffusion * diffusion / pivots[-1])
        self.planes = planes
        self.inverse_pivot = [1.0 / p for p in pivots]
        self.factor = [0.0] + [diffusion / p for p in pivots[:-1]]
        block = (
            leading * np.eye(planes)
            - diffusion * np.eye(planes, k=1)
            - diffusion * np.eye(planes, k=-1)
        )
        self.from_low = diffusion * np.linalg.inv(block)[:, 0]
        self.from_high = self.from_low[::-1]

    def sweep(self, source):
        carried = [source[0]]
        for i in range(1, len(source)):
            carried.append(source[i] + self.factor[i] * carried[-1])
        return carried

    def unwind(self, carried, meeting):
        solved = [None] * len(carried)
        solved[-1] = meeting
        for i in range(len(carried) - 2, -1, -1):
            solved[i] = carried[i] * self.inverse_pivot[i] + self.factor[i + 1] * solved[i + 1]
        return solved

    def solve(self, source):
        half = self.planes // 2
        low, high = self.sweep(source[:half]), self.sweep(source[half:][::-1])
        pivot_low = 1.0 / self.inverse_pivot[len(low) - 1]
        pivot_high = 1.0 / self.inverse_pivot[len(high) - 1]
        scale = 1.0 / (pivot_low * pivot_high - diffusion * diffusion)
        cross = diffusion * scale
        meeting_low = low[-1] * (pivot_high * scale) + high[-1] * cross
        meeting_high = high[-1] * (pivot_low * scale) + low[-1] * cross
        return self.unwind(low, meeting_low) + self.unwind(high, meeting_high)[::-1]

    def ends(self, source):
        found = []
        for weights in (self.from_low, self.from_high):
            total = source[0] * float(weights[0] / diffusion)
            for weight, value in zip(weights[1:], source[1:]):
                total = total + value * float(weight / diffusion)
            found.append(total)
        return found


class Level:
    def __init__(self, length, radix):
        self.radix = radix
        line = Line(length)
        near, far = line.from_low[0], line.from_low[-1]
        count = 2 * radix
        inside = np.kron(np.eye(radix), np.array([[near, far], [far, near]]))
        pick = np.zeros((count, count))
        for r in range(radix):
            if r > 0:
                pick[2 * r, 2 * r - 1] = 1.0
            if r < radix - 1:
                pick[2 * r + 1, 2 * r + 2] = 1.0
        outer = np.zeros((count, 2))
        outer[0, 0] = outer[count - 1, 1] = 1.0
        settle = np.linalg.inv(np.eye(count) - pick @ inside)
        self.ghosts = settle @ pick
        self.passed = settle @ outer
        ends = (np.eye(count) + inside @ self.ghosts)[[0, count - 1]]
        self.ends = ends


def radices_of(groups):
    found = []
    while groups > 1:
        radix = 4 if groups % 4 == 0 else 2
        assert groups % radix == 0
        found.append(radix)
        groups //= radix
    return found


def combine(weights, terms):
    total = None
    for weight, term in zip(weights, terms):
        if weight == 0.0 or term is None:
            continue
        part = term * float(weight)
        total = part if total is None else total + part
    return total


def make_levels(planes, groups):
    found = []
    for radix in radices_of(groups):
        found.append(Level(planes, radix))
        planes *= radix
    return found


def settle(levels, ends):
    level, count = levels[0], 2 * levels[0].radix
    if len(levels) == 1:
        return [combine(weights, ends) for weights in level.ghosts]
    joined = []
    for start in range(0, len(ends), count):
        part = ends[start : start + count]
        joined += [combine(weights, part) for weights in level.ends]
    outer = settle(levels[1:], joined)
    found = []
    for at, start in enumerate(range(0, len(ends), count)):
        part = list(ends[start : start + count]) + [outer[2 * at], outer[2 * at + 1]]
        for inside, passed in zip(level.ghosts, level.passed):
            found.append(combine(list(inside) + list(passed), part))
    return found


def plus(total, weight, term):
    return total if term is None else total + weight * term


def pieces(value, values, units, tile, rows):
    step = min(units, rows)
    for start in range(0, rows, step):
        at = tile * rows + start
        to = (at // units * values + value) * units + at % units
        yield slice(start, start + step), slice(to, to + step)


def pinned(source, pins_ref, component, lanes):
    position = lax.axis_index("gx")
    first = jnp.where(position == 0, diffusion, 0.0).astype(jnp.float32)
    last = jnp.where(position == lax.axis_size("gx") - 1, diffusion, 0.0).astype(jnp.float32)
    source[0] = source[0] + first * pins_ref[0, component, :, lanes]
    source[-1] = source[-1] + last * pins_ref[1, component, :, lanes]
    return source


def read_field(field_ref, lanes):
    planes = field_ref.shape[1]
    return [[field_ref[c, i, :, lanes] for i in range(planes)] for c in range(3)]


def solve_components(line, field, axes_ref, pins_ref, lanes, ghosts):
    planes = line.planes
    field = list(field)
    axes = [[axes_ref[c, i, :, lanes] for i in range(planes)] for c in range(3)]
    for component in range(3):
        source = []
        for i in range(planes):
            projection = (
                field[0][i] * axes[0][i] + field[1][i] * axes[1][i] + field[2][i] * axes[2][i]
            )
            source.append(
                field[component][i] + (anisotropy_rate * projection) * axes[component][i]
            )
        source = pinned(source, pins_ref, component, lanes)
        if ghosts is not None:
            source[0] = source[0] + diffusion * ghosts[component][0]
            source[-1] = source[-1] + diffusion * ghosts[component][1]
        if ghosts is None and component == 2:
            return field[:2] + [line.ends(source)]
        field[component] = line.solve(source)
    return field


def couplings(line, axes_ref, lanes):
    planes = line.planes
    low, high = line.from_low, line.from_high
    axes = [[axes_ref[c, i, :, lanes] for i in range(planes)] for c in range(3)]
    scaled = [anisotropy_rate * a for a in axes[1]]
    first_second = [axes[0][i] * scaled[i] for i in range(planes)]
    second_third = [axes[2][i] * scaled[i] for i in range(planes)]
    first_third = [(anisotropy_rate * axes[0][i]) * axes[2][i] for i in range(planes)]

    def weighted(terms, weights):
        total = terms[0] * float(weights[0] / diffusion)
        for i in range(1, planes):
            total = total + terms[i] * float(weights[i] / diffusion)
        return total

    found = []
    for product in (first_second, second_third):
        for weights in (low * low, low * high, high * high):
            found.append(weighted(product, weights))
    for ghost in (low, high):
        moved = line.solve([first_second[i] * float(ghost[i]) for i in range(planes)])
        pushed = [
            second_third[i] * moved[i] + first_third[i] * float(ghost[i]) for i in range(planes)
        ]
        found.append(weighted(pushed, low))
        found.append(weighted(pushed, high))
    return found


def send_tile(line, units, values, field, axes_ref, pins_ref, out_ref, tile):
    rows = axes_ref.shape[2]
    lanes = slice(tile * LANES, (tile + 1) * LANES)
    solved = solve_components(line, field, axes_ref, pins_ref, lanes, None)
    for component in range(3):
        for side, end in enumerate((0, -1)):
            value = 2 * component + side
            for source, target in pieces(value, values, units, tile, rows):
                out_ref[target, :] = solved[component][end][source]


def coupling_kernel(line, units, axes_ref, out_ref):
    rows, width = axes_ref.shape[2:]
    tiles = width // LANES
    for tile in range(tiles):
        found = couplings(line, axes_ref, slice(tile * LANES, (tile + 1) * LANES))
        for value, one in enumerate(found):
            for source, target in pieces(value, COUPLED - RHS, units, tile, rows):
                out_ref[target, :] = one[source]


def first_kernel(line, groups, units, coupling_ref, field_ref, axes_ref, pins_ref, out_ref):
    extra = (COUPLED - RHS) * units
    for d in range(groups):
        start = (d * COUPLED + RHS) * units
        out_ref[start : start + extra, :] = coupling_ref[d * extra : (d + 1) * extra, :]
    for tile in range(field_ref.shape[3] // LANES):
        field = read_field(field_ref, slice(tile * LANES, (tile + 1) * LANES))
        send_tile(line, units, COUPLED, field, axes_ref, pins_ref, out_ref, tile)


def solve_children(level, levels, rhs, coupling, outer):
    def ghosts(ends, component):
        found = settle(levels, ends)
        if outer is None:
            return found
        low, high = outer[component]
        moved = []
        for ghost, passed in zip(found, level.passed):
            terms = combine(passed, [low, high])
            moved.append(terms if ghost is None else ghost if terms is None else ghost + terms)
        return moved

    first = ghosts(rhs[0], 0)
    middle = []
    for d in range(level.radix):
        c, low, high = coupling[d], first[2 * d], first[2 * d + 1]
        middle.append(plus(plus(rhs[1][2 * d], c[0], low), c[1], high))
        middle.append(plus(plus(rhs[1][2 * d + 1], c[1], low), c[2], high))
    second = ghosts(middle, 1)
    last = []
    for d in range(level.radix):
        c, low1, high1 = coupling[d], first[2 * d], first[2 * d + 1]
        low2, high2 = second[2 * d], second[2 * d + 1]
        total = plus(plus(rhs[2][2 * d], c[3], low2), c[4], high2)
        last.append(plus(plus(total, c[6], low1), c[8], high1))
        total = plus(plus(rhs[2][2 * d + 1], c[4], low2), c[5], high2)
        last.append(plus(plus(total, c[7], low1), c[9], high1))
    return (first, second, ghosts(last, 2)), (rhs[0], middle, last)


def facing_coupling(level, levels, coupling, side):
    passed = level.passed[:, side]
    moved2, moved3 = [], []
    for r in range(level.radix):
        c, low, high = coupling[r], float(passed[2 * r]), float(passed[2 * r + 1])
        moved2 += [c[0] * low + c[1] * high, c[1] * low + c[2] * high]
        moved3 += [c[3] * low + c[4] * high, c[4] * low + c[5] * high]
    inner = settle(levels, moved2)
    through = []
    for r in range(level.radix):
        c, low, high = coupling[r], float(passed[2 * r]), float(passed[2 * r + 1])
        k_low, k_high = inner[2 * r], inner[2 * r + 1]
        total = plus(c[6] * low + c[8] * high, c[3], k_low)
        through.append(plus(total, c[4], k_high))
        total = plus(c[7] * low + c[9] * high, c[4], k_low)
        through.append(plus(total, c[5], k_high))
    return [combine(level.ends[side], moved) for moved in (moved2, moved3, through)]


def read_children(level, units, rhs_values, rhs_ref, coupling_ref):
    def read(ref, values, d, value):
        start = (d * values + value) * units
        return ref[start : start + units, :]

    rhs = [
        [read(rhs_ref, rhs_values, k // 2, 2 * c + k % 2) for k in range(2 * level.radix)]
        for c in range(3)
    ]
    coupling = [
        [read(coupling_ref, COUPLED, d, v) for v in range(RHS, COUPLED)]
        for d in range(level.radix)
    ]
    return rhs, coupling


def join_kernel(level, levels, units, coupled, rhs_ref, coupling_ref, out_ref):
    upper = lax.axis_index("gx") >= level.radix
    values = COUPLED if coupled else RHS
    rhs, coupling = read_children(level, units, values, rhs_ref, coupling_ref)
    _, seen = solve_children(level, levels, rhs, coupling, None)
    ends = [[combine(level.ends[side], seen[c]) for c in range(3)] for side in range(2)]
    if coupled:
        for side in range(2):
            ends[side] += facing_coupling(level, levels, coupling, side)
    for value, (first, last) in enumerate(zip(*ends)):
        out_ref[value * units : (value + 1) * units, :] = jnp.where(upper, first, last)


def part_kernel(
    level,
    levels,
    near,
    units,
    coupled,
    own_ref,
    other_ref,
    own_coupling_ref,
    other_coupling_ref,
    rhs_ref,
    coupling_ref,
    out_ref,
):
    upper = lax.axis_index("gx") >= level.radix

    def read(ref, value):
        return ref[value * units : (value + 1) * units, :]

    settled = 1.0 / (1.0 - near * near)

    def meet(own, other):
        beyond = other * settled + own * (near * settled)
        return beyond, own * settled + other * (near * settled)

    own = [read(own_ref, c) for c in range(3)]
    other = [read(other_ref, c) for c in range(3)]
    own_c = [read(own_coupling_ref, 3 + v) for v in range(3)]
    other_c = [read(other_coupling_ref, 3 + v) for v in range(3)]
    beyond1, back1 = meet(own[0], other[0])
    beyond2, back2 = meet(own[1] + own_c[0] * beyond1, other[1] + other_c[0] * back1)
    beyond3, _ = meet(
        own[2] + own_c[1] * beyond2 + own_c[2] * beyond1,
        other[2] + other_c[1] * back2 + other_c[2] * back1,
    )
    outer = [
        [jnp.where(upper, beyond, 0.0), jnp.where(upper, 0.0, beyond)]
        for beyond in (beyond1, beyond2, beyond3)
    ]
    values = COUPLED if coupled else RHS
    rhs, coupling = read_children(level, units, values, rhs_ref, coupling_ref)
    found, _ = solve_children(level, levels, rhs, coupling, outer)
    for c, ghosts in enumerate(found):
        for k, ghost in enumerate(ghosts):
            start = (k // 2 * RHS + 2 * c + k % 2) * units
            out_ref[start : start + units, :] = ghost


def finish_kernel(line, units, field_ref, axes_ref, pins_ref, ghost_ref, out_ref, edge_ref):
    planes = line.planes
    rows, width = field_ref.shape[2], field_ref.shape[3]
    tiles = width // LANES
    for tile in range(tiles):
        lanes = slice(tile * LANES, (tile + 1) * LANES)
        ghosts = [
            [
                jnp.concatenate(
                    [
                        ghost_ref[target, :]
                        for _, target in pieces(2 * c + side, RHS, units, tile, rows)
                    ],
                    axis=0,
                )
                for side in range(2)
            ]
            for c in range(3)
        ]
        field = read_field(field_ref, lanes)
        solved = solve_components(line, field, axes_ref, pins_ref, lanes, ghosts)
        for c in range(3):
            for i in range(planes):
                out_ref[c, i, :, lanes] = solved[c][i]
                at = c * planes + i
                edge_ref[0, at : at + 1, lanes] = solved[c][i][:1]
                edge_ref[1, at : at + 1, lanes] = solved[c][i][rows - 1 :]


def unit_scale(parts):
    square = parts[0] * parts[0] + parts[1] * parts[1] + parts[2] * parts[2]
    return jnp.minimum(lax.rsqrt(square), 1.0 / norm_floor)


def turn_kernel(field_ref, axes_ref, out_ref, raw_ref):
    planes, rows, width = field_ref.shape[1:]
    row = lax.broadcasted_iota(jnp.int32, (rows, width), 0)
    for i in range(planes):
        field = [field_ref[c, i] for c in range(3)]
        axes = [axes_ref[c, i] for c in range(3)]
        projection = field[0] * axes[0] + field[1] * axes[1] + field[2] * axes[2]
        effective = []
        for c in range(3):
            below = jnp.where(row == 0, 0.0, pltpu.roll(field[c], 1, 0))
            above = jnp.where(row == rows - 1, 0.0, pltpu.roll(field[c], rows - 1, 0))
            beside = pltpu.roll(field[c], 1, 1) + pltpu.roll(field[c], width - 1, 1)
            effective.append(
                exchange_rate * (((above + below) + beside) - 4.0 * field[c])
                + projection * axes[c]
            )
        rotated = []
        for c in range(3):
            d, e = (c + 1) % 3, (c + 2) % 3
            twisted = field[d] * effective[e] - field[e] * effective[d]
            rotated.append(field[c] - torque_rate * twisted)
        scale = unit_scale(rotated)
        for c in range(3):
            at = c * planes + i
            out_ref[c, i] = rotated[c] * scale
            raw_ref[0, at : at + 1, :] = rotated[c][:1]
            raw_ref[1, at : at + 1, :] = rotated[c][rows - 1 :]


def mend_edges(edge_ref, raw_ref, beyond_ref, mended_ref):
    planes = edge_ref.shape[1] // 3
    for side in range(2):
        parts = [slice(c * planes, (c + 1) * planes) for c in range(3)]
        field = [edge_ref[side, part, :] for part in parts]
        beyond = [beyond_ref[1 - side, part, :] for part in parts]
        rotated = []
        for c in range(3):
            d, e = (c + 1) % 3, (c + 2) % 3
            twisted = field[d] * beyond[e] - field[e] * beyond[d]
            rotated.append(raw_ref[side, parts[c], :] - (torque_rate * exchange_rate) * twisted)
        scale = unit_scale(rotated)
        for c in range(3):
            mended_ref[side, parts[c], :] = rotated[c] * scale


def mended(turned, mended_ref, at, lanes):
    rows = turned.shape[0]
    row = lax.broadcasted_iota(jnp.int32, turned.shape, 0)
    turned = jnp.where(row == 0, mended_ref[0, at : at + 1, lanes], turned)
    return jnp.where(row == rows - 1, mended_ref[1, at : at + 1, lanes], turned)


def mend_and_send_kernel(
    line,
    units,
    turned_ref,
    edge_ref,
    raw_ref,
    beyond_ref,
    axes_ref,
    pins_ref,
    out_ref,
    sent_ref,
    mended_ref,
):
    planes = line.planes
    mend_edges(edge_ref, raw_ref, beyond_ref, mended_ref)
    for tile in range(turned_ref.shape[3] // LANES):
        lanes = slice(tile * LANES, (tile + 1) * LANES)
        field = read_field(turned_ref, lanes)
        for c in range(3):
            for i in range(planes):
                field[c][i] = mended(field[c][i], mended_ref, c * planes + i, lanes)
                out_ref[c, i, :, lanes] = field[c][i]
        send_tile(line, units, RHS, field, axes_ref, pins_ref, sent_ref, tile)


def last_kernel(turned_ref, edge_ref, raw_ref, beyond_ref, out_hbm, out_ref, mended_ref, sems):
    planes = turned_ref.shape[1]

    def copy(i):
        return pltpu.make_async_copy(out_ref.at[:, i], out_hbm.at[:, i], sems.at[i])

    mend_edges(edge_ref, raw_ref, beyond_ref, mended_ref)
    for i in range(planes):
        for c in range(3):
            out_ref[c, i] = mended(turned_ref[c, i], mended_ref, c * planes + i, slice(None))
        copy(i).start()
    for i in range(planes):
        copy(i).wait()


VMEM = pl.BlockSpec(memory_space=pltpu.VMEM)
HBM = pl.BlockSpec(memory_space=pltpu.HBM)
LIMIT = 32 * 1024 * 1024


def call(kernel, shapes, *operands, written=VMEM, scratch=()):
    shapes = [jax.ShapeDtypeStruct(shape, jnp.float32) for shape in shapes]
    return pl.pallas_call(
        kernel,
        out_shape=tuple(shapes),
        in_specs=[VMEM] * len(operands),
        out_specs=(written,) * len(shapes),
        scratch_shapes=scratch,
        compiler_params=pltpu.CompilerParams(vmem_limit_bytes=LIMIT),
    )(*operands)


def exchange(block, groups):
    parts = block.reshape(groups, -1, LANES)
    members = [
        list(range(start, start + groups)) for start in range(0, lax.axis_size("gx"), groups)
    ]
    return lax.all_to_all(
        parts, "gx", split_axis=0, concat_axis=0, axis_index_groups=members, tiled=True
    ).reshape(block.shape)


def swap_halves(block, groups):
    pairs = [(i, (i + groups) % (2 * groups)) for i in range(2 * groups)]
    return lax.ppermute(block, "gx", pairs)


def from_neighbours(edges):
    count = lax.axis_size("gy")
    forward = [(i, (i + 1) % count) for i in range(count)]
    if count == 2:
        return lax.ppermute(edges, "gy", forward)
    backward = [(target, source) for source, target in forward]
    return jnp.stack(
        [lax.ppermute(edges[0], "gy", backward), lax.ppermute(edges[1], "gy", forward)]
    )


def per_device(magnetization, easy_axes, pins):
    _, planes, rows, width = magnetization.shape
    groups = lax.axis_size("gx") // 2
    units = rows * (width // LANES) // groups
    line = Line(planes)
    levels = make_levels(planes, groups)
    level = Level(planes, groups)
    near = float(Line(planes * groups).from_low[0])
    whole = magnetization.shape
    sent_shape = (groups * RHS * units, LANES)
    edge_shape = (2, 3 * planes, width)

    field = magnetization
    (coupling,) = call(
        functools.partial(coupling_kernel, line, units),
        [(groups * (COUPLED - RHS) * units, LANES)],
        easy_axes,
    )
    (sent,) = call(
        functools.partial(first_kernel, line, groups, units),
        [(groups * COUPLED * units, LANES)],
        coupling,
        field,
        easy_axes,
        pins,
    )
    coupling = None
    for stepno in range(STEPS):
        gathered = exchange(sent, groups)
        coupled = stepno == 0
        if coupled:
            coupling = gathered
        (joined,) = call(
            functools.partial(join_kernel, level, levels, units, coupled),
            [((6 if coupled else 3) * units, LANES)],
            gathered,
            coupling,
        )
        swapped = swap_halves(joined, groups)
        if coupled:
            across = (joined, swapped)
        (ghosts,) = call(
            functools.partial(part_kernel, level, levels, near, units, coupled),
            [sent_shape],
            joined,
            swapped,
            *across,
            gathered,
            coupling,
        )
        ghosts = exchange(ghosts, groups)
        solved, edges = call(
            functools.partial(finish_kernel, line, units),
            [whole, edge_shape],
            field,
            easy_axes,
            pins,
            ghosts,
        )
        beyond = from_neighbours(edges)
        turned, raw = call(turn_kernel, [whole, edge_shape], solved, easy_axes)
        if stepno < STEPS - 1:
            field, sent = call(
                functools.partial(mend_and_send_kernel, line, units),
                [whole, sent_shape],
                turned,
                edges,
                raw,
                beyond,
                easy_axes,
                pins,
                scratch=[pltpu.VMEM(edge_shape, jnp.float32)],
            )
        else:
            (field,) = call(
                last_kernel,
                [whole],
                turned,
                edges,
                raw,
                beyond,
                written=HBM,
                scratch=[
                    pltpu.VMEM(whole, jnp.float32),
                    pltpu.VMEM(edge_shape, jnp.float32),
                    pltpu.SemaphoreType.DMA((planes,)),
                ],
            )
    return field


def solution(mesh):
    in_specs = (P(None, "gx", "gy", None), P(None, "gx", "gy", None), P(None, None, "gy", None))
    out_specs = P(None, "gx", "gy", None)
    return jax.shard_map(
        per_device, mesh=mesh, in_specs=in_specs, out_specs=out_specs, check_vma=False
    )
```

```python
import functools

import jax
import jax.numpy as jnp
import numpy as np
from jax import lax
from jax.experimental import pallas as pl
from jax.experimental.pallas import tpu as pltpu
from jax.sharding import PartitionSpec as P

STEPS = 2
LANES = 128
SUBLANES = 8
RHS = 6
COUPLED = 16

diffusion = 4000.0
anisotropy_rate = 0.3
torque_rate = 0.2
exchange_rate = 0.1
norm_floor = 0.5


class Line:
    def __init__(self, planes):
        leading = 1.0 + 2.0 * diffusion
        pivots = [leading]
        for _ in range(1, planes):
            pivots.append(leading - diffusion * diffusion / pivots[-1])
        self.planes = planes
        self.inverse_pivot = [1.0 / p for p in pivots]
        self.factor = [0.0] + [diffusion / p for p in pivots[:-1]]
        block = (
            leading * np.eye(planes)
            - diffusion * np.eye(planes, k=1)
            - diffusion * np.eye(planes, k=-1)
        )
        self.from_low = diffusion * np.linalg.inv(block)[:, 0]
        self.from_high = self.from_low[::-1]

    def sweep(self, source):
        carried = [source[0]]
        for i in range(1, len(source)):
            carried.append(source[i] + self.factor[i] * carried[-1])
        return carried

    def unwind(self, carried, meeting):
        solved = [None] * len(carried)
        solved[-1] = meeting
        for i in range(len(carried) - 2, -1, -1):
            solved[i] = carried[i] * self.inverse_pivot[i] + self.factor[i + 1] * solved[i + 1]
        return solved

    def solve(self, source):
        half = self.planes // 2
        low, high = self.sweep(source[:half]), self.sweep(source[half:][::-1])
        pivot_low = 1.0 / self.inverse_pivot[len(low) - 1]
        pivot_high = 1.0 / self.inverse_pivot[len(high) - 1]
        scale = 1.0 / (pivot_low * pivot_high - diffusion * diffusion)
        cross = diffusion * scale
        meeting_low = low[-1] * (pivot_high * scale) + high[-1] * cross
        meeting_high = high[-1] * (pivot_low * scale) + low[-1] * cross
        return self.unwind(low, meeting_low) + self.unwind(high, meeting_high)[::-1]

    def ends(self, source):
        found = []
        for weights in (self.from_low, self.from_high):
            total = source[0] * float(weights[0] / diffusion)
            for weight, value in zip(weights[1:], source[1:]):
                total = total + value * float(weight / diffusion)
            found.append(total)
        return found


class Level:
    def __init__(self, length, radix):
        self.radix = radix
        line = Line(length)
        near, far = line.from_low[0], line.from_low[-1]
        count = 2 * radix
        inside = np.kron(np.eye(radix), np.array([[near, far], [far, near]]))
        pick = np.zeros((count, count))
        for r in range(radix):
            if r > 0:
                pick[2 * r, 2 * r - 1] = 1.0
            if r < radix - 1:
                pick[2 * r + 1, 2 * r + 2] = 1.0
        outer = np.zeros((count, 2))
        outer[0, 0] = outer[count - 1, 1] = 1.0
        settle = np.linalg.inv(np.eye(count) - pick @ inside)
        self.ghosts = settle @ pick
        self.passed = settle @ outer
        ends = (np.eye(count) + inside @ self.ghosts)[[0, count - 1]]
        self.ends = ends


def radices_of(groups):
    found = []
    while groups > 1:
        radix = 4 if groups % 4 == 0 else 2
        assert groups % radix == 0
        found.append(radix)
        groups //= radix
    return found


def combine(weights, terms):
    total = None
    for weight, term in zip(weights, terms):
        if weight == 0.0 or term is None:
            continue
        part = term * float(weight)
        total = part if total is None else total + part
    return total


def make_levels(planes, groups):
    found = []
    for radix in radices_of(groups):
        found.append(Level(planes, radix))
        planes *= radix
    return found


def settle(levels, ends):
    level, count = levels[0], 2 * levels[0].radix
    if len(levels) == 1:
        return [combine(weights, ends) for weights in level.ghosts]
    joined = []
    for start in range(0, len(ends), count):
        part = ends[start : start + count]
        joined += [combine(weights, part) for weights in level.ends]
    outer = settle(levels[1:], joined)
    found = []
    for at, start in enumerate(range(0, len(ends), count)):
        part = list(ends[start : start + count]) + [outer[2 * at], outer[2 * at + 1]]
        for inside, passed in zip(level.ghosts, level.passed):
            found.append(combine(list(inside) + list(passed), part))
    return found


def plus(total, weight, term):
    return total if term is None else total + weight * term


def tiles_of(shape):
    rows, width = shape[-2:]
    band = SUBLANES if rows % SUBLANES == 0 else rows
    for tile in range(width // LANES):
        for row in range(0, rows, band):
            yield tile, slice(row, row + band), slice(tile * LANES, (tile + 1) * LANES)


def pieces(value, values, units, tile, band, rows):
    count = band.stop - band.start
    step = min(units, count)
    for start in range(0, count, step):
        at = tile * rows + band.start + start
        to = (at // units * values + value) * units + at % units
        yield slice(start, start + step), slice(to, to + step)


def pinned(source, pins_ref, component, band, lanes):
    position = lax.axis_index("gx")
    first = jnp.where(position == 0, diffusion, 0.0).astype(jnp.float32)
    last = jnp.where(position == lax.axis_size("gx") - 1, diffusion, 0.0).astype(jnp.float32)
    source[0] = source[0] + first * pins_ref[0, component, band, lanes]
    source[-1] = source[-1] + last * pins_ref[1, component, band, lanes]
    return source


def read_field(field_ref, band, lanes):
    planes = field_ref.shape[1]
    return [[field_ref[c, i, band, lanes] for i in range(planes)] for c in range(3)]


def solve_components(line, field, axes_ref, pins_ref, band, lanes, ghosts):
    planes = line.planes
    field = list(field)
    axes = [[axes_ref[c, i, band, lanes] for i in range(planes)] for c in range(3)]
    for component in range(3):
        source = []
        for i in range(planes):
            projection = (
                field[0][i] * axes[0][i] + field[1][i] * axes[1][i] + field[2][i] * axes[2][i]
            )
            source.append(
                field[component][i] + (anisotropy_rate * projection) * axes[component][i]
            )
        source = pinned(source, pins_ref, component, band, lanes)
        if ghosts is not None:
            source[0] = source[0] + diffusion * ghosts[component][0]
            source[-1] = source[-1] + diffusion * ghosts[component][1]
        if ghosts is None and component == 2:
            return field[:2] + [line.ends(source)]
        field[component] = line.solve(source)
    return field


def couplings(line, axes_ref, band, lanes):
    planes = line.planes
    low, high = line.from_low, line.from_high
    axes = [[axes_ref[c, i, band, lanes] for i in range(planes)] for c in range(3)]
    scaled = [anisotropy_rate * a for a in axes[1]]
    first_second = [axes[0][i] * scaled[i] for i in range(planes)]
    second_third = [axes[2][i] * scaled[i] for i in range(planes)]
    first_third = [(anisotropy_rate * axes[0][i]) * axes[2][i] for i in range(planes)]

    def weighted(terms, weights):
        total = terms[0] * float(weights[0] / diffusion)
        for i in range(1, planes):
            total = total + terms[i] * float(weights[i] / diffusion)
        return total

    found = []
    for product in (first_second, second_third):
        for weights in (low * low, low * high, high * high):
            found.append(weighted(product, weights))
    for ghost in (low, high):
        moved = line.solve([first_second[i] * float(ghost[i]) for i in range(planes)])
        pushed = [
            second_third[i] * moved[i] + first_third[i] * float(ghost[i]) for i in range(planes)
        ]
        found.append(weighted(pushed, low))
        found.append(weighted(pushed, high))
    return found


def send_tile(line, units, values, field, axes_ref, pins_ref, out_ref, tile, band, lanes):
    rows = axes_ref.shape[2]
    solved = solve_components(line, field, axes_ref, pins_ref, band, lanes, None)
    for component in range(3):
        for side, end in enumerate((0, -1)):
            value = 2 * component + side
            for source, target in pieces(value, values, units, tile, band, rows):
                out_ref[target, :] = solved[component][end][source]


def coupling_kernel(line, units, axes_ref, out_ref):
    rows = axes_ref.shape[2]
    for tile, band, lanes in tiles_of(axes_ref.shape):
        for value, one in enumerate(couplings(line, axes_ref, band, lanes)):
            for source, target in pieces(value, COUPLED - RHS, units, tile, band, rows):
                out_ref[target, :] = one[source]


def first_kernel(line, groups, units, coupling_ref, field_ref, axes_ref, pins_ref, out_ref):
    extra = (COUPLED - RHS) * units
    for d in range(groups):
        start = (d * COUPLED + RHS) * units
        out_ref[start : start + extra, :] = coupling_ref[d * extra : (d + 1) * extra, :]
    for tile, band, lanes in tiles_of(field_ref.shape):
        field = read_field(field_ref, band, lanes)
        send_tile(line, units, COUPLED, field, axes_ref, pins_ref, out_ref, tile, band, lanes)


def solve_children(level, levels, rhs, coupling, outer):
    def ghosts(ends, component):
        found = settle(levels, ends)
        if outer is None:
            return found
        low, high = outer[component]
        moved = []
        for ghost, passed in zip(found, level.passed):
            terms = combine(passed, [low, high])
            moved.append(terms if ghost is None else ghost if terms is None else ghost + terms)
        return moved

    first = ghosts(rhs[0], 0)
    middle = []
    for d in range(level.radix):
        c, low, high = coupling[d], first[2 * d], first[2 * d + 1]
        middle.append(plus(plus(rhs[1][2 * d], c[0], low), c[1], high))
        middle.append(plus(plus(rhs[1][2 * d + 1], c[1], low), c[2], high))
    second = ghosts(middle, 1)
    last = []
    for d in range(level.radix):
        c, low1, high1 = coupling[d], first[2 * d], first[2 * d + 1]
        low2, high2 = second[2 * d], second[2 * d + 1]
        total = plus(plus(rhs[2][2 * d], c[3], low2), c[4], high2)
        last.append(plus(plus(total, c[6], low1), c[8], high1))
        total = plus(plus(rhs[2][2 * d + 1], c[4], low2), c[5], high2)
        last.append(plus(plus(total, c[7], low1), c[9], high1))
    return (first, second, ghosts(last, 2)), (rhs[0], middle, last)


def facing_coupling(level, levels, coupling, side):
    passed = level.passed[:, side]
    moved2, moved3 = [], []
    for r in range(level.radix):
        c, low, high = coupling[r], float(passed[2 * r]), float(passed[2 * r + 1])
        moved2 += [c[0] * low + c[1] * high, c[1] * low + c[2] * high]
        moved3 += [c[3] * low + c[4] * high, c[4] * low + c[5] * high]
    inner = settle(levels, moved2)
    through = []
    for r in range(level.radix):
        c, low, high = coupling[r], float(passed[2 * r]), float(passed[2 * r + 1])
        k_low, k_high = inner[2 * r], inner[2 * r + 1]
        total = plus(c[6] * low + c[8] * high, c[3], k_low)
        through.append(plus(total, c[4], k_high))
        total = plus(c[7] * low + c[9] * high, c[4], k_low)
        through.append(plus(total, c[5], k_high))
    return [combine(level.ends[side], moved) for moved in (moved2, moved3, through)]


def read_children(level, units, rhs_values, rhs_ref, coupling_ref):
    def read(ref, values, d, value):
        start = (d * values + value) * units
        return ref[start : start + units, :]

    rhs = [
        [read(rhs_ref, rhs_values, k // 2, 2 * c + k % 2) for k in range(2 * level.radix)]
        for c in range(3)
    ]
    coupling = [
        [read(coupling_ref, COUPLED, d, v) for v in range(RHS, COUPLED)]
        for d in range(level.radix)
    ]
    return rhs, coupling


def join_kernel(level, levels, units, coupled, rhs_ref, coupling_ref, out_ref):
    upper = lax.axis_index("gx") >= level.radix
    values = COUPLED if coupled else RHS
    rhs, coupling = read_children(level, units, values, rhs_ref, coupling_ref)
    _, seen = solve_children(level, levels, rhs, coupling, None)
    ends = [[combine(level.ends[side], seen[c]) for c in range(3)] for side in range(2)]
    if coupled:
        for side in range(2):
            ends[side] += facing_coupling(level, levels, coupling, side)
    for value, (first, last) in enumerate(zip(*ends)):
        out_ref[value * units : (value + 1) * units, :] = jnp.where(upper, first, last)


def part_kernel(
    level,
    levels,
    near,
    units,
    coupled,
    own_ref,
    other_ref,
    own_coupling_ref,
    other_coupling_ref,
    rhs_ref,
    coupling_ref,
    out_ref,
):
    upper = lax.axis_index("gx") >= level.radix

    def read(ref, value):
        return ref[value * units : (value + 1) * units, :]

    settled = 1.0 / (1.0 - near * near)

    def meet(own, other):
        beyond = other * settled + own * (near * settled)
        return beyond, own * settled + other * (near * settled)

    own = [read(own_ref, c) for c in range(3)]
    other = [read(other_ref, c) for c in range(3)]
    own_c = [read(own_coupling_ref, 3 + v) for v in range(3)]
    other_c = [read(other_coupling_ref, 3 + v) for v in range(3)]
    beyond1, back1 = meet(own[0], other[0])
    beyond2, back2 = meet(own[1] + own_c[0] * beyond1, other[1] + other_c[0] * back1)
    beyond3, _ = meet(
        own[2] + own_c[1] * beyond2 + own_c[2] * beyond1,
        other[2] + other_c[1] * back2 + other_c[2] * back1,
    )
    outer = [
        [jnp.where(upper, beyond, 0.0), jnp.where(upper, 0.0, beyond)]
        for beyond in (beyond1, beyond2, beyond3)
    ]
    values = COUPLED if coupled else RHS
    rhs, coupling = read_children(level, units, values, rhs_ref, coupling_ref)
    found, _ = solve_children(level, levels, rhs, coupling, outer)
    for c, ghosts in enumerate(found):
        for k, ghost in enumerate(ghosts):
            start = (k // 2 * RHS + 2 * c + k % 2) * units
            out_ref[start : start + units, :] = ghost


def finish_kernel(line, units, field_ref, axes_ref, pins_ref, ghost_ref, out_ref, edge_ref):
    planes, rows = line.planes, field_ref.shape[2]

    def ghost(value, tile, band):
        parts = [ghost_ref[at, :] for _, at in pieces(value, RHS, units, tile, band, rows)]
        return jnp.concatenate(parts, axis=0) if len(parts) > 1 else parts[0]

    for tile, band, lanes in tiles_of(field_ref.shape):
        ghosts = [[ghost(2 * c + side, tile, band) for side in range(2)] for c in range(3)]
        field = read_field(field_ref, band, lanes)
        solved = solve_components(line, field, axes_ref, pins_ref, band, lanes, ghosts)
        for c in range(3):
            for i in range(planes):
                at = c * planes + i
                out_ref[c, i, band, lanes] = solved[c][i]
                if band.start == 0:
                    edge_ref[0, at : at + 1, lanes] = solved[c][i][:1]
                if band.stop == rows:
                    edge_ref[1, at : at + 1, lanes] = solved[c][i][-1:]


def unit_scale(parts):
    square = parts[0] * parts[0] + parts[1] * parts[1] + parts[2] * parts[2]
    return jnp.minimum(lax.rsqrt(square), 1.0 / norm_floor)


def turn_kernel(field_ref, axes_ref, out_ref, raw_ref):
    planes, rows, width = field_ref.shape[1:]
    row = lax.broadcasted_iota(jnp.int32, (rows, width), 0)
    for i in range(planes):
        field = [field_ref[c, i] for c in range(3)]
        axes = [axes_ref[c, i] for c in range(3)]
        projection = field[0] * axes[0] + field[1] * axes[1] + field[2] * axes[2]
        effective = []
        for c in range(3):
            below = jnp.where(row == 0, 0.0, pltpu.roll(field[c], 1, 0))
            above = jnp.where(row == rows - 1, 0.0, pltpu.roll(field[c], rows - 1, 0))
            beside = pltpu.roll(field[c], 1, 1) + pltpu.roll(field[c], width - 1, 1)
            effective.append(
                exchange_rate * (((above + below) + beside) - 4.0 * field[c])
                + projection * axes[c]
            )
        rotated = []
        for c in range(3):
            d, e = (c + 1) % 3, (c + 2) % 3
            twisted = field[d] * effective[e] - field[e] * effective[d]
            rotated.append(field[c] - torque_rate * twisted)
        scale = unit_scale(rotated)
        for c in range(3):
            at = c * planes + i
            out_ref[c, i] = rotated[c] * scale
            raw_ref[0, at : at + 1, :] = rotated[c][:1]
            raw_ref[1, at : at + 1, :] = rotated[c][rows - 1 :]


def mend_edges(edge_ref, raw_ref, beyond_ref, mended_ref):
    planes = edge_ref.shape[1] // 3
    for side in range(2):
        parts = [slice(c * planes, (c + 1) * planes) for c in range(3)]
        field = [edge_ref[side, part, :] for part in parts]
        beyond = [beyond_ref[1 - side, part, :] for part in parts]
        rotated = []
        for c in range(3):
            d, e = (c + 1) % 3, (c + 2) % 3
            twisted = field[d] * beyond[e] - field[e] * beyond[d]
            rotated.append(raw_ref[side, parts[c], :] - (torque_rate * exchange_rate) * twisted)
        scale = unit_scale(rotated)
        for c in range(3):
            mended_ref[side, parts[c], :] = rotated[c] * scale


def mended(turned, mended_ref, at, band, rows, lanes):
    row = lax.broadcasted_iota(jnp.int32, turned.shape, 0)
    if band.start == 0:
        turned = jnp.where(row == 0, mended_ref[0, at : at + 1, lanes], turned)
    if band.stop == rows:
        last = row == turned.shape[0] - 1
        turned = jnp.where(last, mended_ref[1, at : at + 1, lanes], turned)
    return turned


def mend_and_send_kernel(
    line,
    units,
    turned_ref,
    edge_ref,
    raw_ref,
    beyond_ref,
    axes_ref,
    pins_ref,
    out_ref,
    sent_ref,
    mended_ref,
):
    planes = line.planes
    mend_edges(edge_ref, raw_ref, beyond_ref, mended_ref)
    rows = turned_ref.shape[2]
    for tile, band, lanes in tiles_of(turned_ref.shape):
        field = read_field(turned_ref, band, lanes)
        for c in range(3):
            for i in range(planes):
                at = c * planes + i
                field[c][i] = mended(field[c][i], mended_ref, at, band, rows, lanes)
                out_ref[c, i, band, lanes] = field[c][i]
        send_tile(line, units, RHS, field, axes_ref, pins_ref, sent_ref, tile, band, lanes)


def last_kernel(turned_ref, edge_ref, raw_ref, beyond_ref, out_hbm, out_ref, mended_ref, sems):
    planes, rows = turned_ref.shape[1:3]
    whole = slice(0, rows)

    def copy(i):
        return pltpu.make_async_copy(out_ref.at[:, i], out_hbm.at[:, i], sems.at[i])

    mend_edges(edge_ref, raw_ref, beyond_ref, mended_ref)
    for i in range(planes):
        for c in range(3):
            at = c * planes + i
            out_ref[c, i] = mended(turned_ref[c, i], mended_ref, at, whole, rows, slice(None))
        copy(i).start()
    for i in range(planes):
        copy(i).wait()


VMEM = pl.BlockSpec(memory_space=pltpu.VMEM)
HBM = pl.BlockSpec(memory_space=pltpu.HBM)
LIMIT = 32 * 1024 * 1024


def call(kernel, shapes, *operands, written=VMEM, scratch=()):
    shapes = [jax.ShapeDtypeStruct(shape, jnp.float32) for shape in shapes]
    return pl.pallas_call(
        kernel,
        out_shape=tuple(shapes),
        in_specs=[VMEM] * len(operands),
        out_specs=(written,) * len(shapes),
        scratch_shapes=scratch,
        compiler_params=pltpu.CompilerParams(vmem_limit_bytes=LIMIT),
    )(*operands)


def exchange(block, groups):
    parts = block.reshape(groups, -1, LANES)
    members = [
        list(range(start, start + groups)) for start in range(0, lax.axis_size("gx"), groups)
    ]
    return lax.all_to_all(
        parts, "gx", split_axis=0, concat_axis=0, axis_index_groups=members, tiled=True
    ).reshape(block.shape)


def swap_halves(block, groups):
    pairs = [(i, (i + groups) % (2 * groups)) for i in range(2 * groups)]
    return lax.ppermute(block, "gx", pairs)


def from_neighbours(edges):
    count = lax.axis_size("gy")
    forward = [(i, (i + 1) % count) for i in range(count)]
    if count == 2:
        return lax.ppermute(edges, "gy", forward)
    backward = [(target, source) for source, target in forward]
    return jnp.stack(
        [lax.ppermute(edges[0], "gy", backward), lax.ppermute(edges[1], "gy", forward)]
    )


def per_device(magnetization, easy_axes, pins):
    _, planes, rows, width = magnetization.shape
    groups = lax.axis_size("gx") // 2
    units = rows * (width // LANES) // groups
    line = Line(planes)
    levels = make_levels(planes, groups)
    level = Level(planes, groups)
    near = float(Line(planes * groups).from_low[0])
    whole = magnetization.shape
    sent_shape = (groups * RHS * units, LANES)
    edge_shape = (2, 3 * planes, width)

    field = magnetization
    (coupling,) = call(
        functools.partial(coupling_kernel, line, units),
        [(groups * (COUPLED - RHS) * units, LANES)],
        easy_axes,
    )
    (sent,) = call(
        functools.partial(first_kernel, line, groups, units),
        [(groups * COUPLED * units, LANES)],
        coupling,
        field,
        easy_axes,
        pins,
    )
    coupling = None
    for stepno in range(STEPS):
        gathered = exchange(sent, groups)
        coupled = stepno == 0
        if coupled:
            coupling = gathered
        (joined,) = call(
            functools.partial(join_kernel, level, levels, units, coupled),
            [((6 if coupled else 3) * units, LANES)],
            gathered,
            coupling,
        )
        swapped = swap_halves(joined, groups)
        if coupled:
            across = (joined, swapped)
        (ghosts,) = call(
            functools.partial(part_kernel, level, levels, near, units, coupled),
            [sent_shape],
            joined,
            swapped,
            *across,
            gathered,
            coupling,
        )
        ghosts = exchange(ghosts, groups)
        solved, edges = call(
            functools.partial(finish_kernel, line, units),
            [whole, edge_shape],
            field,
            easy_axes,
            pins,
            ghosts,
        )
        beyond = from_neighbours(edges)
        turned, raw = call(turn_kernel, [whole, edge_shape], solved, easy_axes)
        if stepno < STEPS - 1:
            field, sent = call(
                functools.partial(mend_and_send_kernel, line, units),
                [whole, sent_shape],
                turned,
                edges,
                raw,
                beyond,
                easy_axes,
                pins,
                scratch=[pltpu.VMEM(edge_shape, jnp.float32)],
            )
        else:
            (field,) = call(
                last_kernel,
                [whole],
                turned,
                edges,
                raw,
                beyond,
                written=HBM,
                scratch=[
                    pltpu.VMEM(whole, jnp.float32),
                    pltpu.VMEM(edge_shape, jnp.float32),
                    pltpu.SemaphoreType.DMA((planes,)),
                ],
            )
    return field


def solution(mesh):
    in_specs = (P(None, "gx", "gy", None), P(None, "gx", "gy", None), P(None, None, "gy", None))
    out_specs = P(None, "gx", "gy", None)
    return jax.shard_map(
        per_device, mesh=mesh, in_specs=in_specs, out_specs=out_specs, check_vma=False
    )
```

```python
import functools

import jax
import jax.numpy as jnp
import numpy as np
from jax import lax
from jax.experimental import pallas as pl
from jax.experimental.pallas import tpu as pltpu
from jax.sharding import PartitionSpec as P

STEPS = 2
LANES = 128
SUBLANES = 8
RHS = 6
COUPLED = 16

diffusion = 4000.0
anisotropy_rate = 0.3
torque_rate = 0.2
exchange_rate = 0.1
norm_floor = 0.5


class Line:
    def __init__(self, planes):
        leading = 1.0 + 2.0 * diffusion
        pivots = [leading]
        for _ in range(1, planes):
            pivots.append(leading - diffusion * diffusion / pivots[-1])
        self.planes = planes
        self.inverse_pivot = [1.0 / p for p in pivots]
        self.factor = [0.0] + [diffusion / p for p in pivots[:-1]]
        block = (
            leading * np.eye(planes)
            - diffusion * np.eye(planes, k=1)
            - diffusion * np.eye(planes, k=-1)
        )
        self.from_low = diffusion * np.linalg.inv(block)[:, 0]
        self.from_high = self.from_low[::-1]

    def sweep(self, source):
        carried = [source[0]]
        for i in range(1, len(source)):
            carried.append(source[i] + self.factor[i] * carried[-1])
        return carried

    def unwind(self, carried, meeting):
        solved = [None] * len(carried)
        solved[-1] = meeting
        for i in range(len(carried) - 2, -1, -1):
            solved[i] = carried[i] * self.inverse_pivot[i] + self.factor[i + 1] * solved[i + 1]
        return solved

    def solve(self, source):
        half = self.planes // 2
        low, high = self.sweep(source[:half]), self.sweep(source[half:][::-1])
        pivot_low = 1.0 / self.inverse_pivot[len(low) - 1]
        pivot_high = 1.0 / self.inverse_pivot[len(high) - 1]
        scale = 1.0 / (pivot_low * pivot_high - diffusion * diffusion)
        cross = diffusion * scale
        meeting_low = low[-1] * (pivot_high * scale) + high[-1] * cross
        meeting_high = high[-1] * (pivot_low * scale) + low[-1] * cross
        return self.unwind(low, meeting_low) + self.unwind(high, meeting_high)[::-1]

    def ends(self, source):
        found = []
        for weights in (self.from_low, self.from_high):
            total = source[0] * float(weights[0] / diffusion)
            for weight, value in zip(weights[1:], source[1:]):
                total = total + value * float(weight / diffusion)
            found.append(total)
        return found


class Level:
    def __init__(self, length, radix):
        self.radix = radix
        line = Line(length)
        near, far = line.from_low[0], line.from_low[-1]
        count = 2 * radix
        inside = np.kron(np.eye(radix), np.array([[near, far], [far, near]]))
        pick = np.zeros((count, count))
        for r in range(radix):
            if r > 0:
                pick[2 * r, 2 * r - 1] = 1.0
            if r < radix - 1:
                pick[2 * r + 1, 2 * r + 2] = 1.0
        outer = np.zeros((count, 2))
        outer[0, 0] = outer[count - 1, 1] = 1.0
        settle = np.linalg.inv(np.eye(count) - pick @ inside)
        self.ghosts = settle @ pick
        self.passed = settle @ outer
        ends = (np.eye(count) + inside @ self.ghosts)[[0, count - 1]]
        self.ends = ends


def radices_of(groups):
    found = []
    while groups > 1:
        radix = 4 if groups % 4 == 0 else 2
        assert groups % radix == 0
        found.append(radix)
        groups //= radix
    return found


def combine(weights, terms):
    total = None
    for weight, term in zip(weights, terms):
        if weight == 0.0 or term is None:
            continue
        part = term * float(weight)
        total = part if total is None else total + part
    return total


def make_levels(planes, groups):
    found = []
    for radix in radices_of(groups):
        found.append(Level(planes, radix))
        planes *= radix
    return found


def settle(levels, ends):
    level, count = levels[0], 2 * levels[0].radix
    if len(levels) == 1:
        return [combine(weights, ends) for weights in level.ghosts]
    joined = []
    for start in range(0, len(ends), count):
        part = ends[start : start + count]
        joined += [combine(weights, part) for weights in level.ends]
    outer = settle(levels[1:], joined)
    found = []
    for at, start in enumerate(range(0, len(ends), count)):
        part = list(ends[start : start + count]) + [outer[2 * at], outer[2 * at + 1]]
        for inside, passed in zip(level.ghosts, level.passed):
            found.append(combine(list(inside) + list(passed), part))
    return found


def plus(total, weight, term):
    return total if term is None else total + weight * term


def tiles_of(shape):
    rows, width = shape[-2:]
    band = SUBLANES if rows % SUBLANES == 0 else rows
    for tile in range(width // LANES):
        for row in range(0, rows, band):
            yield tile, slice(row, row + band), slice(tile * LANES, (tile + 1) * LANES)


def pieces(value, values, units, tile, band, rows):
    count = band.stop - band.start
    step = min(units, count)
    for start in range(0, count, step):
        at = tile * rows + band.start + start
        to = (at // units * values + value) * units + at % units
        yield slice(start, start + step), slice(to, to + step)


def pinned(source, pins_ref, component, band, lanes):
    position = lax.axis_index("gx")
    first = jnp.where(position == 0, diffusion, 0.0).astype(jnp.float32)
    last = jnp.where(position == lax.axis_size("gx") - 1, diffusion, 0.0).astype(jnp.float32)
    source[0] = source[0] + first * pins_ref[0, component, band, lanes]
    source[-1] = source[-1] + last * pins_ref[1, component, band, lanes]
    return source


def read_field(field_ref, band, lanes):
    planes = field_ref.shape[1]
    return [[field_ref[c, i, band, lanes] for i in range(planes)] for c in range(3)]


def solve_components(line, field, axes_ref, pins_ref, band, lanes, ghosts):
    planes = line.planes
    field = list(field)
    axes = [[axes_ref[c, i, band, lanes] for i in range(planes)] for c in range(3)]
    for component in range(3):
        source = []
        for i in range(planes):
            projection = (
                field[0][i] * axes[0][i] + field[1][i] * axes[1][i] + field[2][i] * axes[2][i]
            )
            source.append(
                field[component][i] + (anisotropy_rate * projection) * axes[component][i]
            )
        source = pinned(source, pins_ref, component, band, lanes)
        if ghosts is not None:
            source[0] = source[0] + diffusion * ghosts[component][0]
            source[-1] = source[-1] + diffusion * ghosts[component][1]
        if ghosts is None and component == 2:
            return field[:2] + [line.ends(source)]
        field[component] = line.solve(source)
    return field


def couplings(line, axes_ref, band, lanes):
    planes = line.planes
    low, high = line.from_low, line.from_high
    axes = [[axes_ref[c, i, band, lanes] for i in range(planes)] for c in range(3)]
    scaled = [anisotropy_rate * a for a in axes[1]]
    first_second = [axes[0][i] * scaled[i] for i in range(planes)]
    second_third = [axes[2][i] * scaled[i] for i in range(planes)]
    first_third = [(anisotropy_rate * axes[0][i]) * axes[2][i] for i in range(planes)]

    def weighted(terms, weights):
        total = terms[0] * float(weights[0] / diffusion)
        for i in range(1, planes):
            total = total + terms[i] * float(weights[i] / diffusion)
        return total

    found = []
    for product in (first_second, second_third):
        for weights in (low * low, low * high, high * high):
            found.append(weighted(product, weights))
    for ghost in (low, high):
        moved = line.solve([first_second[i] * float(ghost[i]) for i in range(planes)])
        pushed = [
            second_third[i] * moved[i] + first_third[i] * float(ghost[i]) for i in range(planes)
        ]
        found.append(weighted(pushed, low))
        found.append(weighted(pushed, high))
    return found


def send_tile(line, units, values, field, axes_ref, pins_ref, out_ref, tile, band, lanes):
    rows = axes_ref.shape[2]
    solved = solve_components(line, field, axes_ref, pins_ref, band, lanes, None)
    for component in range(3):
        for side, end in enumerate((0, -1)):
            value = 2 * component + side
            for source, target in pieces(value, values, units, tile, band, rows):
                out_ref[target, :] = solved[component][end][source]


def coupling_kernel(line, units, axes_ref, out_ref):
    rows = axes_ref.shape[2]
    for tile, band, lanes in tiles_of(axes_ref.shape):
        for value, one in enumerate(couplings(line, axes_ref, band, lanes)):
            for source, target in pieces(value, COUPLED - RHS, units, tile, band, rows):
                out_ref[target, :] = one[source]


def first_kernel(line, groups, units, coupling_ref, field_ref, axes_ref, pins_ref, out_ref):
    extra = (COUPLED - RHS) * units
    for d in range(groups):
        start = (d * COUPLED + RHS) * units
        out_ref[start : start + extra, :] = coupling_ref[d * extra : (d + 1) * extra, :]
    for tile, band, lanes in tiles_of(field_ref.shape):
        field = read_field(field_ref, band, lanes)
        send_tile(line, units, COUPLED, field, axes_ref, pins_ref, out_ref, tile, band, lanes)


def solve_children(level, levels, rhs, coupling, outer):
    def ghosts(ends, component):
        found = settle(levels, ends)
        if outer is None:
            return found
        low, high = outer[component]
        moved = []
        for ghost, passed in zip(found, level.passed):
            terms = combine(passed, [low, high])
            moved.append(terms if ghost is None else ghost if terms is None else ghost + terms)
        return moved

    first = ghosts(rhs[0], 0)
    middle = []
    for d in range(level.radix):
        c, low, high = coupling[d], first[2 * d], first[2 * d + 1]
        middle.append(plus(plus(rhs[1][2 * d], c[0], low), c[1], high))
        middle.append(plus(plus(rhs[1][2 * d + 1], c[1], low), c[2], high))
    second = ghosts(middle, 1)
    last = []
    for d in range(level.radix):
        c, low1, high1 = coupling[d], first[2 * d], first[2 * d + 1]
        low2, high2 = second[2 * d], second[2 * d + 1]
        total = plus(plus(rhs[2][2 * d], c[3], low2), c[4], high2)
        last.append(plus(plus(total, c[6], low1), c[8], high1))
        total = plus(plus(rhs[2][2 * d + 1], c[4], low2), c[5], high2)
        last.append(plus(plus(total, c[7], low1), c[9], high1))
    return (first, second, ghosts(last, 2)), (rhs[0], middle, last)


def facing_coupling(level, levels, coupling, side):
    passed = level.passed[:, side]
    moved2, moved3 = [], []
    for r in range(level.radix):
        c, low, high = coupling[r], float(passed[2 * r]), float(passed[2 * r + 1])
        moved2 += [c[0] * low + c[1] * high, c[1] * low + c[2] * high]
        moved3 += [c[3] * low + c[4] * high, c[4] * low + c[5] * high]
    inner = settle(levels, moved2)
    through = []
    for r in range(level.radix):
        c, low, high = coupling[r], float(passed[2 * r]), float(passed[2 * r + 1])
        k_low, k_high = inner[2 * r], inner[2 * r + 1]
        total = plus(c[6] * low + c[8] * high, c[3], k_low)
        through.append(plus(total, c[4], k_high))
        total = plus(c[7] * low + c[9] * high, c[4], k_low)
        through.append(plus(total, c[5], k_high))
    return [combine(level.ends[side], moved) for moved in (moved2, moved3, through)]


def read_children(level, units, rhs_values, rhs_ref, coupling_ref):
    def read(ref, values, d, value):
        start = (d * values + value) * units
        return ref[start : start + units, :]

    rhs = [
        [read(rhs_ref, rhs_values, k // 2, 2 * c + k % 2) for k in range(2 * level.radix)]
        for c in range(3)
    ]
    coupling = [
        [read(coupling_ref, COUPLED, d, v) for v in range(RHS, COUPLED)]
        for d in range(level.radix)
    ]
    return rhs, coupling


def join_kernel(level, levels, units, coupled, rhs_ref, coupling_ref, out_ref):
    upper = lax.axis_index("gx") >= level.radix
    values = COUPLED if coupled else RHS
    rhs, coupling = read_children(level, units, values, rhs_ref, coupling_ref)
    _, seen = solve_children(level, levels, rhs, coupling, None)
    ends = [[combine(level.ends[side], seen[c]) for c in range(3)] for side in range(2)]
    if coupled:
        for side in range(2):
            ends[side] += facing_coupling(level, levels, coupling, side)
    for value, (first, last) in enumerate(zip(*ends)):
        out_ref[value * units : (value + 1) * units, :] = jnp.where(upper, first, last)


def part_kernel(
    level,
    levels,
    near,
    units,
    coupled,
    own_ref,
    other_ref,
    own_coupling_ref,
    other_coupling_ref,
    rhs_ref,
    coupling_ref,
    out_ref,
):
    upper = lax.axis_index("gx") >= level.radix

    def read(ref, value):
        return ref[value * units : (value + 1) * units, :]

    settled = 1.0 / (1.0 - near * near)

    def meet(own, other):
        beyond = other * settled + own * (near * settled)
        return beyond, own * settled + other * (near * settled)

    own = [read(own_ref, c) for c in range(3)]
    other = [read(other_ref, c) for c in range(3)]
    own_c = [read(own_coupling_ref, 3 + v) for v in range(3)]
    other_c = [read(other_coupling_ref, 3 + v) for v in range(3)]
    beyond1, back1 = meet(own[0], other[0])
    beyond2, back2 = meet(own[1] + own_c[0] * beyond1, other[1] + other_c[0] * back1)
    beyond3, _ = meet(
        own[2] + own_c[1] * beyond2 + own_c[2] * beyond1,
        other[2] + other_c[1] * back2 + other_c[2] * back1,
    )
    outer = [
        [jnp.where(upper, beyond, 0.0), jnp.where(upper, 0.0, beyond)]
        for beyond in (beyond1, beyond2, beyond3)
    ]
    values = COUPLED if coupled else RHS
    rhs, coupling = read_children(level, units, values, rhs_ref, coupling_ref)
    found, _ = solve_children(level, levels, rhs, coupling, outer)
    for c, ghosts in enumerate(found):
        for k, ghost in enumerate(ghosts):
            start = (k // 2 * RHS + 2 * c + k % 2) * units
            out_ref[start : start + units, :] = ghost


def finish_kernel(line, units, field_ref, axes_ref, pins_ref, ghost_ref, out_ref, edge_ref):
    planes, rows = line.planes, field_ref.shape[2]

    def ghost(value, tile, band):
        parts = [ghost_ref[at, :] for _, at in pieces(value, RHS, units, tile, band, rows)]
        return jnp.concatenate(parts, axis=0) if len(parts) > 1 else parts[0]

    for tile, band, lanes in tiles_of(field_ref.shape):
        ghosts = [[ghost(2 * c + side, tile, band) for side in range(2)] for c in range(3)]
        field = read_field(field_ref, band, lanes)
        solved = solve_components(line, field, axes_ref, pins_ref, band, lanes, ghosts)
        for c in range(3):
            for i in range(planes):
                at = c * planes + i
                out_ref[c, i, band, lanes] = solved[c][i]
                if band.start == 0:
                    edge_ref[0, at : at + 1, lanes] = solved[c][i][:1]
                if band.stop == rows:
                    edge_ref[1, at : at + 1, lanes] = solved[c][i][-1:]


def unit_scale(parts):
    square = parts[0] * parts[0] + parts[1] * parts[1] + parts[2] * parts[2]
    return jnp.minimum(lax.rsqrt(square), 1.0 / norm_floor)


def turn_kernel(field_ref, axes_ref, out_ref, raw_ref):
    planes, rows, width = field_ref.shape[1:]
    for i in range(planes):
        field = [field_ref[c, i] for c in range(3)]
        axes = [axes_ref[c, i] for c in range(3)]
        projection = field[0] * axes[0] + field[1] * axes[1] + field[2] * axes[2]
        projection = torque_rate * projection
        effective = []
        for c in range(3):
            below = pltpu.roll(field[c], 1, 0)
            above = pltpu.roll(field[c], rows - 1, 0)
            beside = pltpu.roll(field[c], 1, 1) + pltpu.roll(field[c], width - 1, 1)
            effective.append(
                (torque_rate * exchange_rate) * (((above + below) + beside) - 4.0 * field[c])
                + projection * axes[c]
            )
        rotated = []
        for c in range(3):
            d, e = (c + 1) % 3, (c + 2) % 3
            rotated.append(field[c] - field[d] * effective[e] + field[e] * effective[d])
        scale = unit_scale(rotated)
        for c in range(3):
            at = c * planes + i
            out_ref[c, i] = rotated[c] * scale
            raw_ref[0, at : at + 1, :] = rotated[c][:1]
            raw_ref[1, at : at + 1, :] = rotated[c][rows - 1 :]


def mend_edges(edge_ref, raw_ref, beyond_ref, mended_ref):
    planes = edge_ref.shape[1] // 3
    for side in range(2):
        parts = [slice(c * planes, (c + 1) * planes) for c in range(3)]
        field = [edge_ref[side, part, :] for part in parts]
        beyond = [beyond_ref[1 - side, part, :] - edge_ref[1 - side, part, :] for part in parts]
        rotated = []
        for c in range(3):
            d, e = (c + 1) % 3, (c + 2) % 3
            twisted = field[d] * beyond[e] - field[e] * beyond[d]
            rotated.append(raw_ref[side, parts[c], :] - (torque_rate * exchange_rate) * twisted)
        scale = unit_scale(rotated)
        for c in range(3):
            mended_ref[side, parts[c], :] = rotated[c] * scale


def mended(turned, mended_ref, at, band, rows, lanes):
    row = lax.broadcasted_iota(jnp.int32, turned.shape, 0)
    if band.start == 0:
        turned = jnp.where(row == 0, mended_ref[0, at : at + 1, lanes], turned)
    if band.stop == rows:
        last = row == turned.shape[0] - 1
        turned = jnp.where(last, mended_ref[1, at : at + 1, lanes], turned)
    return turned


def mend_and_send_kernel(
    line,
    units,
    turned_ref,
    edge_ref,
    raw_ref,
    beyond_ref,
    axes_ref,
    pins_ref,
    out_ref,
    sent_ref,
    mended_ref,
):
    planes = line.planes
    mend_edges(edge_ref, raw_ref, beyond_ref, mended_ref)
    rows = turned_ref.shape[2]
    for tile, band, lanes in tiles_of(turned_ref.shape):
        field = read_field(turned_ref, band, lanes)
        for c in range(3):
            for i in range(planes):
                at = c * planes + i
                field[c][i] = mended(field[c][i], mended_ref, at, band, rows, lanes)
                out_ref[c, i, band, lanes] = field[c][i]
        send_tile(line, units, RHS, field, axes_ref, pins_ref, sent_ref, tile, band, lanes)


def last_kernel(turned_ref, edge_ref, raw_ref, beyond_ref, out_hbm, out_ref, mended_ref, sems):
    planes, rows = turned_ref.shape[1:3]
    whole = slice(0, rows)

    def copy(i):
        return pltpu.make_async_copy(out_ref.at[:, i], out_hbm.at[:, i], sems.at[i])

    mend_edges(edge_ref, raw_ref, beyond_ref, mended_ref)
    for i in range(planes):
        for c in range(3):
            at = c * planes + i
            out_ref[c, i] = mended(turned_ref[c, i], mended_ref, at, whole, rows, slice(None))
        copy(i).start()
    for i in range(planes):
        copy(i).wait()


VMEM = pl.BlockSpec(memory_space=pltpu.VMEM)
HBM = pl.BlockSpec(memory_space=pltpu.HBM)
LIMIT = 32 * 1024 * 1024


def call(kernel, shapes, *operands, written=VMEM, scratch=()):
    shapes = [jax.ShapeDtypeStruct(shape, jnp.float32) for shape in shapes]
    return pl.pallas_call(
        kernel,
        out_shape=tuple(shapes),
        in_specs=[VMEM] * len(operands),
        out_specs=(written,) * len(shapes),
        scratch_shapes=scratch,
        compiler_params=pltpu.CompilerParams(vmem_limit_bytes=LIMIT),
    )(*operands)


def exchange(block, groups):
    parts = block.reshape(groups, -1, LANES)
    members = [
        list(range(start, start + groups)) for start in range(0, lax.axis_size("gx"), groups)
    ]
    return lax.all_to_all(
        parts, "gx", split_axis=0, concat_axis=0, axis_index_groups=members, tiled=True
    ).reshape(block.shape)


def swap_halves(block, groups):
    pairs = [(i, (i + groups) % (2 * groups)) for i in range(2 * groups)]
    return lax.ppermute(block, "gx", pairs)


def from_neighbours(edges):
    count = lax.axis_size("gy")
    forward = [(i, (i + 1) % count) for i in range(count)]
    if count == 2:
        return lax.ppermute(edges, "gy", forward)
    backward = [(target, source) for source, target in forward]
    return jnp.stack(
        [lax.ppermute(edges[0], "gy", backward), lax.ppermute(edges[1], "gy", forward)]
    )


def per_device(magnetization, easy_axes, pins):
    _, planes, rows, width = magnetization.shape
    groups = lax.axis_size("gx") // 2
    units = rows * (width // LANES) // groups
    line = Line(planes)
    levels = make_levels(planes, groups)
    level = Level(planes, groups)
    near = float(Line(planes * groups).from_low[0])
    whole = magnetization.shape
    sent_shape = (groups * RHS * units, LANES)
    edge_shape = (2, 3 * planes, width)

    field = magnetization
    (coupling,) = call(
        functools.partial(coupling_kernel, line, units),
        [(groups * (COUPLED - RHS) * units, LANES)],
        easy_axes,
    )
    (sent,) = call(
        functools.partial(first_kernel, line, groups, units),
        [(groups * COUPLED * units, LANES)],
        coupling,
        field,
        easy_axes,
        pins,
    )
    coupling = None
    for stepno in range(STEPS):
        gathered = exchange(sent, groups)
        coupled = stepno == 0
        if coupled:
            coupling = gathered
        (joined,) = call(
            functools.partial(join_kernel, level, levels, units, coupled),
            [((6 if coupled else 3) * units, LANES)],
            gathered,
            coupling,
        )
        swapped = swap_halves(joined, groups)
        if coupled:
            across = (joined, swapped)
        (ghosts,) = call(
            functools.partial(part_kernel, level, levels, near, units, coupled),
            [sent_shape],
            joined,
            swapped,
            *across,
            gathered,
            coupling,
        )
        ghosts = exchange(ghosts, groups)
        solved, edges = call(
            functools.partial(finish_kernel, line, units),
            [whole, edge_shape],
            field,
            easy_axes,
            pins,
            ghosts,
        )
        beyond = from_neighbours(edges)
        turned, raw = call(turn_kernel, [whole, edge_shape], solved, easy_axes)
        if stepno < STEPS - 1:
            field, sent = call(
                functools.partial(mend_and_send_kernel, line, units),
                [whole, sent_shape],
                turned,
                edges,
                raw,
                beyond,
                easy_axes,
                pins,
                scratch=[pltpu.VMEM(edge_shape, jnp.float32)],
            )
        else:
            (field,) = call(
                last_kernel,
                [whole],
                turned,
                edges,
                raw,
                beyond,
                written=HBM,
                scratch=[
                    pltpu.VMEM(whole, jnp.float32),
                    pltpu.VMEM(edge_shape, jnp.float32),
                    pltpu.SemaphoreType.DMA((planes,)),
                ],
            )
    return field


def solution(mesh):
    in_specs = (P(None, "gx", "gy", None), P(None, "gx", "gy", None), P(None, None, "gy", None))
    out_specs = P(None, "gx", "gy", None)
    return jax.shard_map(
        per_device, mesh=mesh, in_specs=in_specs, out_specs=out_specs, check_vma=False
    )
```

```python
import functools

import jax
import jax.numpy as jnp
import numpy as np
from jax import lax
from jax.experimental import pallas as pl
from jax.experimental.pallas import tpu as pltpu
from jax.sharding import PartitionSpec as P

STEPS = 2
LANES = 128
SUBLANES = 8
RHS = 6
COUPLED = 16

diffusion = 4000.0
anisotropy_rate = 0.3
torque_rate = 0.2
exchange_rate = 0.1
norm_floor = 0.5


class Line:
    def __init__(self, planes):
        leading = 1.0 + 2.0 * diffusion
        pivots = [leading]
        for _ in range(1, planes):
            pivots.append(leading - diffusion * diffusion / pivots[-1])
        self.planes = planes
        self.inverse_pivot = [1.0 / p for p in pivots]
        self.factor = [0.0] + [diffusion / p for p in pivots[:-1]]
        block = (
            leading * np.eye(planes)
            - diffusion * np.eye(planes, k=1)
            - diffusion * np.eye(planes, k=-1)
        )
        self.from_low = diffusion * np.linalg.inv(block)[:, 0]
        self.from_high = self.from_low[::-1]

    def sweep(self, source):
        carried = [source[0]]
        for i in range(1, len(source)):
            carried.append(source[i] + self.factor[i] * carried[-1])
        return carried

    def unwind(self, carried, meeting):
        solved = [None] * len(carried)
        solved[-1] = meeting
        for i in range(len(carried) - 2, -1, -1):
            solved[i] = carried[i] * self.inverse_pivot[i] + self.factor[i + 1] * solved[i + 1]
        return solved

    def solve_one_way(self, source):
        carried = self.sweep(source)
        return self.unwind(carried, carried[-1] * self.inverse_pivot[-1])

    def solve(self, source):
        half = self.planes // 2
        low, high = self.sweep(source[:half]), self.sweep(source[half:][::-1])
        pivot_low = 1.0 / self.inverse_pivot[len(low) - 1]
        pivot_high = 1.0 / self.inverse_pivot[len(high) - 1]
        scale = 1.0 / (pivot_low * pivot_high - diffusion * diffusion)
        cross = diffusion * scale
        meeting_low = low[-1] * (pivot_high * scale) + high[-1] * cross
        meeting_high = high[-1] * (pivot_low * scale) + low[-1] * cross
        return self.unwind(low, meeting_low) + self.unwind(high, meeting_high)[::-1]

    def ends(self, source):
        found = []
        for weights in (self.from_low, self.from_high):
            total = source[0] * float(weights[0] / diffusion)
            for weight, value in zip(weights[1:], source[1:]):
                total = total + value * float(weight / diffusion)
            found.append(total)
        return found


class Level:
    def __init__(self, length, radix):
        self.radix = radix
        line = Line(length)
        near, far = line.from_low[0], line.from_low[-1]
        count = 2 * radix
        inside = np.kron(np.eye(radix), np.array([[near, far], [far, near]]))
        pick = np.zeros((count, count))
        for r in range(radix):
            if r > 0:
                pick[2 * r, 2 * r - 1] = 1.0
            if r < radix - 1:
                pick[2 * r + 1, 2 * r + 2] = 1.0
        outer = np.zeros((count, 2))
        outer[0, 0] = outer[count - 1, 1] = 1.0
        settle = np.linalg.inv(np.eye(count) - pick @ inside)
        self.ghosts = settle @ pick
        self.passed = settle @ outer
        ends = (np.eye(count) + inside @ self.ghosts)[[0, count - 1]]
        self.ends = ends


def radices_of(groups):
    found = []
    while groups > 1:
        radix = 4 if groups % 4 == 0 else 2
        assert groups % radix == 0
        found.append(radix)
        groups //= radix
    return found


def combine(weights, terms):
    total = None
    for weight, term in zip(weights, terms):
        if weight == 0.0 or term is None:
            continue
        part = term * float(weight)
        total = part if total is None else total + part
    return total


def make_levels(planes, groups):
    found = []
    for radix in radices_of(groups):
        found.append(Level(planes, radix))
        planes *= radix
    return found


def settle(levels, ends):
    level, count = levels[0], 2 * levels[0].radix
    if len(levels) == 1:
        return [combine(weights, ends) for weights in level.ghosts]
    joined = []
    for start in range(0, len(ends), count):
        part = ends[start : start + count]
        joined += [combine(weights, part) for weights in level.ends]
    outer = settle(levels[1:], joined)
    found = []
    for at, start in enumerate(range(0, len(ends), count)):
        part = list(ends[start : start + count]) + [outer[2 * at], outer[2 * at + 1]]
        for inside, passed in zip(level.ghosts, level.passed):
            found.append(combine(list(inside) + list(passed), part))
    return found


def plus(total, weight, term):
    return total if term is None else total + weight * term


def tiles_of(shape, banded=True):
    rows, width = shape[-2:]
    band = SUBLANES if banded and rows % SUBLANES == 0 else rows
    for tile in range(width // LANES):
        for row in range(0, rows, band):
            yield tile, slice(row, row + band), slice(tile * LANES, (tile + 1) * LANES)


def pieces(value, values, units, tile, band, rows):
    count = band.stop - band.start
    step = min(units, count)
    for start in range(0, count, step):
        at = tile * rows + band.start + start
        to = (at // units * values + value) * units + at % units
        yield slice(start, start + step), slice(to, to + step)


def pinned(source, pins_ref, component, band, lanes):
    position = lax.axis_index("gx")
    first = jnp.where(position == 0, diffusion, 0.0).astype(jnp.float32)
    last = jnp.where(position == lax.axis_size("gx") - 1, diffusion, 0.0).astype(jnp.float32)
    source[0] = source[0] + first * pins_ref[0, component, band, lanes]
    source[-1] = source[-1] + last * pins_ref[1, component, band, lanes]
    return source


def read_field(field_ref, band, lanes):
    planes = field_ref.shape[1]
    return [[field_ref[c, i, band, lanes] for i in range(planes)] for c in range(3)]


def solve_components(line, field, axes_ref, pins_ref, band, lanes, ghosts):
    planes = line.planes
    field = list(field)
    axes = [[axes_ref[c, i, band, lanes] for i in range(planes)] for c in range(3)]
    for component in range(3):
        source = []
        for i in range(planes):
            projection = (
                field[0][i] * axes[0][i] + field[1][i] * axes[1][i] + field[2][i] * axes[2][i]
            )
            source.append(
                field[component][i] + (anisotropy_rate * projection) * axes[component][i]
            )
        source = pinned(source, pins_ref, component, band, lanes)
        if ghosts is not None:
            source[0] = source[0] + diffusion * ghosts[component][0]
            source[-1] = source[-1] + diffusion * ghosts[component][1]
        if ghosts is None and component == 2:
            return field[:2] + [line.ends(source)]
        field[component] = line.solve(source) if ghosts is None else line.solve_one_way(source)
    return field


def couplings(line, axes_ref, band, lanes):
    planes = line.planes
    low, high = line.from_low, line.from_high
    axes = [[axes_ref[c, i, band, lanes] for i in range(planes)] for c in range(3)]
    scaled = [anisotropy_rate * a for a in axes[1]]
    first_second = [axes[0][i] * scaled[i] for i in range(planes)]
    second_third = [axes[2][i] * scaled[i] for i in range(planes)]
    first_third = [(anisotropy_rate * axes[0][i]) * axes[2][i] for i in range(planes)]

    def weighted(terms, weights):
        total = terms[0] * float(weights[0] / diffusion)
        for i in range(1, planes):
            total = total + terms[i] * float(weights[i] / diffusion)
        return total

    found = []
    for product in (first_second, second_third):
        for weights in (low * low, low * high, high * high):
            found.append(weighted(product, weights))
    for ghost in (low, high):
        moved = line.solve([first_second[i] * float(ghost[i]) for i in range(planes)])
        pushed = [
            second_third[i] * moved[i] + first_third[i] * float(ghost[i]) for i in range(planes)
        ]
        found.append(weighted(pushed, low))
        found.append(weighted(pushed, high))
    return found


def send_tile(line, units, values, field, axes_ref, pins_ref, out_ref, tile, band, lanes):
    rows = axes_ref.shape[2]
    solved = solve_components(line, field, axes_ref, pins_ref, band, lanes, None)
    for component in range(3):
        for side, end in enumerate((0, -1)):
            value = 2 * component + side
            for source, target in pieces(value, values, units, tile, band, rows):
                out_ref[target, :] = solved[component][end][source]


def coupling_kernel(line, units, axes_ref, out_ref):
    rows = axes_ref.shape[2]
    for tile, band, lanes in tiles_of(axes_ref.shape):
        for value, one in enumerate(couplings(line, axes_ref, band, lanes)):
            for source, target in pieces(value, COUPLED - RHS, units, tile, band, rows):
                out_ref[target, :] = one[source]


def first_kernel(line, groups, units, coupling_ref, field_ref, axes_ref, pins_ref, out_ref):
    extra = (COUPLED - RHS) * units
    for d in range(groups):
        start = (d * COUPLED + RHS) * units
        out_ref[start : start + extra, :] = coupling_ref[d * extra : (d + 1) * extra, :]
    for tile, band, lanes in tiles_of(field_ref.shape):
        field = read_field(field_ref, band, lanes)
        send_tile(line, units, COUPLED, field, axes_ref, pins_ref, out_ref, tile, band, lanes)


def solve_children(level, levels, rhs, coupling, outer):
    def ghosts(ends, component):
        found = settle(levels, ends)
        if outer is None:
            return found
        low, high = outer[component]
        moved = []
        for ghost, passed in zip(found, level.passed):
            terms = combine(passed, [low, high])
            moved.append(terms if ghost is None else ghost if terms is None else ghost + terms)
        return moved

    first = ghosts(rhs[0], 0)
    middle = []
    for d in range(level.radix):
        c, low, high = coupling[d], first[2 * d], first[2 * d + 1]
        middle.append(plus(plus(rhs[1][2 * d], c[0], low), c[1], high))
        middle.append(plus(plus(rhs[1][2 * d + 1], c[1], low), c[2], high))
    second = ghosts(middle, 1)
    last = []
    for d in range(level.radix):
        c, low1, high1 = coupling[d], first[2 * d], first[2 * d + 1]
        low2, high2 = second[2 * d], second[2 * d + 1]
        total = plus(plus(rhs[2][2 * d], c[3], low2), c[4], high2)
        last.append(plus(plus(total, c[6], low1), c[8], high1))
        total = plus(plus(rhs[2][2 * d + 1], c[4], low2), c[5], high2)
        last.append(plus(plus(total, c[7], low1), c[9], high1))
    return (first, second, ghosts(last, 2)), (rhs[0], middle, last)


def facing_coupling(level, levels, coupling, side):
    passed = level.passed[:, side]
    moved2, moved3 = [], []
    for r in range(level.radix):
        c, low, high = coupling[r], float(passed[2 * r]), float(passed[2 * r + 1])
        moved2 += [c[0] * low + c[1] * high, c[1] * low + c[2] * high]
        moved3 += [c[3] * low + c[4] * high, c[4] * low + c[5] * high]
    inner = settle(levels, moved2)
    through = []
    for r in range(level.radix):
        c, low, high = coupling[r], float(passed[2 * r]), float(passed[2 * r + 1])
        k_low, k_high = inner[2 * r], inner[2 * r + 1]
        total = plus(c[6] * low + c[8] * high, c[3], k_low)
        through.append(plus(total, c[4], k_high))
        total = plus(c[7] * low + c[9] * high, c[4], k_low)
        through.append(plus(total, c[5], k_high))
    return [combine(level.ends[side], moved) for moved in (moved2, moved3, through)]


def read_children(level, units, rhs_values, rhs_ref, coupling_ref):
    def read(ref, values, d, value):
        start = (d * values + value) * units
        return ref[start : start + units, :]

    rhs = [
        [read(rhs_ref, rhs_values, k // 2, 2 * c + k % 2) for k in range(2 * level.radix)]
        for c in range(3)
    ]
    coupling = [
        [read(coupling_ref, COUPLED, d, v) for v in range(RHS, COUPLED)]
        for d in range(level.radix)
    ]
    return rhs, coupling


def join_kernel(level, levels, units, coupled, rhs_ref, coupling_ref, out_ref):
    upper = lax.axis_index("gx") >= level.radix
    values = COUPLED if coupled else RHS
    rhs, coupling = read_children(level, units, values, rhs_ref, coupling_ref)
    _, seen = solve_children(level, levels, rhs, coupling, None)
    ends = [[combine(level.ends[side], seen[c]) for c in range(3)] for side in range(2)]
    if coupled:
        for side in range(2):
            ends[side] += facing_coupling(level, levels, coupling, side)
    for value, (first, last) in enumerate(zip(*ends)):
        out_ref[value * units : (value + 1) * units, :] = jnp.where(upper, first, last)


def part_kernel(
    level,
    levels,
    near,
    units,
    coupled,
    own_ref,
    other_ref,
    own_coupling_ref,
    other_coupling_ref,
    rhs_ref,
    coupling_ref,
    out_ref,
):
    upper = lax.axis_index("gx") >= level.radix

    def read(ref, value):
        return ref[value * units : (value + 1) * units, :]

    settled = 1.0 / (1.0 - near * near)

    def meet(own, other):
        beyond = other * settled + own * (near * settled)
        return beyond, own * settled + other * (near * settled)

    own = [read(own_ref, c) for c in range(3)]
    other = [read(other_ref, c) for c in range(3)]
    own_c = [read(own_coupling_ref, 3 + v) for v in range(3)]
    other_c = [read(other_coupling_ref, 3 + v) for v in range(3)]
    beyond1, back1 = meet(own[0], other[0])
    beyond2, back2 = meet(own[1] + own_c[0] * beyond1, other[1] + other_c[0] * back1)
    beyond3, _ = meet(
        own[2] + own_c[1] * beyond2 + own_c[2] * beyond1,
        other[2] + other_c[1] * back2 + other_c[2] * back1,
    )
    outer = [
        [jnp.where(upper, beyond, 0.0), jnp.where(upper, 0.0, beyond)]
        for beyond in (beyond1, beyond2, beyond3)
    ]
    values = COUPLED if coupled else RHS
    rhs, coupling = read_children(level, units, values, rhs_ref, coupling_ref)
    found, _ = solve_children(level, levels, rhs, coupling, outer)
    for c, ghosts in enumerate(found):
        for k, ghost in enumerate(ghosts):
            start = (k // 2 * RHS + 2 * c + k % 2) * units
            out_ref[start : start + units, :] = ghost


def finish_kernel(line, units, field_ref, axes_ref, pins_ref, ghost_ref, out_ref, edge_ref):
    planes, rows = line.planes, field_ref.shape[2]

    def ghost(value, tile, band):
        parts = [ghost_ref[at, :] for _, at in pieces(value, RHS, units, tile, band, rows)]
        return jnp.concatenate(parts, axis=0) if len(parts) > 1 else parts[0]

    for tile, band, lanes in tiles_of(field_ref.shape, banded=False):
        ghosts = [[ghost(2 * c + side, tile, band) for side in range(2)] for c in range(3)]
        field = read_field(field_ref, band, lanes)
        solved = solve_components(line, field, axes_ref, pins_ref, band, lanes, ghosts)
        for c in range(3):
            for i in range(planes):
                at = c * planes + i
                out_ref[c, i, band, lanes] = solved[c][i]
                if band.start == 0:
                    edge_ref[0, at : at + 1, lanes] = solved[c][i][:1]
                if band.stop == rows:
                    edge_ref[1, at : at + 1, lanes] = solved[c][i][-1:]


def unit_scale(parts):
    square = parts[0] * parts[0] + parts[1] * parts[1] + parts[2] * parts[2]
    return jnp.minimum(lax.rsqrt(square), 1.0 / norm_floor)


def turn_kernel(field_ref, axes_ref, out_ref, raw_ref):
    planes, rows, width = field_ref.shape[1:]
    for i in range(planes):
        field = [field_ref[c, i] for c in range(3)]
        axes = [axes_ref[c, i] for c in range(3)]
        projection = field[0] * axes[0] + field[1] * axes[1] + field[2] * axes[2]
        projection = torque_rate * projection
        effective = []
        for c in range(3):
            below = pltpu.roll(field[c], 1, 0)
            above = pltpu.roll(field[c], rows - 1, 0)
            beside = pltpu.roll(field[c], 1, 1) + pltpu.roll(field[c], width - 1, 1)
            effective.append(
                (torque_rate * exchange_rate) * (((above + below) + beside) - 4.0 * field[c])
                + projection * axes[c]
            )
        rotated = []
        for c in range(3):
            d, e = (c + 1) % 3, (c + 2) % 3
            rotated.append(field[c] - field[d] * effective[e] + field[e] * effective[d])
        scale = unit_scale(rotated)
        for c in range(3):
            at = c * planes + i
            out_ref[c, i] = rotated[c] * scale
            raw_ref[0, at : at + 1, :] = rotated[c][:1]
            raw_ref[1, at : at + 1, :] = rotated[c][rows - 1 :]


def mend_edges(edge_ref, raw_ref, beyond_ref, mended_ref):
    planes = edge_ref.shape[1] // 3
    for side in range(2):
        parts = [slice(c * planes, (c + 1) * planes) for c in range(3)]
        field = [edge_ref[side, part, :] for part in parts]
        beyond = [beyond_ref[1 - side, part, :] - edge_ref[1 - side, part, :] for part in parts]
        rotated = []
        for c in range(3):
            d, e = (c + 1) % 3, (c + 2) % 3
            twisted = field[d] * beyond[e] - field[e] * beyond[d]
            rotated.append(raw_ref[side, parts[c], :] - (torque_rate * exchange_rate) * twisted)
        scale = unit_scale(rotated)
        for c in range(3):
            mended_ref[side, parts[c], :] = rotated[c] * scale


def mended(turned, mended_ref, at, band, rows, lanes):
    row = lax.broadcasted_iota(jnp.int32, turned.shape, 0)
    if band.start == 0:
        turned = jnp.where(row == 0, mended_ref[0, at : at + 1, lanes], turned)
    if band.stop == rows:
        last = row == turned.shape[0] - 1
        turned = jnp.where(last, mended_ref[1, at : at + 1, lanes], turned)
    return turned


def mend_and_send_kernel(
    line,
    units,
    turned_ref,
    edge_ref,
    raw_ref,
    beyond_ref,
    axes_ref,
    pins_ref,
    out_ref,
    sent_ref,
    mended_ref,
):
    planes = line.planes
    mend_edges(edge_ref, raw_ref, beyond_ref, mended_ref)
    rows = turned_ref.shape[2]
    for tile, band, lanes in tiles_of(turned_ref.shape):
        field = read_field(turned_ref, band, lanes)
        for c in range(3):
            for i in range(planes):
                at = c * planes + i
                field[c][i] = mended(field[c][i], mended_ref, at, band, rows, lanes)
                out_ref[c, i, band, lanes] = field[c][i]
        send_tile(line, units, RHS, field, axes_ref, pins_ref, sent_ref, tile, band, lanes)


def last_kernel(turned_ref, edge_ref, raw_ref, beyond_ref, out_hbm, out_ref, mended_ref, sems):
    planes, rows = turned_ref.shape[1:3]
    whole = slice(0, rows)

    def copy(i):
        return pltpu.make_async_copy(out_ref.at[:, i], out_hbm.at[:, i], sems.at[i])

    mend_edges(edge_ref, raw_ref, beyond_ref, mended_ref)
    for i in range(planes):
        for c in range(3):
            at = c * planes + i
            out_ref[c, i] = mended(turned_ref[c, i], mended_ref, at, whole, rows, slice(None))
        copy(i).start()
    for i in range(planes):
        copy(i).wait()


VMEM = pl.BlockSpec(memory_space=pltpu.VMEM)
HBM = pl.BlockSpec(memory_space=pltpu.HBM)
LIMIT = 32 * 1024 * 1024


def call(kernel, shapes, *operands, written=VMEM, scratch=()):
    shapes = [jax.ShapeDtypeStruct(shape, jnp.float32) for shape in shapes]
    return pl.pallas_call(
        kernel,
        out_shape=tuple(shapes),
        in_specs=[VMEM] * len(operands),
        out_specs=(written,) * len(shapes),
        scratch_shapes=scratch,
        compiler_params=pltpu.CompilerParams(vmem_limit_bytes=LIMIT),
    )(*operands)


def exchange(block, groups):
    parts = block.reshape(groups, -1, LANES)
    members = [
        list(range(start, start + groups)) for start in range(0, lax.axis_size("gx"), groups)
    ]
    return lax.all_to_all(
        parts, "gx", split_axis=0, concat_axis=0, axis_index_groups=members, tiled=True
    ).reshape(block.shape)


def swap_halves(block, groups):
    pairs = [(i, (i + groups) % (2 * groups)) for i in range(2 * groups)]
    return lax.ppermute(block, "gx", pairs)


def from_neighbours(edges):
    count = lax.axis_size("gy")
    forward = [(i, (i + 1) % count) for i in range(count)]
    if count == 2:
        return lax.ppermute(edges, "gy", forward)
    backward = [(target, source) for source, target in forward]
    return jnp.stack(
        [lax.ppermute(edges[0], "gy", backward), lax.ppermute(edges[1], "gy", forward)]
    )


def per_device(magnetization, easy_axes, pins):
    _, planes, rows, width = magnetization.shape
    groups = lax.axis_size("gx") // 2
    units = rows * (width // LANES) // groups
    line = Line(planes)
    levels = make_levels(planes, groups)
    level = Level(planes, groups)
    near = float(Line(planes * groups).from_low[0])
    whole = magnetization.shape
    sent_shape = (groups * RHS * units, LANES)
    edge_shape = (2, 3 * planes, width)

    field = magnetization
    (coupling,) = call(
        functools.partial(coupling_kernel, line, units),
        [(groups * (COUPLED - RHS) * units, LANES)],
        easy_axes,
    )
    (sent,) = call(
        functools.partial(first_kernel, line, groups, units),
        [(groups * COUPLED * units, LANES)],
        coupling,
        field,
        easy_axes,
        pins,
    )
    coupling = None
    for stepno in range(STEPS):
        gathered = exchange(sent, groups)
        coupled = stepno == 0
        if coupled:
            coupling = gathered
        (joined,) = call(
            functools.partial(join_kernel, level, levels, units, coupled),
            [((6 if coupled else 3) * units, LANES)],
            gathered,
            coupling,
        )
        swapped = swap_halves(joined, groups)
        if coupled:
            across = (joined, swapped)
        (ghosts,) = call(
            functools.partial(part_kernel, level, levels, near, units, coupled),
            [sent_shape],
            joined,
            swapped,
            *across,
            gathered,
            coupling,
        )
        ghosts = exchange(ghosts, groups)
        solved, edges = call(
            functools.partial(finish_kernel, line, units),
            [whole, edge_shape],
            field,
            easy_axes,
            pins,
            ghosts,
        )
        beyond = from_neighbours(edges)
        turned, raw = call(turn_kernel, [whole, edge_shape], solved, easy_axes)
        if stepno < STEPS - 1:
            field, sent = call(
                functools.partial(mend_and_send_kernel, line, units),
                [whole, sent_shape],
                turned,
                edges,
                raw,
                beyond,
                easy_axes,
                pins,
                scratch=[pltpu.VMEM(edge_shape, jnp.float32)],
            )
        else:
            (field,) = call(
                last_kernel,
                [whole],
                turned,
                edges,
                raw,
                beyond,
                written=HBM,
                scratch=[
                    pltpu.VMEM(whole, jnp.float32),
                    pltpu.VMEM(edge_shape, jnp.float32),
                    pltpu.SemaphoreType.DMA((planes,)),
                ],
            )
    return field


def solution(mesh):
    in_specs = (P(None, "gx", "gy", None), P(None, "gx", "gy", None), P(None, None, "gy", None))
    out_specs = P(None, "gx", "gy", None)
    return jax.shard_map(
        per_device, mesh=mesh, in_specs=in_specs, out_specs=out_specs, check_vma=False
    )
```

```python
import functools

import jax
import jax.numpy as jnp
import numpy as np
from jax import lax
from jax.experimental import pallas as pl
from jax.experimental.pallas import tpu as pltpu
from jax.sharding import PartitionSpec as P

STEPS = 2
LANES = 128
SUBLANES = 8
RHS = 6
COUPLED = 16

diffusion = 4000.0
anisotropy_rate = 0.3
torque_rate = 0.2
exchange_rate = 0.1
norm_floor = 0.5


class Line:
    def __init__(self, planes):
        leading = 1.0 + 2.0 * diffusion
        pivots = [leading]
        for _ in range(1, planes):
            pivots.append(leading - diffusion * diffusion / pivots[-1])
        self.planes = planes
        self.inverse_pivot = [1.0 / p for p in pivots]
        self.factor = [0.0] + [diffusion / p for p in pivots[:-1]]
        block = (
            leading * np.eye(planes)
            - diffusion * np.eye(planes, k=1)
            - diffusion * np.eye(planes, k=-1)
        )
        self.from_low = diffusion * np.linalg.inv(block)[:, 0]
        self.from_high = self.from_low[::-1]

    def sweep(self, source):
        carried = [source[0]]
        for i in range(1, len(source)):
            carried.append(source[i] + self.factor[i] * carried[-1])
        return carried

    def unwind(self, carried, meeting):
        solved = [None] * len(carried)
        solved[-1] = meeting
        for i in range(len(carried) - 2, -1, -1):
            solved[i] = carried[i] * self.inverse_pivot[i] + self.factor[i + 1] * solved[i + 1]
        return solved

    def solve_one_way(self, source):
        carried = self.sweep(source)
        return self.unwind(carried, carried[-1] * self.inverse_pivot[-1])

    def solve(self, source):
        half = self.planes // 2
        low, high = self.sweep(source[:half]), self.sweep(source[half:][::-1])
        pivot_low = 1.0 / self.inverse_pivot[len(low) - 1]
        pivot_high = 1.0 / self.inverse_pivot[len(high) - 1]
        scale = 1.0 / (pivot_low * pivot_high - diffusion * diffusion)
        cross = diffusion * scale
        meeting_low = low[-1] * (pivot_high * scale) + high[-1] * cross
        meeting_high = high[-1] * (pivot_low * scale) + low[-1] * cross
        return self.unwind(low, meeting_low) + self.unwind(high, meeting_high)[::-1]

    def ends(self, source):
        found = []
        for weights in (self.from_low, self.from_high):
            total = source[0] * float(weights[0] / diffusion)
            for weight, value in zip(weights[1:], source[1:]):
                total = total + value * float(weight / diffusion)
            found.append(total)
        return found


class Level:
    def __init__(self, length, radix):
        self.radix = radix
        line = Line(length)
        near, far = line.from_low[0], line.from_low[-1]
        count = 2 * radix
        inside = np.kron(np.eye(radix), np.array([[near, far], [far, near]]))
        pick = np.zeros((count, count))
        for r in range(radix):
            if r > 0:
                pick[2 * r, 2 * r - 1] = 1.0
            if r < radix - 1:
                pick[2 * r + 1, 2 * r + 2] = 1.0
        outer = np.zeros((count, 2))
        outer[0, 0] = outer[count - 1, 1] = 1.0
        settle = np.linalg.inv(np.eye(count) - pick @ inside)
        self.ghosts = settle @ pick
        self.passed = settle @ outer
        ends = (np.eye(count) + inside @ self.ghosts)[[0, count - 1]]
        self.ends = ends


def radices_of(groups):
    found = []
    while groups > 1:
        radix = 4 if groups % 4 == 0 else 2
        assert groups % radix == 0
        found.append(radix)
        groups //= radix
    return found


def combine(weights, terms):
    total = None
    for weight, term in zip(weights, terms):
        if weight == 0.0 or term is None:
            continue
        part = term * float(weight)
        total = part if total is None else total + part
    return total


def make_levels(planes, groups):
    found = []
    for radix in radices_of(groups):
        found.append(Level(planes, radix))
        planes *= radix
    return found


def settle(levels, ends):
    level, count = levels[0], 2 * levels[0].radix
    if len(levels) == 1:
        return [combine(weights, ends) for weights in level.ghosts]
    joined = []
    for start in range(0, len(ends), count):
        part = ends[start : start + count]
        joined += [combine(weights, part) for weights in level.ends]
    outer = settle(levels[1:], joined)
    found = []
    for at, start in enumerate(range(0, len(ends), count)):
        part = list(ends[start : start + count]) + [outer[2 * at], outer[2 * at + 1]]
        for inside, passed in zip(level.ghosts, level.passed):
            found.append(combine(list(inside) + list(passed), part))
    return found


def plus(total, weight, term):
    return total if term is None else total + weight * term


def tiles_of(shape, banded=True):
    rows, width = shape[-2:]
    band = SUBLANES if banded and rows % SUBLANES == 0 else rows
    for tile in range(width // LANES):
        for row in range(0, rows, band):
            yield tile, slice(row, row + band), slice(tile * LANES, (tile + 1) * LANES)


def pieces(value, values, units, tile, band, rows):
    count = band.stop - band.start
    step = min(units, count)
    for start in range(0, count, step):
        at = tile * rows + band.start + start
        to = (at // units * values + value) * units + at % units
        yield slice(start, start + step), slice(to, to + step)


def pinned(source, pins_ref, component, band, lanes):
    position = lax.axis_index("gx")
    first = jnp.where(position == 0, diffusion, 0.0).astype(jnp.float32)
    last = jnp.where(position == lax.axis_size("gx") - 1, diffusion, 0.0).astype(jnp.float32)
    source[0] = source[0] + first * pins_ref[0, component, band, lanes]
    source[-1] = source[-1] + last * pins_ref[1, component, band, lanes]
    return source


def read_field(field_ref, band, lanes):
    planes = field_ref.shape[1]
    return [[field_ref[c, i, band, lanes] for i in range(planes)] for c in range(3)]


def solve_components(line, field, axes_ref, pins_ref, band, lanes, ghosts):
    planes = line.planes
    field = list(field)
    axes = [[axes_ref[c, i, band, lanes] for i in range(planes)] for c in range(3)]
    for component in range(3):
        source = []
        for i in range(planes):
            projection = (
                field[0][i] * axes[0][i] + field[1][i] * axes[1][i] + field[2][i] * axes[2][i]
            )
            source.append(
                field[component][i] + (anisotropy_rate * projection) * axes[component][i]
            )
        source = pinned(source, pins_ref, component, band, lanes)
        if ghosts is not None:
            source[0] = source[0] + diffusion * ghosts[component][0]
            source[-1] = source[-1] + diffusion * ghosts[component][1]
        if ghosts is None and component == 2:
            return field[:2] + [line.ends(source)]
        field[component] = line.solve(source) if ghosts is None else line.solve_one_way(source)
    return field


def couplings(line, axes_ref, band, lanes):
    planes = line.planes
    low, high = line.from_low, line.from_high
    axes = [[axes_ref[c, i, band, lanes] for i in range(planes)] for c in range(3)]
    scaled = [anisotropy_rate * a for a in axes[1]]
    first_second = [axes[0][i] * scaled[i] for i in range(planes)]
    second_third = [axes[2][i] * scaled[i] for i in range(planes)]
    first_third = [(anisotropy_rate * axes[0][i]) * axes[2][i] for i in range(planes)]

    def weighted(terms, weights):
        total = terms[0] * float(weights[0] / diffusion)
        for i in range(1, planes):
            total = total + terms[i] * float(weights[i] / diffusion)
        return total

    found = []
    for product in (first_second, second_third):
        for weights in (low * low, low * high, high * high):
            found.append(weighted(product, weights))
    for ghost in (low, high):
        moved = line.solve([first_second[i] * float(ghost[i]) for i in range(planes)])
        pushed = [
            second_third[i] * moved[i] + first_third[i] * float(ghost[i]) for i in range(planes)
        ]
        found.append(weighted(pushed, low))
        found.append(weighted(pushed, high))
    return found


def send_tile(line, units, values, field, axes_ref, pins_ref, out_ref, tile, band, lanes):
    rows = axes_ref.shape[2]
    solved = solve_components(line, field, axes_ref, pins_ref, band, lanes, None)
    for component in range(3):
        for side, end in enumerate((0, -1)):
            value = 2 * component + side
            for source, target in pieces(value, values, units, tile, band, rows):
                out_ref[target, :] = solved[component][end][source]


def coupling_kernel(line, units, axes_ref, out_ref):
    rows = axes_ref.shape[2]
    for tile, band, lanes in tiles_of(axes_ref.shape):
        for value, one in enumerate(couplings(line, axes_ref, band, lanes)):
            for source, target in pieces(value, COUPLED - RHS, units, tile, band, rows):
                out_ref[target, :] = one[source]


def first_kernel(line, groups, units, coupling_ref, field_ref, axes_ref, pins_ref, out_ref):
    extra = (COUPLED - RHS) * units
    for d in range(groups):
        start = (d * COUPLED + RHS) * units
        out_ref[start : start + extra, :] = coupling_ref[d * extra : (d + 1) * extra, :]
    for tile, band, lanes in tiles_of(field_ref.shape):
        field = read_field(field_ref, band, lanes)
        send_tile(line, units, COUPLED, field, axes_ref, pins_ref, out_ref, tile, band, lanes)


def solve_children(level, levels, rhs, coupling, outer):
    def ghosts(ends, component):
        found = settle(levels, ends)
        if outer is None:
            return found
        low, high = outer[component]
        moved = []
        for ghost, passed in zip(found, level.passed):
            terms = combine(passed, [low, high])
            moved.append(terms if ghost is None else ghost if terms is None else ghost + terms)
        return moved

    first = ghosts(rhs[0], 0)
    middle = []
    for d in range(level.radix):
        c, low, high = coupling[d], first[2 * d], first[2 * d + 1]
        middle.append(plus(plus(rhs[1][2 * d], c[0], low), c[1], high))
        middle.append(plus(plus(rhs[1][2 * d + 1], c[1], low), c[2], high))
    second = ghosts(middle, 1)
    last = []
    for d in range(level.radix):
        c, low1, high1 = coupling[d], first[2 * d], first[2 * d + 1]
        low2, high2 = second[2 * d], second[2 * d + 1]
        total = plus(plus(rhs[2][2 * d], c[3], low2), c[4], high2)
        last.append(plus(plus(total, c[6], low1), c[8], high1))
        total = plus(plus(rhs[2][2 * d + 1], c[4], low2), c[5], high2)
        last.append(plus(plus(total, c[7], low1), c[9], high1))
    return (first, second, ghosts(last, 2)), (rhs[0], middle, last)


def facing_coupling(level, levels, coupling, side):
    passed = level.passed[:, side]
    moved2, moved3 = [], []
    for r in range(level.radix):
        c, low, high = coupling[r], float(passed[2 * r]), float(passed[2 * r + 1])
        moved2 += [c[0] * low + c[1] * high, c[1] * low + c[2] * high]
        moved3 += [c[3] * low + c[4] * high, c[4] * low + c[5] * high]
    inner = settle(levels, moved2)
    through = []
    for r in range(level.radix):
        c, low, high = coupling[r], float(passed[2 * r]), float(passed[2 * r + 1])
        k_low, k_high = inner[2 * r], inner[2 * r + 1]
        total = plus(c[6] * low + c[8] * high, c[3], k_low)
        through.append(plus(total, c[4], k_high))
        total = plus(c[7] * low + c[9] * high, c[4], k_low)
        through.append(plus(total, c[5], k_high))
    return [combine(level.ends[side], moved) for moved in (moved2, moved3, through)]


def read_children(level, units, rhs_values, rhs_ref, coupling_ref):
    def read(ref, values, d, value):
        start = (d * values + value) * units
        return ref[start : start + units, :]

    rhs = [
        [read(rhs_ref, rhs_values, k // 2, 2 * c + k % 2) for k in range(2 * level.radix)]
        for c in range(3)
    ]
    coupling = [
        [read(coupling_ref, COUPLED, d, v) for v in range(RHS, COUPLED)]
        for d in range(level.radix)
    ]
    return rhs, coupling


def join_kernel(level, levels, units, coupled, rhs_ref, coupling_ref, out_ref):
    upper = lax.axis_index("gx") >= level.radix
    values = COUPLED if coupled else RHS
    rhs, coupling = read_children(level, units, values, rhs_ref, coupling_ref)
    _, seen = solve_children(level, levels, rhs, coupling, None)
    ends = [[combine(level.ends[side], seen[c]) for c in range(3)] for side in range(2)]
    if coupled:
        for side in range(2):
            ends[side] += facing_coupling(level, levels, coupling, side)
    for value, (first, last) in enumerate(zip(*ends)):
        out_ref[value * units : (value + 1) * units, :] = jnp.where(upper, first, last)


def part_kernel(
    level,
    levels,
    near,
    units,
    coupled,
    own_ref,
    other_ref,
    own_coupling_ref,
    other_coupling_ref,
    rhs_ref,
    coupling_ref,
    out_ref,
):
    upper = lax.axis_index("gx") >= level.radix

    def read(ref, value):
        return ref[value * units : (value + 1) * units, :]

    settled = 1.0 / (1.0 - near * near)

    def meet(own, other):
        beyond = other * settled + own * (near * settled)
        return beyond, own * settled + other * (near * settled)

    own = [read(own_ref, c) for c in range(3)]
    other = [read(other_ref, c) for c in range(3)]
    own_c = [read(own_coupling_ref, 3 + v) for v in range(3)]
    other_c = [read(other_coupling_ref, 3 + v) for v in range(3)]
    beyond1, back1 = meet(own[0], other[0])
    beyond2, back2 = meet(own[1] + own_c[0] * beyond1, other[1] + other_c[0] * back1)
    beyond3, _ = meet(
        own[2] + own_c[1] * beyond2 + own_c[2] * beyond1,
        other[2] + other_c[1] * back2 + other_c[2] * back1,
    )
    outer = [
        [jnp.where(upper, beyond, 0.0), jnp.where(upper, 0.0, beyond)]
        for beyond in (beyond1, beyond2, beyond3)
    ]
    values = COUPLED if coupled else RHS
    rhs, coupling = read_children(level, units, values, rhs_ref, coupling_ref)
    found, _ = solve_children(level, levels, rhs, coupling, outer)
    for c, ghosts in enumerate(found):
        for k, ghost in enumerate(ghosts):
            start = (k // 2 * RHS + 2 * c + k % 2) * units
            out_ref[start : start + units, :] = ghost


def finish_kernel(line, units, field_ref, axes_ref, pins_ref, ghost_ref, out_ref, edge_ref):
    planes, rows = line.planes, field_ref.shape[2]

    def ghost(value, tile, band):
        parts = [ghost_ref[at, :] for _, at in pieces(value, RHS, units, tile, band, rows)]
        return jnp.concatenate(parts, axis=0) if len(parts) > 1 else parts[0]

    for tile, band, lanes in tiles_of(field_ref.shape, banded=False):
        ghosts = [[ghost(2 * c + side, tile, band) for side in range(2)] for c in range(3)]
        field = read_field(field_ref, band, lanes)
        solved = solve_components(line, field, axes_ref, pins_ref, band, lanes, ghosts)
        for c in range(3):
            for i in range(planes):
                at = c * planes + i
                out_ref[c, i, band, lanes] = solved[c][i]
                if band.start == 0:
                    edge_ref[0, at : at + 1, lanes] = solved[c][i][:1]
                if band.stop == rows:
                    edge_ref[1, at : at + 1, lanes] = solved[c][i][-1:]


def unit_scale(parts):
    square = parts[0] * parts[0] + parts[1] * parts[1] + parts[2] * parts[2]
    return jnp.minimum(lax.rsqrt(square), 1.0 / norm_floor)


def turn_kernel(field_ref, axes_ref, out_ref, raw_ref):
    planes, rows, width = field_ref.shape[1:]
    for i in range(planes):
        field = [field_ref[c, i] for c in range(3)]
        axes = [axes_ref[c, i] for c in range(3)]
        projection = field[0] * axes[0] + field[1] * axes[1] + field[2] * axes[2]
        projection = torque_rate * projection
        effective = []
        for c in range(3):
            below = pltpu.roll(field[c], 1, 0)
            above = pltpu.roll(field[c], rows - 1, 0)
            beside = pltpu.roll(field[c], 1, 1) + pltpu.roll(field[c], width - 1, 1)
            effective.append(
                (torque_rate * exchange_rate) * (((above + below) + beside) - 4.0 * field[c])
                + projection * axes[c]
            )
        rotated = []
        for c in range(3):
            d, e = (c + 1) % 3, (c + 2) % 3
            rotated.append(field[c] - field[d] * effective[e] + field[e] * effective[d])
        scale = unit_scale(rotated)
        for c in range(3):
            at = c * planes + i
            out_ref[c, i] = rotated[c] * scale
            raw_ref[0, at : at + 1, :] = rotated[c][:1]
            raw_ref[1, at : at + 1, :] = rotated[c][rows - 1 :]


def mend_edges(edge_ref, raw_ref, beyond_ref, mended_ref):
    planes = edge_ref.shape[1] // 3
    for side in range(2):
        parts = [slice(c * planes, (c + 1) * planes) for c in range(3)]
        field = [edge_ref[side, part, :] for part in parts]
        beyond = [beyond_ref[1 - side, part, :] - edge_ref[1 - side, part, :] for part in parts]
        rotated = []
        for c in range(3):
            d, e = (c + 1) % 3, (c + 2) % 3
            twisted = field[d] * beyond[e] - field[e] * beyond[d]
            rotated.append(raw_ref[side, parts[c], :] - (torque_rate * exchange_rate) * twisted)
        scale = unit_scale(rotated)
        for c in range(3):
            mended_ref[side, parts[c], :] = rotated[c] * scale


def mended(turned, mended_ref, at, band, rows, lanes):
    row = lax.broadcasted_iota(jnp.int32, turned.shape, 0)
    if band.start == 0:
        turned = jnp.where(row == 0, mended_ref[0, at : at + 1, lanes], turned)
    if band.stop == rows:
        last = row == turned.shape[0] - 1
        turned = jnp.where(last, mended_ref[1, at : at + 1, lanes], turned)
    return turned


def mend_and_send_kernel(
    line,
    units,
    turned_ref,
    edge_ref,
    raw_ref,
    beyond_ref,
    axes_ref,
    pins_ref,
    out_ref,
    sent_ref,
    mended_ref,
):
    planes = line.planes
    mend_edges(edge_ref, raw_ref, beyond_ref, mended_ref)
    rows = turned_ref.shape[2]
    for tile, band, lanes in tiles_of(turned_ref.shape):
        field = read_field(turned_ref, band, lanes)
        for c in range(3):
            for i in range(planes):
                at = c * planes + i
                field[c][i] = mended(field[c][i], mended_ref, at, band, rows, lanes)
                out_ref[c, i, band, lanes] = field[c][i]
        send_tile(line, units, RHS, field, axes_ref, pins_ref, sent_ref, tile, band, lanes)


def last_kernel(turned_ref, edge_ref, raw_ref, beyond_ref, out_hbm, out_ref, mended_ref, sems):
    planes, rows = turned_ref.shape[1:3]
    whole = slice(0, rows)

    group = 4 if planes % 4 == 0 else 1

    def copy(i):
        part = pl.ds(i, group)
        return pltpu.make_async_copy(out_ref.at[:, part], out_hbm.at[:, part], sems.at[i])

    mend_edges(edge_ref, raw_ref, beyond_ref, mended_ref)
    for i in range(planes):
        for c in range(3):
            at = c * planes + i
            out_ref[c, i] = mended(turned_ref[c, i], mended_ref, at, whole, rows, slice(None))
        if i % group == group - 1:
            copy(i + 1 - group).start()
    for i in range(0, planes, group):
        copy(i).wait()


VMEM = pl.BlockSpec(memory_space=pltpu.VMEM)
HBM = pl.BlockSpec(memory_space=pltpu.HBM)
LIMIT = 32 * 1024 * 1024


def call(kernel, shapes, *operands, written=VMEM, scratch=()):
    shapes = [jax.ShapeDtypeStruct(shape, jnp.float32) for shape in shapes]
    return pl.pallas_call(
        kernel,
        out_shape=tuple(shapes),
        in_specs=[VMEM] * len(operands),
        out_specs=(written,) * len(shapes),
        scratch_shapes=scratch,
        compiler_params=pltpu.CompilerParams(vmem_limit_bytes=LIMIT),
    )(*operands)


def exchange(block, groups):
    parts = block.reshape(groups, -1, LANES)
    members = [
        list(range(start, start + groups)) for start in range(0, lax.axis_size("gx"), groups)
    ]
    return lax.all_to_all(
        parts, "gx", split_axis=0, concat_axis=0, axis_index_groups=members, tiled=True
    ).reshape(block.shape)


def swap_halves(block, groups):
    pairs = [(i, (i + groups) % (2 * groups)) for i in range(2 * groups)]
    return lax.ppermute(block, "gx", pairs)


def from_neighbours(edges):
    count = lax.axis_size("gy")
    forward = [(i, (i + 1) % count) for i in range(count)]
    if count == 2:
        return lax.ppermute(edges, "gy", forward)
    backward = [(target, source) for source, target in forward]
    return jnp.stack(
        [lax.ppermute(edges[0], "gy", backward), lax.ppermute(edges[1], "gy", forward)]
    )


def per_device(magnetization, easy_axes, pins):
    _, planes, rows, width = magnetization.shape
    groups = lax.axis_size("gx") // 2
    units = rows * (width // LANES) // groups
    line = Line(planes)
    levels = make_levels(planes, groups)
    level = Level(planes, groups)
    near = float(Line(planes * groups).from_low[0])
    whole = magnetization.shape
    sent_shape = (groups * RHS * units, LANES)
    edge_shape = (2, 3 * planes, width)

    field = magnetization
    (coupling,) = call(
        functools.partial(coupling_kernel, line, units),
        [(groups * (COUPLED - RHS) * units, LANES)],
        easy_axes,
    )
    (sent,) = call(
        functools.partial(first_kernel, line, groups, units),
        [(groups * COUPLED * units, LANES)],
        coupling,
        field,
        easy_axes,
        pins,
    )
    coupling = None
    for stepno in range(STEPS):
        gathered = exchange(sent, groups)
        coupled = stepno == 0
        if coupled:
            coupling = gathered
        (joined,) = call(
            functools.partial(join_kernel, level, levels, units, coupled),
            [((6 if coupled else 3) * units, LANES)],
            gathered,
            coupling,
        )
        swapped = swap_halves(joined, groups)
        if coupled:
            across = (joined, swapped)
        (ghosts,) = call(
            functools.partial(part_kernel, level, levels, near, units, coupled),
            [sent_shape],
            joined,
            swapped,
            *across,
            gathered,
            coupling,
        )
        ghosts = exchange(ghosts, groups)
        solved, edges = call(
            functools.partial(finish_kernel, line, units),
            [whole, edge_shape],
            field,
            easy_axes,
            pins,
            ghosts,
        )
        beyond = from_neighbours(edges)
        turned, raw = call(turn_kernel, [whole, edge_shape], solved, easy_axes)
        if stepno < STEPS - 1:
            field, sent = call(
                functools.partial(mend_and_send_kernel, line, units),
                [whole, sent_shape],
                turned,
                edges,
                raw,
                beyond,
                easy_axes,
                pins,
                scratch=[pltpu.VMEM(edge_shape, jnp.float32)],
            )
        else:
            (field,) = call(
                last_kernel,
                [whole],
                turned,
                edges,
                raw,
                beyond,
                written=HBM,
                scratch=[
                    pltpu.VMEM(whole, jnp.float32),
                    pltpu.VMEM(edge_shape, jnp.float32),
                    pltpu.SemaphoreType.DMA((planes,)),
                ],
            )
    return field


def solution(mesh):
    in_specs = (P(None, "gx", "gy", None), P(None, "gx", "gy", None), P(None, None, "gy", None))
    out_specs = P(None, "gx", "gy", None)
    return jax.shard_map(
        per_device, mesh=mesh, in_specs=in_specs, out_specs=out_specs, check_vma=False
    )
```
